32 devices in a mesh: grp: 2 (over core), ep: 16 (over z, y, x).
Axes of the slice: x: 2, y: 2, z: 4, core: 2. Of those that a mesh axis runs over, the one named last changes fastest.
Arguments:
- hidden: bfloat16 [2, 4096, 2048], P('grp', 'ep'), may hold values from -6 to 6
- norm_gain: float32 [2, 2048], P('grp'), may hold values from 0.1 to 1.9
- final_gain: float32 [2, 2048], P('grp'), may hold values from 0.1 to 1.9
- router: bfloat16 [2, 2048, 128], P('grp'), may hold values from -0.125 to 0.125
- w_in: bfloat16 [2, 2048, 16384], P('grp', None, 'ep'), may hold values from -0.125 to 0.125
- w_out: bfloat16 [2, 16384, 2048], P('grp', 'ep'), may hold values from -0.125 to 0.125
- expert_ids: int32 [2, 4096, 2], P('grp', 'ep'), may hold values from 0 to 127, as said below
- slot_ids: int32 [2, 4096, 2], P('grp', 'ep'), may hold values from -1 to 5, as said below
- src_len: int32 [16, 4], P('ep'), may hold values from 1 to 128, 256 in all within a row
- tgt_len: int32 [16, 4], P('ep'), may hold values from 1 to 85, 171 in all within a row
- wq: bfloat16 [2048, 1024], P('ep'), may hold values from -1 to 1
- wk: bfloat16 [2048, 1024], P('ep'), may hold values from -1 to 1
- wv: bfloat16 [2048, 1024], P('ep'), may hold values from -0.125 to 0.125
- wo: bfloat16 [2048, 1024], P('ep'), may hold values from -0.5 to 0.5
Outputs:
- layer_out: bfloat16 [2, 4096, 2048], P('grp', 'ep')
The draws below stay inside these ranges and needn't reach their ends.
Inputs may be any that keep to these rules, and one draw needn't show every extreme that they name: `expert_ids`: each row names two different experts; at most one of them is below 2. `slot_ids`: -1 where the expert is 2 or more; otherwise a slot that no other route of the same device block to the same expert takes. In each group one expert gets all 6 slots from every device block.
All inputs are finite; a program needn't handle non-finite values.
Results may differ from the reference program's by a relative error of at most 0.02.
The reference program's roundings to bfloat16 on the way count: a program that leaves them out, or rounds other values in their place, can miss the bound.
Values may be sent and summed in bfloat16 or wider, within the bound.
No kernel may reach another device: no remote copies, remote signals or barrier semaphores. Data moves between devices by JAX's collectives and lax.ppermute only.
A program may use at most 128 MiB of HBM per device.

```python
import math
import jax
import jax.numpy as jnp
import numpy as np
from jax import lax

D = 2048
FF = 8192
EXPERTS = 128
HEADS = 8
HD = 128
SPLIT = 8
C = 6
ROWS = 256
SENT = 4
E_WIN = 2
FF_DEV = 1024
HW = 1024
TOKENS = 4096
SRC_MOST = 128
TGT_TOTAL = 171
TGT_MOST = 85
N_EP = 16


def route_tables(key):
    blocks = 2 * N_EP
    k_hot, k_dev, k_cnt, k_perm, k_side, k_first, k_second = jax.random.split(key, 7)
    hot_group = jnp.repeat(jax.random.randint(k_hot, (2, 1), 0, E_WIN), N_EP, axis=0)
    hot_dev = jax.random.randint(k_dev, (blocks, 1), 0, E_WIN)
    expert_iota = jnp.arange(E_WIN, dtype=jnp.int32)[None, :]
    counts = jax.random.randint(k_cnt, (blocks, E_WIN), (C + 2) // 3, C + 1)
    counts = jnp.where((expert_iota == hot_group) | (expert_iota == hot_dev), C, counts)
    order = jnp.arange(ROWS, dtype=jnp.int32)
    q_expert = jnp.minimum(order // C, E_WIN - 1)
    q_slot = order % C
    fill = jnp.take_along_axis(counts, jnp.broadcast_to(q_expert[None, :], (blocks, ROWS)), axis=1)
    live = (order[None, :] < E_WIN * C) & (q_slot[None, :] < fill)
    expert_q = jnp.where(live, q_expert[None, :], -1)
    slot_q = jnp.where(live, q_slot[None, :], -1)
    perms = jax.vmap(lambda k: jax.random.permutation(k, ROWS))(jax.random.split(k_perm, blocks))
    block_iota = jnp.arange(blocks, dtype=jnp.int32)[:, None]
    win_expert = jnp.zeros((blocks, ROWS), jnp.int32).at[block_iota, perms].set(expert_q)
    win_slot = jnp.zeros((blocks, ROWS), jnp.int32).at[block_iota, perms].set(slot_q)
    span = EXPERTS - E_WIN
    first = E_WIN + jax.random.randint(k_first, (blocks, ROWS), 0, span)
    second = E_WIN + (first - E_WIN + 1 + jax.random.randint(k_second, (blocks, ROWS), 0, span - 1)) % span
    has = win_expert >= 0
    lead = jnp.where(has, win_expert, first)
    other = jnp.where(has, first, second)
    slot_lead = jnp.where(has, win_slot, -1)
    side = jax.random.randint(k_side, (blocks, ROWS), 0, 2)
    id_zero = jnp.where(side == 1, other, lead)
    id_one = jnp.where(side == 1, lead, other)
    slot_zero = jnp.where(side == 1, -1, slot_lead)
    slot_one = jnp.where(side == 1, slot_lead, -1)
    ids = jnp.stack([id_zero, id_one], axis=-1).reshape(2, TOKENS, 2).astype(jnp.int32)
    slots = jnp.stack([slot_zero, slot_one], axis=-1).reshape(2, TOKENS, 2).astype(jnp.int32)
    return (ids, slots)


def draw_expert_ids(key, part):
    return route_tables(key)[0]


def draw_slot_ids(key, part):
    return route_tables(key)[1]


def draw_wq(key, part):
    key = jax.random.fold_in(key, 21)
    own = jax.random.normal(key, (D, HW), jnp.float32)
    values = own * D ** (-0.5)
    return jnp.clip(values, -1.0, 1.0).astype(jnp.bfloat16)


def draw_wk(key, part):
    key = jax.random.fold_in(key, 22)
    own = jax.random.normal(key, (D, HW), jnp.float32)
    values = own * D ** (-0.5)
    return jnp.clip(values, -1.0, 1.0).astype(jnp.bfloat16)


def spiked(drawn, rng, source, target, blocks, factor):
    owner, partner = [(jnp.arange(drawn.shape[dim]) // (drawn.shape[dim] // blocks)).reshape([-1 if axis == dim else 1 for axis in range(drawn.ndim)]) for dim in (source, target)]
    chosen = jax.random.permutation(rng, blocks)[partner]
    strong = (owner == chosen) | (owner == (partner + blocks // 2) % blocks)
    return jnp.where(strong, factor * drawn, drawn)


def levels(rng, shape, cuts, low, top_value):
    level = 1.0
    for dim, blocks in cuts:
        heights = jax.random.uniform(jax.random.fold_in(jax.random.fold_in(rng, 6), dim), (blocks,), jnp.float32, low / len(cuts), top_value / len(cuts))
        level = level * jnp.repeat(jnp.exp(heights), shape[dim] // blocks).reshape((-1,) + (1,) * (len(shape) - 1 - dim))
    return level


def split_up(number_of, total, bound, slope):
    loads = [(1 << 20) // math.isqrt(standing ** slope) + 1 for standing in range(2, number_of + 1)]
    rest, given = total - bound - (number_of - 1), [1] * (number_of - 1)
    while rest > 0:
        movable = [i for i in range(number_of - 1) if given[i] < bound]
        whole, remaining = sum([loads[i] for i in movable]), rest
        for i in movable:
            more = min(bound - given[i], max(1, remaining * loads[i] // whole), rest)
            given[i] = given[i] + more
            rest = rest - more
    return np.array([bound] + given)


def ragged_sizes(rng, amount, total, reach, skew):
    if amount == 2:
        one = jax.random.randint(rng, (), max(1, total - reach), min(reach, total - 1) + 1)
        return jnp.stack([one, total - one])
    sizes = jnp.asarray(split_up(amount, total, reach, skew), jnp.int32)
    pairs = (amount - 1) // 2
    giver, receiver = sizes[1:1 + 2 * pairs:2], sizes[2:2 + 2 * pairs:2]
    margin = jnp.minimum(giver - 1, reach - receiver)
    shifted = jax.random.randint(jax.random.fold_in(rng, 1), (pairs,), 0, 1 << 20) % (margin + 1)
    sizes = sizes.at[1:1 + 2 * pairs:2].set(giver - shifted).at[2:2 + 2 * pairs:2].set(receiver + shifted)
    return sizes[jax.random.permutation(jax.random.fold_in(rng, 2), amount)]


def scatter_about(stream_key, shape, width, most, cuts=(), kind=jnp.bfloat16):
    result = width * jax.random.normal(stream_key, shape, jnp.float32)
    if cuts:
        result = result * levels(stream_key, shape, cuts, -0.22, 0.18)
    return jnp.clip(result, -most, most).astype(kind)


def heavy_noise(rng, extent, deviation, most, cuts, heavy, kind=jnp.bfloat16):
    result = deviation * jax.random.normal(rng, extent, jnp.float32)
    if cuts:
        result = result * levels(rng, extent, cuts, -0.22, 0.18)
    return jnp.clip(spiked(result, jax.random.fold_in(rng, 3), *heavy), -most, most).astype(kind)


def setup_inputs(seed: int = 0) -> dict:
    key_of = jax.random.split(jax.random.key(seed), 15)
    hidden = scatter_about(key_of[0], (2, TOKENS, D), 1.0, 6.0, ((0, 2), (1, 16)))
    norm_gain = jnp.clip(1.0 + 0.18 * jax.random.normal(key_of[1], (2, D), jnp.float32), 0.1, 1.9)
    final_gain = jnp.clip(1.0 + 0.18 * jax.random.normal(key_of[2], (2, D), jnp.float32), 0.1, 1.9)
    router = scatter_about(key_of[3], (2, D, EXPERTS), D ** -0.5, 0.125, ((0, 2),))
    w_in = scatter_about(key_of[4], (2, D, E_WIN * FF), D ** -0.5, 0.125, ((0, 2), (2, 16)))
    w_out = heavy_noise(key_of[5], (2, E_WIN * FF, D), (FF // 2) ** -0.5, 0.125, ((0, 2), (1, 16)), (1, 2, 16, 2.0))
    expert_ids = draw_expert_ids(jax.random.fold_in(key_of[14], 71), 0)
    slot_ids = draw_slot_ids(jax.random.fold_in(key_of[14], 71), 0)
    src_len = jax.vmap(lambda own: ragged_sizes(own, SENT, ROWS, SRC_MOST, 2))(jax.random.split(key_of[8], N_EP)).reshape((N_EP, SENT)).astype(jnp.int32)
    tgt_len = jax.vmap(lambda own: ragged_sizes(own, SENT, TGT_TOTAL, TGT_MOST, 2))(jax.random.split(key_of[9], N_EP)).reshape((N_EP, SENT)).astype(jnp.int32)
    wq = draw_wq(jax.random.fold_in(key_of[14], 71), 0)
    wk = draw_wk(jax.random.fold_in(key_of[14], 71), 0)
    wv = scatter_about(key_of[12], (D, HW), D ** -0.5, 0.125, ((0, 16),))
    wo = scatter_about(key_of[13], (D, HW), (HW // 8) ** -0.5, 0.5, ((0, 16),))
    return dict(hidden=hidden, norm_gain=norm_gain, final_gain=final_gain, router=router, w_in=w_in, w_out=w_out, expert_ids=expert_ids, slot_ids=slot_ids, src_len=src_len, tgt_len=tgt_len, wq=wq, wk=wk, wv=wv, wo=wo)


def layer_norm(values, gain):
    mean = lax.optimization_barrier(jnp.mean(values, -1, keepdims=True))
    centred = values - mean
    spread = lax.optimization_barrier(jnp.mean(centred * centred, -1, keepdims=True))
    return centred * lax.rsqrt(spread + 1e-05) * gain

def segments(lengths, count):
    ends = jnp.cumsum(lengths).astype(jnp.int32)
    above = (jnp.arange(count, dtype=jnp.int32)[:, None] >= ends[None, :]).astype(jnp.int32)
    return lax.optimization_barrier(jnp.sum(above, axis=1)).astype(jnp.int32)

def group_moe(hidden, norm_gain, router, w_in, w_out, expert_ids, slot_ids):
    resid = hidden.astype(jnp.float32)
    normed = layer_norm(resid, norm_gain).astype(jnp.bfloat16)
    logits = jnp.dot(normed, router, preferred_element_type=jnp.float32)
    picked = jnp.take_along_axis(logits, expert_ids, axis=1)
    gate = jax.nn.sigmoid(picked - picked[:, ::-1])
    live = slot_ids >= 0
    place = lax.optimization_barrier(jnp.max(jnp.where(live, expert_ids * C + slot_ids, -1), axis=1)).astype(jnp.int32)
    weight = lax.optimization_barrier(jnp.sum(jnp.where(live, gate, jnp.float32(0.0)), axis=1))
    place_dev = place.reshape(N_EP, ROWS)
    normed_dev = normed.reshape(N_EP, ROWS, D)
    slots_all = E_WIN * C

    def pack(args):
        spots, rows = args
        target = jnp.where(spots >= 0, spots, slots_all).astype(jnp.int32)
        buffer = jnp.zeros((slots_all + 1, D), jnp.bfloat16).at[target].set(rows)
        return buffer[:slots_all]
    packed = lax.map(pack, (place_dev, normed_dev)).reshape(N_EP, E_WIN, C, D)

    def expert(index):
        rows = lax.dynamic_index_in_dim(packed, index, 1, keepdims=False).reshape(N_EP * C, D)
        first = lax.dynamic_slice_in_dim(w_in, index * FF, FF, 1)
        second = lax.dynamic_slice_in_dim(w_out, index * FF, FF, 0)
        inner = jax.nn.relu(jnp.dot(rows, first, preferred_element_type=jnp.float32)).astype(jnp.bfloat16)
        total = jnp.zeros((N_EP * C, D), jnp.float32)
        for piece_index in range(SPLIT):
            low = piece_index * FF_DEV
            part = jnp.dot(inner[:, low:low + FF_DEV], second[low:low + FF_DEV], preferred_element_type=jnp.float32)
            part = lax.optimization_barrier(part.astype(jnp.bfloat16))
            total = total + part.astype(jnp.float32)
        return total.reshape(N_EP, C, D)
    outputs = lax.map(expert, jnp.arange(E_WIN, dtype=jnp.int32))
    combined = jnp.transpose(outputs, (1, 0, 2, 3)).reshape(N_EP, E_WIN * C, D)

    def unpack(args):
        table, spots = args
        return jnp.take(table, jnp.maximum(spots, 0), axis=0)
    moe_rows = lax.map(unpack, (combined, place_dev)).reshape(TOKENS, D)
    return resid + moe_rows * weight[:, None]

def reference(hidden, norm_gain, final_gain, router, w_in, w_out, expert_ids, slot_ids, src_len, tgt_len, wq, wk, wv, wo):
    mixed = [group_moe(hidden[g], norm_gain[g], router[g], w_in[g], w_out[g], expert_ids[g], slot_ids[g]) for g in range(2)]
    normed_out = [layer_norm(mixed[g], final_gain[g]).astype(jnp.bfloat16) for g in range(2)]
    memory = normed_out[0]
    query = jnp.dot(normed_out[1], wq, preferred_element_type=jnp.float32).astype(jnp.bfloat16)
    keys = jnp.dot(memory, wk, preferred_element_type=jnp.float32).astype(jnp.bfloat16)
    values = jnp.dot(memory, wv, preferred_element_type=jnp.float32).astype(jnp.bfloat16)
    query = query.reshape(N_EP, ROWS, HEADS, HD)
    keys = keys.reshape(N_EP, ROWS, HEADS, HD)
    values = values.reshape(N_EP, ROWS, HEADS, HD)

    def attend(args):
        block_q, block_k, block_v, lengths_t, lengths_s = args
        seg_q = segments(lengths_t, ROWS)
        seg_k = segments(lengths_s, ROWS)
        valid = seg_q < SENT
        allowed = (seg_q[:, None] == seg_k[None, :]) & valid[:, None]
        scores = jnp.einsum('qhd,khd->hqk', block_q.astype(jnp.float32), block_k.astype(jnp.float32)) * HD ** (-0.5)
        scores = jnp.where(allowed[None], scores, jnp.float32(-1e+30))
        top = lax.optimization_barrier(jnp.max(scores, axis=-1, keepdims=True))
        expd = jnp.exp(scores - top)
        prob = (expd / lax.optimization_barrier(jnp.sum(expd, axis=-1, keepdims=True))).astype(jnp.bfloat16)
        context = jnp.einsum('hqk,khd->qhd', prob.astype(jnp.float32), block_v.astype(jnp.float32))
        context = context.astype(jnp.bfloat16).reshape(ROWS, HW)
        out = jnp.dot(context, wo.T, preferred_element_type=jnp.float32)
        return jnp.where(valid[:, None], out, jnp.float32(0.0))
    attended = lax.map(attend, (query, keys, values, tgt_len, src_len)).reshape(TOKENS, D)
    decoded = (mixed[1] + attended).astype(jnp.bfloat16)
    return jnp.stack([memory, decoded])
```

```python
import functools

import jax
import jax.numpy as jnp
from jax import lax
from jax.experimental import pallas as pl
from jax.experimental.pallas import tpu as pltpu
from jax.sharding import PartitionSpec as P

HD = 128
SPLIT = 8
C = 6
PAD = 8
SENT = 4
TGT_TOTAL = 171
MIB = 1 << 20


def normalize(values, gain):
    mean = jnp.mean(values, -1, keepdims=True)
    centred = values - mean
    spread = jnp.mean(centred * centred, -1, keepdims=True)
    return centred * lax.rsqrt(spread + 1e-05) * gain


def positions(lengths, count):
    upto = jnp.arange(SENT)[:, None] <= jnp.arange(SENT)[None, :]
    ends = jnp.sum(jnp.where(upto, lengths[:, None], 0), axis=0)
    above = (jnp.arange(count, dtype=jnp.int32)[:, None] >= ends[None, :]).astype(jnp.int32)
    return jnp.sum(above, axis=1)


def dot(left, right):
    return jnp.dot(left, right, preferred_element_type=jnp.float32)


def dot_rows(left, right):
    return lax.dot_general(
        left, right, (((1,), (1,)), ((), ())), preferred_element_type=jnp.float32
    )


def chips():
    return (4, 2, 2) if lax.axis_size("ep") == 16 else None


def place_of(index):
    depth, high, wide = chips()
    return index // (high * wide), index // wide % high, index % wide


def index_of(z, y, x):
    depth, high, wide = chips()
    return (z % depth * high + y) * wide + x


def moved(value, dz=0, dy=0, dx=0):
    pairs = []
    for source in range(lax.axis_size("ep")):
        z, y, x = place_of(source)
        pairs.append((source, index_of(z + dz, y ^ dy, x ^ dx)))
    return lax.ppermute(value, "ep", pairs)


def specs(smem, vmem, unread=0):
    return (
        [pl.BlockSpec(memory_space=pltpu.SMEM)] * smem
        + [pl.BlockSpec(memory_space=pltpu.VMEM)] * vmem
        + [pl.BlockSpec(memory_space=pl.ANY)] * unread
    )


def local(kernel, name, outs, vmem, after=(), onward=(), order=None):
    scalars = () if order is None else (order,)
    read = len(scalars) + len(vmem)

    def run(*refs):
        kernel(*refs[:read], *refs[read + len(after) + len(onward) :][: len(outs)])

    first = read + len(after)
    return pl.pallas_call(
        run,
        out_shape=[jax.ShapeDtypeStruct(shape, dtype) for shape, dtype in outs]
        + [jax.ShapeDtypeStruct(array.shape, array.dtype) for array in onward],
        in_specs=specs(len(scalars), len(vmem), len(after) + len(onward)),
        out_specs=specs(0, len(outs), len(onward)),
        input_output_aliases={first + i: len(outs) + i for i in range(len(onward))},
        compiler_params=pltpu.CompilerParams(vmem_limit_bytes=16 * MIB),
        name=name,
    )(*scalars, *vmem, *after, *onward)


def pack_kernel(experts, place, both, hidden, gain, router, gate, send):
    count = gate.shape[0]
    slot = lax.broadcasted_iota(jnp.int32, (count, hidden.shape[0]), 0)
    table = slot == place[...]
    rows = dot(table.astype(jnp.bfloat16), hidden[...])
    normed = normalize(rows, gain[...])
    send[...] = jnp.concatenate(
        [normed[e * PAD : (e + 1) * PAD] for e in experts], axis=0
    ).astype(jnp.bfloat16)
    logits = dot(normed.astype(jnp.bfloat16), router[...])
    mine = lax.broadcasted_iota(jnp.int32, (count, 1), 0) // PAD
    others = jnp.sum(jnp.where(table, both[...], 0), axis=1, keepdims=True) - mine
    expert = lax.broadcasted_iota(jnp.int32, logits.shape, 1)
    lead = jnp.where(expert == mine, logits, 0.0) - jnp.where(expert == others, logits, 0.0)
    gate[...] = 1.0 / (1.0 + jnp.exp(-jnp.sum(lead, axis=1, keepdims=True)))


def copies_kernel(rows, out):
    size = rows.shape[0]
    for i in range(out.shape[0] // size):
        out[i * size : (i + 1) * size] = rows[...]


def mlp_kernel(rows, w_in, w_out, pieces):
    inner = jnp.maximum(dot(rows[...], w_in[...]), 0.0).astype(jnp.bfloat16)
    pieces[...] = dot(inner, w_out[...]).astype(jnp.bfloat16)


def sum_kernel(pieces, out):
    size = out.shape[0]
    total = pieces[:size].astype(jnp.float32)
    for low in range(size, pieces.shape[0], size):
        total = total + pieces[low : low + size].astype(jnp.float32)
    out[...] = total


def norm_kernel(experts, place, gate, hidden, gain, parts, mixed, normed):
    count = gate.shape[0]
    summed = [None] * (count // PAD)
    for i, e in enumerate(experts):
        part = parts[i * PAD : (i + 1) * PAD]
        summed[e] = part if summed[e] is None else summed[e] + part
    rows = gate[...] * jnp.concatenate(summed, axis=0)
    high = rows.astype(jnp.bfloat16)
    rest = rows - high.astype(jnp.float32)
    middle = rest.astype(jnp.bfloat16)
    low = (rest - middle.astype(jnp.float32)).astype(jnp.bfloat16)
    slot = lax.broadcasted_iota(jnp.int32, (hidden.shape[0], 3 * count), 1) % count
    picks = (slot == place[...]).astype(jnp.bfloat16)
    total = hidden[...].astype(jnp.float32) + dot(picks, jnp.concatenate([high, middle, low], axis=0))
    mixed[...] = total
    normed[...] = normalize(total, gain[...]).astype(jnp.bfloat16)


def places(routes, slots):
    return jnp.max(jnp.where(slots >= 0, routes * PAD + slots, -1), axis=1)


def expert_rows(hidden, norm_gain, router, w_in, w_out, routes, slots):
    experts = lax.axis_size("ep") // SPLIT
    count = experts * PAD
    width = hidden.shape[1]
    table = jnp.arange(count)[:, None] == places(routes, slots)[None, :]
    rows = dot(table.astype(jnp.bfloat16), hidden)
    normed = normalize(rows, norm_gain).astype(jnp.bfloat16)
    outgoing = jnp.broadcast_to(normed.reshape(experts, 1, PAD, width), (experts, SPLIT, PAD, width))
    arrived = lax.all_to_all(
        outgoing.reshape(experts * SPLIT, PAD, width), "ep", split_axis=0, concat_axis=0, tiled=True
    ).reshape(-1, width)
    inner = jax.nn.relu(dot(arrived, w_in)).astype(jnp.bfloat16)
    piece = dot(inner, w_out).astype(jnp.bfloat16)
    back = lax.all_to_all(
        piece.reshape(-1, PAD, width), "ep", split_axis=0, concat_axis=0, tiled=True
    )
    summed = jnp.sum(back.reshape(experts, SPLIT, PAD, width).astype(jnp.float32), axis=1)
    logits = dot(normed, router)
    mine = jnp.arange(count) // PAD
    both = jnp.sum(routes, axis=1)
    others = jnp.sum(jnp.where(table, both[None, :], 0), axis=1) - mine
    ids = jnp.arange(router.shape[1])[None, :]
    sign = (ids == mine[:, None]).astype(jnp.float32) - (ids == others[:, None]).astype(jnp.float32)
    gate = jax.nn.sigmoid(jnp.sum(logits * sign, axis=1, keepdims=True))
    return gate * summed.reshape(count, width), table


def spread_rows(table, rows):
    high = rows.astype(jnp.bfloat16)
    rest = rows - high.astype(jnp.float32)
    middle = rest.astype(jnp.bfloat16)
    low = (rest - middle.astype(jnp.float32)).astype(jnp.bfloat16)
    picks = jnp.concatenate([table.T.astype(jnp.bfloat16)] * 3, axis=1)
    return dot(picks, jnp.concatenate([high, middle, low], axis=0))


def pairs_of(refs):
    return [tuple(range(low, min(low + 2, len(refs)))) for low in range(0, len(refs), 2)]


def joined(parts, axis):
    return parts[0] if len(parts) == 1 else jnp.concatenate(parts, axis=axis)


def project_kernel(count, order, memory, target, *refs):
    blocks, (kv, q) = refs[:count], refs[-2:]
    add_blocks(order, memory, target, blocks, kv, q, True)


def add_blocks(order, memory, target, blocks, kv, q, fresh):
    rows = blocks[0].shape[0]
    half = q.shape[1]

    def columns(ref, members):
        return joined(
            [ref[:, pl.ds(pl.multiple_of(order[i] * rows, 128), rows)] for i in members], 1
        )

    for step, members in enumerate(pairs_of(blocks)):
        weights = joined([blocks[i][:, : 3 * half] for i in members], 0)
        kv_part = dot(columns(memory, members), weights[:, : 2 * half])
        q_part = dot(columns(target, members), weights[:, 2 * half :])
        if fresh and step == 0:
            kv[...] = kv_part
            q[...] = q_part
        else:
            kv[...] += kv_part
            q[...] += q_part


def attend_kernel(
    early, late, late_order, order, seg_q, seg_k, memory, target, kv_sum, q_sum, *refs
):
    blocks = refs[: early + late]
    own, sent, kv, q, context = refs[early + late :]
    half = q.shape[1]
    rows = blocks[0].shape[0]
    kv[...] = kv_sum[...]
    q[...] = q_sum[...]
    if late:
        add_blocks(late_order, memory, target, blocks[early:], kv, q, False)
    allowed = seg_q[...] == seg_k[...]
    for low in range(0, half, HD):
        query = q[:, low : low + HD].astype(jnp.bfloat16)
        keys = kv[:, low : low + HD].astype(jnp.bfloat16)
        values = kv[:, half + low : half + low + HD].astype(jnp.bfloat16)
        scores = jnp.where(allowed, dot_rows(query, keys) * HD ** (-0.5), -1e30)
        expd = jnp.exp(scores - jnp.max(scores, axis=-1, keepdims=True))
        prob = (expd / jnp.sum(expd, axis=-1, keepdims=True)).astype(jnp.bfloat16)
        context[:, low : low + HD] = dot(prob, values).astype(jnp.bfloat16)
    for members in pairs_of(blocks):
        part = dot_rows(context[...], joined([blocks[i][:, 3 * half :] for i in members], 0))
        for place, i in enumerate(members):
            columns = pl.ds(pl.multiple_of(order[i] * rows, 128), rows)
            value = part[:, place * rows : (place + 1) * rows]
            own[:, columns] = value
            sent[:, columns] = value.astype(jnp.bfloat16)


def project(order, memory, target, blocks):
    half = blocks[0].shape[1] // 4
    return local(
        functools.partial(project_kernel, len(blocks)),
        "project",
        [((memory.shape[0], 2 * half), jnp.float32), ((target.shape[0], half), jnp.float32)],
        (memory, target, *blocks),
        order=order,
    )


def attend(order, seg_q, seg_k, memory, target, sums, early, late):
    half = early[0].shape[1] // 4
    count, width = target.shape
    late_order = order[len(early) :] if late else order
    return pl.pallas_call(
        functools.partial(attend_kernel, len(early), len(late)),
        out_shape=[
            jax.ShapeDtypeStruct((count, width), jnp.float32),
            jax.ShapeDtypeStruct((count, width), jnp.bfloat16),
        ],
        in_specs=specs(2, 6 + len(early) + len(late)),
        out_specs=[pl.BlockSpec(memory_space=pltpu.VMEM)] * 2,
        scratch_shapes=[
            pltpu.VMEM((memory.shape[0], 2 * half), jnp.float32),
            pltpu.VMEM((count, half), jnp.float32),
            pltpu.VMEM((count, half), jnp.bfloat16),
        ],
        compiler_params=pltpu.CompilerParams(vmem_limit_bytes=16 * MIB),
        name="attend",
    )(late_order, order, seg_q[:, None], seg_k[None, :], memory, target, *sums, *early, *late)


def exchanged(rows, groups):
    parts = rows.reshape(len(groups[0]), -1, rows.shape[1])
    return lax.all_to_all(
        parts, "ep", split_axis=0, concat_axis=0, tiled=True, axis_index_groups=groups
    ).reshape(rows.shape)


def by_hand(part, hidden, norm_gain, final_gain, router, w_in, w_out, routes, slots):
    depth, high, wide = chips()
    across = high * wide
    experts = lax.axis_size("ep") // SPLIT
    rows, width = hidden.shape
    z, y, x = place_of(lax.axis_index("ep"))
    place = places(routes, slots)
    held = [level // (depth // experts) for level in range(depth)]
    columns = [[level * across + i for level in range(depth)] for i in range(across)]
    planes = [[level * across + i for i in range(across)] for level in range(depth)]
    line = (depth * PAD, width)
    sheet = (across * depth * PAD, width)

    z1, x0, y0 = moved(part, dz=1), moved(part, dx=1), moved(part, dy=1)
    gate, send = local(
        functools.partial(pack_kernel, held),
        "pack",
        [((experts * PAD, 1), jnp.float32), (line, jnp.bfloat16)],
        (place[None, :], jnp.sum(routes, axis=1)[None, :], hidden, norm_gain[None, :], router),
    )
    column = exchanged(send, columns)

    column, z1, y0 = local(
        copies_kernel, "copies", [(sheet, jnp.bfloat16)], (column,), (x0,), (z1, y0)
    )
    z2, far0, y1 = moved(z1, dz=1), moved(y0, dx=1), moved(z1, dy=1)
    plane = exchanged(column, planes)

    pieces, z1, z2, far0 = local(
        mlp_kernel, "mlp", [(sheet, jnp.bfloat16)], (plane, w_in, w_out), (y1,), (z1, z2, far0)
    )
    z3, x1, y2 = moved(z2, dz=1), moved(z1, dx=1), moved(z2, dy=1)
    back = exchanged(pieces, planes)

    parts, z2, z3, far0 = local(
        sum_kernel, "sum", [(line, jnp.float32)], (back,), (x1, y2), (z2, z3, far0)
    )
    far1, x2, y3 = moved(far0, dz=1), moved(z2, dx=1), moved(z3, dy=1)
    parts = exchanged(parts, columns)

    mixed, normed, z3, far0, x2 = local(
        functools.partial(norm_kernel, held),
        "norm",
        [((rows, width), jnp.float32), ((rows, width), jnp.bfloat16)],
        (place[:, None], gate, hidden, final_gain[None, :], parts),
        (far1, y3),
        (z3, far0, x2),
    )
    far3, x3, far2 = moved(far0, dz=-1), moved(z3, dx=1), moved(x2, dy=1)
    early = {
        (0, 0, 0): part, (1, 0, 0): z1, (2, 0, 0): z2, (3, 0, 0): z3,
        (0, 0, 1): x0, (1, 0, 1): x1, (0, 1, 0): y0, (1, 1, 0): y1,
        (2, 1, 0): y2, (3, 1, 0): y3, (0, 1, 1): far0, (1, 1, 1): far1, (2, 0, 1): x2,
    }
    late = {(3, 0, 1): x3, (3, 1, 1): far3, (2, 1, 1): far2}
    order = jnp.stack([index_of(z - dz, y ^ dy, x ^ dx) for dz, dy, dx in (*early, *late)])
    return mixed, normed, order, list(early.values()), list(late.values())


def body(
    hidden,
    norm_gain,
    final_gain,
    router,
    w_in,
    w_out,
    expert_ids,
    slot_ids,
    src_len,
    tgt_len,
    wq,
    wk,
    wv,
    wo,
):
    group = lax.axis_index("grp")
    encoder = group == 0
    rows_here, width = hidden.shape[1:]
    half = wq.shape[1] // lax.axis_size("grp")
    targets = min(rows_here, -(-TGT_TOTAL // 16) * 16)

    part = jnp.concatenate(
        [lax.dynamic_slice_in_dim(weight, group * half, half, 1) for weight in (wk, wv, wq, wo)], axis=1
    )
    if chips() is None:
        early = [lax.all_gather(part, "ep", axis=0, tiled=True)]
        late = []
        order = jnp.zeros((1,), jnp.int32)
        added, table = expert_rows(
            hidden[0], norm_gain[0], router[0], w_in[0], w_out[0], expert_ids[0], slot_ids[0]
        )
        mixed = hidden[0].astype(jnp.float32) + spread_rows(table, added)
        normed_out = normalize(mixed, final_gain[0]).astype(jnp.bfloat16)
    else:
        mixed, normed_out, order, early, late = by_hand(
            part, hidden[0], norm_gain[0], final_gain[0], router[0], w_in[0], w_out[0],
            expert_ids[0], slot_ids[0],
        )
    other = lax.ppermute(normed_out, "grp", [(0, 1), (1, 0)])
    memory = jnp.where(encoder, normed_out, other)
    target = jnp.where(encoder, other[:targets], normed_out[:targets])

    seg_q = positions(tgt_len[0], targets)
    seg_k = positions(src_len[0], rows_here)
    valid = (seg_q < SENT)[:, None]
    sums = project(order, memory, target, early)
    own, sent = attend(order, seg_q, seg_k, memory, target, sums, early, late)
    total = own + lax.ppermute(sent, "grp", [(0, 1)]).astype(jnp.float32)
    attended = jnp.pad(jnp.where(valid, total, 0.0), ((0, rows_here - targets), (0, 0)))
    decoded = (mixed + attended).astype(jnp.bfloat16)
    return jnp.where(encoder, normed_out, decoded)[None]


def solution(mesh):
    in_specs = (
        P("grp", "ep", None),
        P("grp", None),
        P("grp", None),
        P("grp", None, None),
        P("grp", None, "ep"),
        P("grp", "ep", None),
        P("grp", "ep", None),
        P("grp", "ep", None),
        P("ep", None),
        P("ep", None),
        P("ep", None),
        P("ep", None),
        P("ep", None),
        P("ep", None),
    )
    out_specs = P("grp", "ep", None)
    return jax.shard_map(body, mesh=mesh, in_specs=in_specs, out_specs=out_specs, check_vma=False)
```

```python
import functools

import jax
import jax.numpy as jnp
from jax import lax
from jax.experimental import pallas as pl
from jax.experimental.pallas import tpu as pltpu
from jax.sharding import PartitionSpec as P

HD = 128
SPLIT = 8
C = 6
PAD = 8
SENT = 4
TGT_TOTAL = 171
MIB = 1 << 20


def normalize(values, gain):
    mean = jnp.mean(values, -1, keepdims=True)
    centred = values - mean
    spread = jnp.mean(centred * centred, -1, keepdims=True)
    return centred * lax.rsqrt(spread + 1e-05) * gain


def positions(lengths, count):
    upto = jnp.arange(SENT)[:, None] <= jnp.arange(SENT)[None, :]
    ends = jnp.sum(jnp.where(upto, lengths[:, None], 0), axis=0)
    above = (jnp.arange(count, dtype=jnp.int32)[:, None] >= ends[None, :]).astype(jnp.int32)
    return jnp.sum(above, axis=1)


def dot(left, right):
    return jnp.dot(left, right, preferred_element_type=jnp.float32)


def dot_rows(left, right):
    return lax.dot_general(
        left, right, (((1,), (1,)), ((), ())), preferred_element_type=jnp.float32
    )


def chips():
    return (4, 2, 2) if lax.axis_size("ep") == 16 else None


def place_of(index):
    depth, high, wide = chips()
    return index // (high * wide), index // wide % high, index % wide


def index_of(z, y, x):
    depth, high, wide = chips()
    return (z % depth * high + y) * wide + x


def moved(value, dz=0, dy=0, dx=0):
    pairs = []
    for source in range(lax.axis_size("ep")):
        z, y, x = place_of(source)
        pairs.append((source, index_of(z + dz, y ^ dy, x ^ dx)))
    return lax.ppermute(value, "ep", pairs)


def specs(smem, vmem, unread=0):
    return (
        [pl.BlockSpec(memory_space=pltpu.SMEM)] * smem
        + [pl.BlockSpec(memory_space=pltpu.VMEM)] * vmem
        + [pl.BlockSpec(memory_space=pl.ANY)] * unread
    )


def local(kernel, name, outs, vmem, after=(), onward=(), order=None, far=(), scratch=(), mib=6):
    scalars = () if order is None else (order,)
    read = len(scalars) + len(vmem) + len(far)
    unread = len(after) + len(onward)

    def run(*refs):
        results = refs[read + unread :]
        kernel(*refs[:read], *results[: len(outs)], *results[len(outs) + len(onward) :])

    first = read + len(after)
    return pl.pallas_call(
        run,
        out_shape=[jax.ShapeDtypeStruct(shape, dtype) for shape, dtype in outs]
        + [jax.ShapeDtypeStruct(array.shape, array.dtype) for array in onward],
        in_specs=specs(len(scalars), len(vmem), len(far) + unread),
        out_specs=specs(0, len(outs), len(onward)),
        scratch_shapes=list(scratch),
        input_output_aliases={first + i: len(outs) + i for i in range(len(onward))},
        compiler_params=pltpu.CompilerParams(vmem_limit_bytes=mib * MIB),
        name=name,
    )(*scalars, *vmem, *far, *after, *onward)


def pack_kernel(experts, place, both, hidden, gain, router, gate, send):
    count = gate.shape[0]
    slot = lax.broadcasted_iota(jnp.int32, (count, hidden.shape[0]), 0)
    table = slot == place[...]
    rows = dot(table.astype(jnp.bfloat16), hidden[...])
    normed = normalize(rows, gain[...])
    send[...] = jnp.concatenate(
        [normed[e * PAD : (e + 1) * PAD] for e in experts], axis=0
    ).astype(jnp.bfloat16)
    logits = dot(normed.astype(jnp.bfloat16), router[...])
    mine = lax.broadcasted_iota(jnp.int32, (count, 1), 0) // PAD
    others = jnp.sum(jnp.where(table, both[...], 0), axis=1, keepdims=True) - mine
    expert = lax.broadcasted_iota(jnp.int32, logits.shape, 1)
    lead = jnp.where(expert == mine, logits, 0.0) - jnp.where(expert == others, logits, 0.0)
    gate[...] = 1.0 / (1.0 + jnp.exp(-jnp.sum(lead, axis=1, keepdims=True)))


def gate_kernel():
    pass


def mlp_kernel(rows, w_in, w_out, pieces):
    inner = jnp.maximum(dot(rows[...], w_in[...]), 0.0).astype(jnp.bfloat16)
    pieces[...] = dot(inner, w_out[...]).astype(jnp.bfloat16)


def rows_kernel(experts, gate, parts, rows):
    count = gate.shape[0]
    summed = [None] * (count // PAD)
    for i, e in enumerate(experts):
        part = parts[i * PAD : (i + 1) * PAD].astype(jnp.float32)
        summed[e] = part if summed[e] is None else summed[e] + part
    rows[...] = gate[...] * jnp.concatenate(summed, axis=0)


def mixed_rows(hidden, place, rows_ref):
    rows = rows_ref[...]
    count, size = rows.shape[0], hidden.shape[0]
    high = rows.astype(jnp.bfloat16)
    rest = rows - high.astype(jnp.float32)
    middle = rest.astype(jnp.bfloat16)
    low = (rest - middle.astype(jnp.float32)).astype(jnp.bfloat16)
    slot = lax.broadcasted_iota(jnp.int32, (size, 3 * count), 1) % count
    picks = (slot.astype(jnp.float32) == place[...]).astype(jnp.bfloat16)
    added = dot(picks, jnp.concatenate([high, middle, low], axis=0))
    return hidden[...].astype(jnp.float32) + added


def norm_kernel(group, *refs):
    own, other, (memory, target, mixed) = refs[:4], refs[4:8], refs[8:]

    def run(source, wanted):
        hidden, place, rows, gain = source
        values = mixed_rows(hidden, place, rows)
        memory[...] = normalize(values, gain[...]).astype(jnp.bfloat16)
        hidden, place, rows, gain = wanted
        mixed[...] = mixed_rows(hidden, place, rows)
        target[...] = normalize(mixed[: target.shape[0]], gain[...]).astype(jnp.bfloat16)

    pl.when(group[0] == 0)(lambda: run(own, other))
    pl.when(group[0] != 0)(lambda: run(other, own))


def places(routes, slots):
    return jnp.max(jnp.where(slots >= 0, routes * PAD + slots, -1), axis=1)


def expert_rows(hidden, norm_gain, router, w_in, w_out, routes, slots):
    experts = lax.axis_size("ep") // SPLIT
    count = experts * PAD
    width = hidden.shape[1]
    table = jnp.arange(count)[:, None] == places(routes, slots)[None, :]
    rows = dot(table.astype(jnp.bfloat16), hidden)
    normed = normalize(rows, norm_gain).astype(jnp.bfloat16)
    outgoing = jnp.broadcast_to(normed.reshape(experts, 1, PAD, width), (experts, SPLIT, PAD, width))
    arrived = lax.all_to_all(
        outgoing.reshape(experts * SPLIT, PAD, width), "ep", split_axis=0, concat_axis=0, tiled=True
    ).reshape(-1, width)
    inner = jax.nn.relu(dot(arrived, w_in)).astype(jnp.bfloat16)
    piece = dot(inner, w_out).astype(jnp.bfloat16)
    back = lax.all_to_all(
        piece.reshape(-1, PAD, width), "ep", split_axis=0, concat_axis=0, tiled=True
    )
    summed = jnp.sum(back.reshape(experts, SPLIT, PAD, width).astype(jnp.float32), axis=1)
    logits = dot(normed, router)
    mine = jnp.arange(count) // PAD
    both = jnp.sum(routes, axis=1)
    others = jnp.sum(jnp.where(table, both[None, :], 0), axis=1) - mine
    ids = jnp.arange(router.shape[1])[None, :]
    sign = (ids == mine[:, None]).astype(jnp.float32) - (ids == others[:, None]).astype(jnp.float32)
    gate = jax.nn.sigmoid(jnp.sum(logits * sign, axis=1, keepdims=True))
    return gate * summed.reshape(count, width)


def expert_layer(marks, hidden, norm_gain, router, w_in, w_out, routes, slots):
    devices = lax.axis_size("ep")
    experts = devices // SPLIT
    width = hidden.shape[1]
    place = places(routes, slots)
    held = [device // SPLIT for device in range(devices)]
    blocks = (devices * PAD, width)

    def exchanged(values):
        parts = values.reshape(devices, PAD, width)
        parts = lax.all_to_all(parts, "ep", split_axis=0, concat_axis=0, tiled=True)
        return parts.reshape(values.shape)

    gate, send = local(
        functools.partial(pack_kernel, held),
        "pack",
        [((experts * PAD, 1), jnp.float32), (blocks, jnp.bfloat16)],
        (place[None, :], jnp.sum(routes, axis=1)[None, :], hidden, norm_gain[None, :], router),
    )
    (pieces,) = local(
        mlp_kernel,
        "mlp",
        [(blocks, jnp.bfloat16)],
        (exchanged(send), w_in, w_out),
        marks[0],
    )
    (rows,) = local(
        functools.partial(rows_kernel, held),
        "rows",
        [((experts * PAD, width), jnp.float32)],
        (gate, exchanged(pieces)),
        marks[1],
    )
    return rows


def both_norms(hidden, other_hidden, final_gain, place, rows, targets):
    swap = [(0, 1), (1, 0)]
    place = place[:, None].astype(jnp.float32)
    gain = final_gain[None, :]
    small = jnp.concatenate([gain, jnp.pad(place.T, ((0, 0), (0, gain.shape[1] - place.shape[0])))])
    small = lax.ppermute(small, "grp", swap)
    other_rows = lax.ppermute(rows, "grp", swap)
    own = (hidden, place, rows, gain)
    other = (other_hidden, small[1, : place.shape[0]][:, None], other_rows, small[:1])
    size, width = hidden.shape
    return local(
        norm_kernel,
        "norm",
        [
            ((size, width), jnp.bfloat16),
            ((targets, width), jnp.bfloat16),
            ((size, width), jnp.float32),
        ],
        (*own[:4], *other[:4]),
        order=lax.axis_index("grp")[None],
        mib=12,
    )


EARLY = [
    (0, 0, 0), (1, 0, 0), (2, 0, 0), (3, 0, 0), (0, 0, 1), (1, 0, 1), (0, 1, 0), (1, 1, 0),
    (2, 1, 0), (3, 1, 0), (0, 1, 1), (1, 1, 1), (2, 0, 1),
]
LATE = [(3, 0, 1), (3, 1, 1), (2, 1, 1)]


def gather(part):
    def once(there, *blocks):
        return local(gate_kernel, "gate", [], (), there, blocks)

    z1, x0, y0 = moved(part, dz=1), moved(part, dx=1), moved(part, dy=1)
    z1, y0 = once([x0], z1, y0)
    z2, far0, y1 = moved(z1, dz=1), moved(y0, dx=1), moved(z1, dy=1)
    z1, z2, far0 = once([y1], z1, z2, far0)
    second = [z2]
    z3, x1, y2 = moved(z2, dz=1), moved(z1, dx=1), moved(z2, dy=1)
    z2, z3, far0 = once([x1, y2], z2, z3, far0)
    far1, x2, y3 = moved(far0, dz=1), moved(z2, dx=1), moved(z3, dy=1)
    z3, far0, x2 = once([far1, y3], z3, far0, x2)
    fourth = [x2]
    far3, x3, far2 = moved(far0, dz=-1), moved(z3, dx=1), moved(x2, dy=1)
    early = [part, z1, z2, z3, x0, x1, y0, y1, y2, y3, far0, far1, x2]
    return early, [x3, far3, far2], (second, fourth)


def pairs_of(refs):
    return [tuple(range(low, min(low + 2, len(refs)))) for low in range(0, len(refs), 2)]


def joined(parts, axis):
    return parts[0] if len(parts) == 1 else jnp.concatenate(parts, axis=axis)


def fetched(blocks, columns, near, sems):
    rows = blocks[0].shape[0]
    copies = [
        pltpu.make_async_copy(
            block.at[:, columns], near.at[pl.ds(i * rows, rows)], sems.at[i]
        )
        for i, block in enumerate(blocks)
    ]
    for copy in copies:
        copy.start()
    return copies


def add_blocks(order, memory, target, near, copies, kv, q, fresh):
    rows = near.shape[0] // len(copies)
    half = q.shape[1]

    def columns(ref, members):
        return joined(
            [ref[:, pl.ds(pl.multiple_of(order[i] * rows, 128), rows)] for i in members], 1
        )

    for step, members in enumerate(pairs_of(copies)):
        for i in members:
            copies[i].wait()
        weights = near[members[0] * rows : (members[-1] + 1) * rows]
        kv_part = dot(columns(memory, members), weights[:, : 2 * half])
        q_part = dot(columns(target, members), weights[:, 2 * half :])
        if fresh and step == 0:
            kv[...] = kv_part
            q[...] = q_part
        else:
            kv[...] += kv_part
            q[...] += q_part


def project_kernel(count, order, memory, target, *refs):
    blocks, (kv, q, near, sems) = refs[:count], refs[count:]
    copies = fetched(blocks, pl.ds(0, near.shape[1]), near, sems)
    add_blocks(order, memory, target, near, copies, kv, q, True)


def attend_kernel(early, late, order, seg_q, seg_k, memory, target, kv_sum, q_sum, *refs):
    blocks = refs[: early + late]
    own, sent, kv, q, context, near, near_out, sems, sems_out = refs[early + late :]
    half = q.shape[1]
    rows = blocks[0].shape[0]
    kv[...] = kv_sum[...]
    q[...] = q_sum[...]
    if late:
        copies = fetched(blocks[early:], pl.ds(0, 3 * half), near, sems)
    copies_out = fetched(blocks, pl.ds(3 * half, half), near_out, sems_out)
    if late:
        late_order = [order[early + i] for i in range(late)]
        add_blocks(late_order, memory, target, near, copies, kv, q, False)
    allowed = seg_q[...] == seg_k[...]
    for low in range(0, half, HD):
        query = q[:, low : low + HD].astype(jnp.bfloat16)
        keys = kv[:, low : low + HD].astype(jnp.bfloat16)
        values = kv[:, half + low : half + low + HD].astype(jnp.bfloat16)
        scores = jnp.where(allowed, dot_rows(query, keys) * HD ** (-0.5), -1e30)
        expd = jnp.exp(scores - jnp.max(scores, axis=-1, keepdims=True))
        prob = (expd / jnp.sum(expd, axis=-1, keepdims=True)).astype(jnp.bfloat16)
        context[:, low : low + HD] = dot(prob, values).astype(jnp.bfloat16)
    for copy in copies_out:
        copy.wait()
    for members in pairs_of(blocks):
        part = dot_rows(context[...], near_out[members[0] * rows : (members[-1] + 1) * rows])
        for place, i in enumerate(members):
            columns = pl.ds(pl.multiple_of(order[i] * rows, 128), rows)
            value = part[:, place * rows : (place + 1) * rows]
            own[:, columns] = value
            sent[:, columns] = value.astype(jnp.bfloat16)


def project(order, memory, target, blocks):
    rows, half = blocks[0].shape[0], blocks[0].shape[1] // 4
    return local(
        functools.partial(project_kernel, len(blocks)),
        "project",
        [((memory.shape[0], 2 * half), jnp.float32), ((target.shape[0], half), jnp.float32)],
        (memory, target),
        order=order,
        far=blocks,
        scratch=[
            pltpu.VMEM((len(blocks) * rows, 3 * half), jnp.bfloat16),
            pltpu.SemaphoreType.DMA((len(blocks),)),
        ],
        mib=14,
    )


def attend(order, seg_q, seg_k, memory, target, sums, early, late):
    rows, half = early[0].shape[0], early[0].shape[1] // 4
    count, width = target.shape
    blocks = len(early) + len(late)
    return local(
        functools.partial(attend_kernel, len(early), len(late)),
        "attend",
        [((count, width), jnp.float32), ((count, width), jnp.bfloat16)],
        (seg_q[:, None], seg_k[None, :], memory, target, *sums),
        order=order,
        far=(*early, *late),
        scratch=[
            pltpu.VMEM((memory.shape[0], 2 * half), jnp.float32),
            pltpu.VMEM((count, half), jnp.float32),
            pltpu.VMEM((count, half), jnp.bfloat16),
            pltpu.VMEM((max(len(late), 1) * rows, 3 * half), jnp.bfloat16),
            pltpu.VMEM((blocks * rows, half), jnp.bfloat16),
            pltpu.SemaphoreType.DMA((max(len(late), 1),)),
            pltpu.SemaphoreType.DMA((blocks,)),
        ],
        mib=14,
    )


def body(
    hidden,
    norm_gain,
    final_gain,
    router,
    w_in,
    w_out,
    expert_ids,
    slot_ids,
    src_len,
    tgt_len,
    wq,
    wk,
    wv,
    wo,
):
    group = lax.axis_index("grp")
    encoder = group == 0
    rows_here, width = hidden.shape[1:]
    half = wq.shape[1] // lax.axis_size("grp")
    targets = min(rows_here, -(-TGT_TOTAL // 16) * 16)

    def mine(*weights):
        return jnp.concatenate(
            [lax.dynamic_slice_in_dim(weight, group * half, half, 1) for weight in weights], axis=1
        )

    part = mine(wk, wv, wq, wo)
    other_hidden = lax.ppermute(hidden[0], "grp", [(0, 1), (1, 0)])
    layer = (norm_gain[0], router[0], w_in[0], w_out[0], expert_ids[0], slot_ids[0])
    if chips() is None:
        early, late = [lax.all_gather(part, "ep", axis=0, tiled=True)], []
        order = jnp.zeros((1,), jnp.int32)
        rows = expert_rows(hidden[0], *layer)
    else:
        early, late, marks = gather(part)
        z, y, x = place_of(lax.axis_index("ep"))
        order = jnp.stack([index_of(z - dz, y ^ dy, x ^ dx) for dz, dy, dx in EARLY + LATE])
        rows = expert_layer(marks, hidden[0], *layer)
    memory, target, mixed = both_norms(
        hidden[0], other_hidden, final_gain[0], places(expert_ids[0], slot_ids[0]), rows, targets
    )

    seg_q = positions(tgt_len[0], targets)
    seg_k = positions(src_len[0], rows_here)
    valid = (seg_q < SENT)[:, None]
    sums = project(order, memory, target, early)
    own, sent = attend(order, seg_q, seg_k, memory, target, sums, early, late)
    total = own + lax.ppermute(sent, "grp", [(0, 1)]).astype(jnp.float32)
    attended = jnp.pad(jnp.where(valid, total, 0.0), ((0, rows_here - targets), (0, 0)))
    decoded = (mixed + attended).astype(jnp.bfloat16)
    return jnp.where(encoder, memory, decoded)[None]


def solution(mesh):
    in_specs = (
        P("grp", "ep", None),
        P("grp", None),
        P("grp", None),
        P("grp", None, None),
        P("grp", None, "ep"),
        P("grp", "ep", None),
        P("grp", "ep", None),
        P("grp", "ep", None),
        P("ep", None),
        P("ep", None),
        P("ep", None),
        P("ep", None),
        P("ep", None),
        P("ep", None),
    )
    out_specs = P("grp", "ep", None)
    return jax.shard_map(body, mesh=mesh, in_specs=in_specs, out_specs=out_specs, check_vma=False)
```

```python
import functools

import jax
import jax.numpy as jnp
from jax import lax
from jax.experimental import pallas as pl
from jax.experimental.pallas import tpu as pltpu
from jax.sharding import PartitionSpec as P

HD = 128
SPLIT = 8
C = 6
PAD = 8
SENT = 4
TGT_TOTAL = 171
MIB = 1 << 20


def normalize(values, gain):
    mean = jnp.mean(values, -1, keepdims=True)
    centred = values - mean
    spread = jnp.mean(centred * centred, -1, keepdims=True)
    return centred * lax.rsqrt(spread + 1e-05) * gain


def positions(lengths, count):
    upto = jnp.arange(SENT)[:, None] <= jnp.arange(SENT)[None, :]
    ends = jnp.sum(jnp.where(upto, lengths[:, None], 0), axis=0)
    above = (jnp.arange(count, dtype=jnp.int32)[:, None] >= ends[None, :]).astype(jnp.int32)
    return jnp.sum(above, axis=1)


def dot(left, right):
    return jnp.dot(left, right, preferred_element_type=jnp.float32)


def dot_rows(left, right):
    return lax.dot_general(
        left, right, (((1,), (1,)), ((), ())), preferred_element_type=jnp.float32
    )


def chips():
    return (4, 2, 2) if lax.axis_size("ep") == 16 else None


def place_of(index):
    depth, high, wide = chips()
    return index // (high * wide), index // wide % high, index % wide


def index_of(z, y, x):
    depth, high, wide = chips()
    return (z % depth * high + y) * wide + x


def moved(value, dz=0, dy=0, dx=0):
    pairs = []
    for source in range(lax.axis_size("ep")):
        z, y, x = place_of(source)
        pairs.append((source, index_of(z + dz, y ^ dy, x ^ dx)))
    return lax.ppermute(value, "ep", pairs)


def specs(smem, vmem, unread=0):
    return (
        [pl.BlockSpec(memory_space=pltpu.SMEM)] * smem
        + [pl.BlockSpec(memory_space=pltpu.VMEM)] * vmem
        + [pl.BlockSpec(memory_space=pltpu.HBM)] * unread
    )


def local(kernel, name, outs, vmem, after=(), onward=(), order=None, far=(), scratch=(), mib=6):
    scalars = () if order is None else (order,)
    read = len(scalars) + len(vmem) + len(far)
    unread = len(after) + len(onward)

    def run(*refs):
        results = refs[read + unread :]
        kernel(*refs[:read], *results[: len(outs)], *results[len(outs) + len(onward) :])

    first = read + len(after)
    return pl.pallas_call(
        run,
        out_shape=[jax.ShapeDtypeStruct(shape, dtype) for shape, dtype in outs]
        + [jax.ShapeDtypeStruct(array.shape, array.dtype) for array in onward],
        in_specs=specs(len(scalars), len(vmem), len(far) + unread),
        out_specs=specs(0, len(outs), len(onward)),
        scratch_shapes=list(scratch),
        input_output_aliases={first + i: len(outs) + i for i in range(len(onward))},
        compiler_params=pltpu.CompilerParams(vmem_limit_bytes=mib * MIB),
        name=name,
    )(*scalars, *vmem, *far, *after, *onward)


def pack_kernel(experts, place, both, hidden, gain, router, gate, send):
    count = gate.shape[0]
    slot = lax.broadcasted_iota(jnp.int32, (count, hidden.shape[0]), 0)
    table = slot == place[...]
    rows = dot(table.astype(jnp.bfloat16), hidden[...])
    normed = normalize(rows, gain[...])
    send[...] = jnp.concatenate(
        [normed[e * PAD : (e + 1) * PAD] for e in experts], axis=0
    ).astype(jnp.bfloat16)
    logits = dot(normed.astype(jnp.bfloat16), router[...])
    mine = lax.broadcasted_iota(jnp.int32, (count, 1), 0) // PAD
    others = jnp.sum(jnp.where(table, both[...], 0), axis=1, keepdims=True) - mine
    expert = lax.broadcasted_iota(jnp.int32, logits.shape, 1)
    lead = jnp.where(expert == mine, logits, 0.0) - jnp.where(expert == others, logits, 0.0)
    gate[...] = 1.0 / (1.0 + jnp.exp(-jnp.sum(lead, axis=1, keepdims=True)))


def gate_kernel():
    pass


def mlp_kernel(rows, w_in, w_out, pieces):
    inner = jnp.maximum(dot(rows[...], w_in[...]), 0.0).astype(jnp.bfloat16)
    pieces[...] = dot(inner, w_out[...]).astype(jnp.bfloat16)


def rows_kernel(experts, gate, parts, rows):
    count = gate.shape[0]
    summed = [None] * (count // PAD)
    for i, e in enumerate(experts):
        part = parts[i * PAD : (i + 1) * PAD].astype(jnp.float32)
        summed[e] = part if summed[e] is None else summed[e] + part
    rows[...] = gate[...] * jnp.concatenate(summed, axis=0)


def mixed_rows(hidden, place, rows_ref):
    rows = rows_ref[...]
    count, size = rows.shape[0], hidden.shape[0]
    high = rows.astype(jnp.bfloat16)
    rest = rows - high.astype(jnp.float32)
    middle = rest.astype(jnp.bfloat16)
    low = (rest - middle.astype(jnp.float32)).astype(jnp.bfloat16)
    slot = lax.broadcasted_iota(jnp.int32, (size, 3 * count), 1) % count
    picks = (slot.astype(jnp.float32) == place[...]).astype(jnp.bfloat16)
    added = dot(picks, jnp.concatenate([high, middle, low], axis=0))
    return hidden[...].astype(jnp.float32) + added


def norm_kernel(group, *refs):
    own, other, (memory, target, mixed) = refs[:4], refs[4:8], refs[8:]

    def run(source, wanted):
        hidden, place, rows, gain = source
        values = mixed_rows(hidden, place, rows)
        memory[...] = normalize(values, gain[...]).astype(jnp.bfloat16)
        hidden, place, rows, gain = wanted
        mixed[...] = mixed_rows(hidden, place, rows)
        target[...] = normalize(mixed[: target.shape[0]], gain[...]).astype(jnp.bfloat16)

    pl.when(group[0] == 0)(lambda: run(own, other))
    pl.when(group[0] != 0)(lambda: run(other, own))


def places(routes, slots):
    return jnp.max(jnp.where(slots >= 0, routes * PAD + slots, -1), axis=1)


def expert_rows(hidden, norm_gain, router, w_in, w_out, routes, slots):
    experts = lax.axis_size("ep") // SPLIT
    count = experts * PAD
    width = hidden.shape[1]
    table = jnp.arange(count)[:, None] == places(routes, slots)[None, :]
    rows = dot(table.astype(jnp.bfloat16), hidden)
    normed = normalize(rows, norm_gain).astype(jnp.bfloat16)
    outgoing = jnp.broadcast_to(normed.reshape(experts, 1, PAD, width), (experts, SPLIT, PAD, width))
    arrived = lax.all_to_all(
        outgoing.reshape(experts * SPLIT, PAD, width), "ep", split_axis=0, concat_axis=0, tiled=True
    ).reshape(-1, width)
    inner = jax.nn.relu(dot(arrived, w_in)).astype(jnp.bfloat16)
    piece = dot(inner, w_out).astype(jnp.bfloat16)
    back = lax.all_to_all(
        piece.reshape(-1, PAD, width), "ep", split_axis=0, concat_axis=0, tiled=True
    )
    summed = jnp.sum(back.reshape(experts, SPLIT, PAD, width).astype(jnp.float32), axis=1)
    logits = dot(normed, router)
    mine = jnp.arange(count) // PAD
    both = jnp.sum(routes, axis=1)
    others = jnp.sum(jnp.where(table, both[None, :], 0), axis=1) - mine
    ids = jnp.arange(router.shape[1])[None, :]
    sign = (ids == mine[:, None]).astype(jnp.float32) - (ids == others[:, None]).astype(jnp.float32)
    gate = jax.nn.sigmoid(jnp.sum(logits * sign, axis=1, keepdims=True))
    return gate * summed.reshape(count, width)


def expert_layer(marks, hidden, norm_gain, router, w_in, w_out, routes, slots):
    devices = lax.axis_size("ep")
    experts = devices // SPLIT
    width = hidden.shape[1]
    place = places(routes, slots)
    held = [device // SPLIT for device in range(devices)]
    blocks = (devices * PAD, width)

    def exchanged(values):
        parts = values.reshape(devices, PAD, width)
        parts = lax.all_to_all(parts, "ep", split_axis=0, concat_axis=0, tiled=True)
        return parts.reshape(values.shape)

    gate, send = local(
        functools.partial(pack_kernel, held),
        "pack",
        [((experts * PAD, 1), jnp.float32), (blocks, jnp.bfloat16)],
        (place[None, :], jnp.sum(routes, axis=1)[None, :], hidden, norm_gain[None, :], router),
    )
    (pieces,) = local(
        mlp_kernel,
        "mlp",
        [(blocks, jnp.bfloat16)],
        (exchanged(send), w_in, w_out),
        marks[0],
    )
    (rows,) = local(
        functools.partial(rows_kernel, held),
        "rows",
        [((experts * PAD, width), jnp.float32)],
        (gate, exchanged(pieces)),
        marks[1],
    )
    return rows


def both_norms(hidden, other_hidden, final_gain, place, rows, targets):
    swap = [(0, 1), (1, 0)]
    place = place[:, None].astype(jnp.float32)
    gain = final_gain[None, :]
    small = jnp.concatenate([gain, jnp.pad(place.T, ((0, 0), (0, gain.shape[1] - place.shape[0])))])
    small = lax.ppermute(small, "grp", swap)
    other_rows = lax.ppermute(rows, "grp", swap)
    own = (hidden, place, rows, gain)
    other = (other_hidden, small[1, : place.shape[0]][:, None], other_rows, small[:1])
    size, width = hidden.shape
    return local(
        norm_kernel,
        "norm",
        [
            ((size, width), jnp.bfloat16),
            ((targets, width), jnp.bfloat16),
            ((size, width), jnp.float32),
        ],
        (*own[:4], *other[:4]),
        order=lax.axis_index("grp")[None],
        mib=12,
    )


EARLY = [
    (0, 0, 0), (1, 0, 0), (2, 0, 0), (3, 0, 0), (0, 0, 1), (1, 0, 1), (0, 1, 0), (1, 1, 0),
    (2, 1, 0), (3, 1, 0), (0, 1, 1), (1, 1, 1), (2, 0, 1),
]
LATE = [(3, 0, 1), (3, 1, 1), (2, 1, 1)]


def gather(part):
    def once(there, *blocks):
        return local(gate_kernel, "gate", [], (), there, blocks)

    z1, x0, y0 = moved(part, dz=1), moved(part, dx=1), moved(part, dy=1)
    z1, y0 = once([x0], z1, y0)
    z2, far0, y1 = moved(z1, dz=1), moved(y0, dx=1), moved(z1, dy=1)
    z1, z2, far0 = once([y1], z1, z2, far0)
    second = [z2]
    z3, x1, y2 = moved(z2, dz=1), moved(z1, dx=1), moved(z2, dy=1)
    z2, z3, far0 = once([x1, y2], z2, z3, far0)
    far1, x2, y3 = moved(far0, dz=1), moved(z2, dx=1), moved(z3, dy=1)
    z3, far0, x2 = once([far1, y3], z3, far0, x2)
    fourth = [x2]
    far3, x3, far2 = moved(far0, dz=-1), moved(z3, dx=1), moved(x2, dy=1)
    early = [part, z1, z2, z3, x0, x1, y0, y1, y2, y3, far0, far1, x2]
    return early, [x3, far3, far2], (second, fourth)


def pairs_of(refs):
    return [tuple(range(low, min(low + 2, len(refs)))) for low in range(0, len(refs), 2)]


def joined(parts, axis):
    return parts[0] if len(parts) == 1 else jnp.concatenate(parts, axis=axis)


def fetched(blocks, columns, near, sems):
    rows = blocks[0].shape[0]
    copies = [
        pltpu.make_async_copy(
            block.at[:, columns], near.at[pl.ds(i * rows, rows)], sems.at[i]
        )
        for i, block in enumerate(blocks)
    ]
    for copy in copies:
        copy.start()
    return copies


def add_blocks(order, memory, target, near, copies, kv, q, fresh):
    rows = near.shape[0] // len(copies)
    half = q.shape[1]

    def columns(ref, members):
        return joined(
            [ref[:, pl.ds(pl.multiple_of(order[i] * rows, 128), rows)] for i in members], 1
        )

    for step, members in enumerate(pairs_of(copies)):
        for i in members:
            copies[i].wait()
        weights = near[members[0] * rows : (members[-1] + 1) * rows]
        kv_part = dot(columns(memory, members), weights[:, : 2 * half])
        q_part = dot(columns(target, members), weights[:, 2 * half :])
        if fresh and step == 0:
            kv[...] = kv_part
            q[...] = q_part
        else:
            kv[...] += kv_part
            q[...] += q_part


def project_kernel(count, order, memory, target, *refs):
    blocks, (kv, q, near, sems) = refs[:count], refs[count:]
    copies = fetched(blocks, pl.ds(0, near.shape[1]), near, sems)
    add_blocks(order, memory, target, near, copies, kv, q, True)


def attend_kernel(early, late, order, seg_q, seg_k, memory, target, kv_sum, q_sum, *refs):
    blocks = refs[: early + late]
    own, sent, kv, q, context, near, near_out, sems, sems_out = refs[early + late :]
    half = q.shape[1]
    rows = blocks[0].shape[0]
    kv[...] = kv_sum[...]
    q[...] = q_sum[...]
    if late:
        copies = fetched(blocks[early:], pl.ds(0, 3 * half), near, sems)
    copies_out = fetched(blocks, pl.ds(3 * half, half), near_out, sems_out)
    if late:
        late_order = [order[early + i] for i in range(late)]
        add_blocks(late_order, memory, target, near, copies, kv, q, False)
    allowed = seg_q[...] == seg_k[...]
    for low in range(0, half, HD):
        query = q[:, low : low + HD].astype(jnp.bfloat16)
        keys = kv[:, low : low + HD].astype(jnp.bfloat16)
        values = kv[:, half + low : half + low + HD].astype(jnp.bfloat16)
        scores = jnp.where(allowed, dot_rows(query, keys) * HD ** (-0.5), -1e30)
        expd = jnp.exp(scores - jnp.max(scores, axis=-1, keepdims=True))
        prob = (expd / jnp.sum(expd, axis=-1, keepdims=True)).astype(jnp.bfloat16)
        context[:, low : low + HD] = dot(prob, values).astype(jnp.bfloat16)
    for copy in copies_out:
        copy.wait()
    for members in pairs_of(blocks):
        part = dot_rows(context[...], near_out[members[0] * rows : (members[-1] + 1) * rows])
        for place, i in enumerate(members):
            columns = pl.ds(pl.multiple_of(order[i] * rows, 128), rows)
            value = part[:, place * rows : (place + 1) * rows]
            own[:, columns] = value
            sent[:, columns] = value.astype(jnp.bfloat16)


def finish_kernel(group, memory, mixed, own, received, valid, out):
    count = own.shape[0]

    @pl.when(group[0] == 0)
    def _():
        out[...] = memory[...]

    @pl.when(group[0] != 0)
    def _():
        total = own[...] + received[...].astype(jnp.float32)
        attended = jnp.where(valid[...] > 0.0, total, 0.0)
        out[:count] = (mixed[:count] + attended).astype(jnp.bfloat16)
        out[count:] = mixed[count:].astype(jnp.bfloat16)


def project(order, memory, target, blocks):
    rows, half = blocks[0].shape[0], blocks[0].shape[1] // 4
    return local(
        functools.partial(project_kernel, len(blocks)),
        "project",
        [((memory.shape[0], 2 * half), jnp.float32), ((target.shape[0], half), jnp.float32)],
        (memory, target),
        order=order,
        far=blocks,
        scratch=[
            pltpu.VMEM((len(blocks) * rows, 3 * half), jnp.bfloat16),
            pltpu.SemaphoreType.DMA((len(blocks),)),
        ],
        mib=52,
    )


def attend(order, seg_q, seg_k, memory, target, sums, early, late):
    rows, half = early[0].shape[0], early[0].shape[1] // 4
    count, width = target.shape
    blocks = len(early) + len(late)
    return local(
        functools.partial(attend_kernel, len(early), len(late)),
        "attend",
        [((count, width), jnp.float32), ((count, width), jnp.bfloat16)],
        (seg_q[:, None], seg_k[None, :], memory, target, *sums),
        order=order,
        far=(*early, *late),
        scratch=[
            pltpu.VMEM((memory.shape[0], 2 * half), jnp.float32),
            pltpu.VMEM((count, half), jnp.float32),
            pltpu.VMEM((count, half), jnp.bfloat16),
            pltpu.VMEM((max(len(late), 1) * rows, 3 * half), jnp.bfloat16),
            pltpu.VMEM((blocks * rows, half), jnp.bfloat16),
            pltpu.SemaphoreType.DMA((max(len(late), 1),)),
            pltpu.SemaphoreType.DMA((blocks,)),
        ],
        mib=52,
    )


def body(
    hidden,
    norm_gain,
    final_gain,
    router,
    w_in,
    w_out,
    expert_ids,
    slot_ids,
    src_len,
    tgt_len,
    wq,
    wk,
    wv,
    wo,
):
    group = lax.axis_index("grp")
    rows_here, width = hidden.shape[1:]
    half = wq.shape[1] // lax.axis_size("grp")
    targets = min(rows_here, -(-TGT_TOTAL // 16) * 16)

    def mine(*weights):
        return jnp.concatenate(
            [lax.dynamic_slice_in_dim(weight, group * half, half, 1) for weight in weights], axis=1
        )

    part = mine(wk, wv, wq, wo)
    other_hidden = lax.ppermute(hidden[0], "grp", [(0, 1), (1, 0)])
    layer = (norm_gain[0], router[0], w_in[0], w_out[0], expert_ids[0], slot_ids[0])
    if chips() is None:
        early, late = [lax.all_gather(part, "ep", axis=0, tiled=True)], []
        order = jnp.zeros((1,), jnp.int32)
        rows = expert_rows(hidden[0], *layer)
    else:
        early, late, marks = gather(part)
        z, y, x = place_of(lax.axis_index("ep"))
        order = jnp.stack([index_of(z - dz, y ^ dy, x ^ dx) for dz, dy, dx in EARLY + LATE])
        rows = expert_layer(marks, hidden[0], *layer)
    memory, target, mixed = both_norms(
        hidden[0], other_hidden, final_gain[0], places(expert_ids[0], slot_ids[0]), rows, targets
    )

    seg_q = positions(tgt_len[0], targets)
    seg_k = positions(src_len[0], rows_here)
    sums = project(order, memory, target, early)
    own, sent = attend(order, seg_q, seg_k, memory, target, sums, early, late)
    received = lax.ppermute(sent, "grp", [(0, 1)])
    (out,) = local(
        finish_kernel,
        "finish",
        [((rows_here, width), jnp.bfloat16)],
        (memory, mixed, own, received, (seg_q < SENT).astype(jnp.float32)[:, None]),
        order=group[None],
        mib=8,
    )
    return out[None]


def solution(mesh):
    in_specs = (
        P("grp", "ep", None),
        P("grp", None),
        P("grp", None),
        P("grp", None, None),
        P("grp", None, "ep"),
        P("grp", "ep", None),
        P("grp", "ep", None),
        P("grp", "ep", None),
        P("ep", None),
        P("ep", None),
        P("ep", None),
        P("ep", None),
        P("ep", None),
        P("ep", None),
    )
    out_specs = P("grp", "ep", None)
    return jax.shard_map(body, mesh=mesh, in_specs=in_specs, out_specs=out_specs, check_vma=False)
```

```python
import functools

import jax
import jax.numpy as jnp
from jax import lax
from jax.experimental import pallas as pl
from jax.experimental.pallas import tpu as pltpu
from jax.sharding import PartitionSpec as P

HD = 128
SPLIT = 8
C = 6
PAD = 8
SENT = 4
TGT_TOTAL = 171
MIB = 1 << 20


def normalize(values, gain):
    mean = jnp.mean(values, -1, keepdims=True)
    centred = values - mean
    spread = jnp.mean(centred * centred, -1, keepdims=True)
    return centred * lax.rsqrt(spread + 1e-05) * gain


def positions(lengths, count):
    upto = jnp.arange(SENT)[:, None] <= jnp.arange(SENT)[None, :]
    ends = jnp.sum(jnp.where(upto, lengths[:, None], 0), axis=0)
    above = (jnp.arange(count, dtype=jnp.int32)[:, None] >= ends[None, :]).astype(jnp.int32)
    return jnp.sum(above, axis=1)


def dot(left, right):
    return jnp.dot(left, right, preferred_element_type=jnp.float32)


def dot_rows(left, right):
    return lax.dot_general(
        left, right, (((1,), (1,)), ((), ())), preferred_element_type=jnp.float32
    )


def chips():
    return (4, 2, 2) if lax.axis_size("ep") == 16 else None


def place_of(index):
    depth, high, wide = chips()
    return index // (high * wide), index // wide % high, index % wide


def index_of(z, y, x):
    depth, high, wide = chips()
    return (z % depth * high + y) * wide + x


def moved(value, dz=0, dy=0, dx=0):
    pairs = []
    for source in range(lax.axis_size("ep")):
        z, y, x = place_of(source)
        pairs.append((source, index_of(z + dz, y ^ dy, x ^ dx)))
    return lax.ppermute(value, "ep", pairs)


def local(kernel, name, outs, vmem, order=None, updated=(), after=(), onward=(), scratch=(), mib=6):
    scalars = () if order is None else (order,)
    read = len(scalars) + len(vmem)
    kept = (*updated, *onward)
    first = read + len(after)

    def run(*refs):
        results = refs[first + len(kept) :]
        changed = len(outs) + len(updated)
        kernel(*refs[:read], *results[:changed], *results[len(outs) + len(kept) :])

    def specs(vmem, anywhere):
        return [pl.BlockSpec(memory_space=pltpu.VMEM)] * vmem + [
            pl.BlockSpec(memory_space=pl.ANY)
        ] * anywhere

    inward = specs(len(vmem), len(after)) + specs(len(updated), len(onward))
    return pl.pallas_call(
        run,
        out_shape=[jax.ShapeDtypeStruct(shape, dtype) for shape, dtype in outs]
        + [jax.ShapeDtypeStruct(array.shape, array.dtype) for array in kept],
        in_specs=[pl.BlockSpec(memory_space=pltpu.SMEM)] * len(scalars) + inward,
        out_specs=specs(len(outs) + len(updated), len(onward)),
        scratch_shapes=list(scratch),
        input_output_aliases={first + i: len(outs) + i for i in range(len(kept))},
        compiler_params=pltpu.CompilerParams(vmem_limit_bytes=mib * MIB),
        name=name,
    )(*scalars, *vmem, *after, *kept)


def pack_kernel(experts, place, both, hidden, gain, router, gate, send):
    count = gate.shape[0]
    slot = lax.broadcasted_iota(jnp.int32, (count, hidden.shape[0]), 0)
    table = slot == place[...]
    rows = dot(table.astype(jnp.bfloat16), hidden[...])
    normed = normalize(rows, gain[...])
    send[...] = jnp.concatenate(
        [normed[e * PAD : (e + 1) * PAD] for e in experts], axis=0
    ).astype(jnp.bfloat16)
    logits = dot(normed.astype(jnp.bfloat16), router[...])
    mine = lax.broadcasted_iota(jnp.int32, (count, 1), 0) // PAD
    others = jnp.sum(jnp.where(table, both[...], 0), axis=1, keepdims=True) - mine
    expert = lax.broadcasted_iota(jnp.int32, logits.shape, 1)
    lead = jnp.where(expert == mine, logits, 0.0) - jnp.where(expert == others, logits, 0.0)
    gate[...] = 1.0 / (1.0 + jnp.exp(-jnp.sum(lead, axis=1, keepdims=True)))


def gate_kernel(*refs):
    pass


def mlp_kernel(rows, w_in, w_out, pieces):
    inner = jnp.maximum(dot(rows[...], w_in[...]), 0.0).astype(jnp.bfloat16)
    pieces[...] = dot(inner, w_out[...]).astype(jnp.bfloat16)


def rows_kernel(experts, gate, parts, rows):
    count = gate.shape[0]
    summed = [None] * (count // PAD)
    for i, e in enumerate(experts):
        part = parts[i * PAD : (i + 1) * PAD].astype(jnp.float32)
        summed[e] = part if summed[e] is None else summed[e] + part
    rows[...] = gate[...] * jnp.concatenate(summed, axis=0)


def mixed_rows(hidden, place, rows_ref):
    rows = rows_ref[...]
    count, size = rows.shape[0], hidden.shape[0]
    high = rows.astype(jnp.bfloat16)
    rest = rows - high.astype(jnp.float32)
    middle = rest.astype(jnp.bfloat16)
    low = (rest - middle.astype(jnp.float32)).astype(jnp.bfloat16)
    slot = lax.broadcasted_iota(jnp.int32, (size, 3 * count), 1) % count
    picks = (slot.astype(jnp.float32) == place[...]).astype(jnp.bfloat16)
    added = dot(picks, jnp.concatenate([high, middle, low], axis=0))
    return hidden[...].astype(jnp.float32) + added


def norm_kernel(group, *refs):
    own, other, (memory, target, mixed) = refs[:4], refs[4:8], refs[8:]

    def run(source, wanted):
        hidden, place, rows, gain = source
        values = mixed_rows(hidden, place, rows)
        memory[...] = normalize(values, gain[...]).astype(jnp.bfloat16)
        hidden, place, rows, gain = wanted
        mixed[...] = mixed_rows(hidden, place, rows)
        target[...] = normalize(mixed[: target.shape[0]], gain[...]).astype(jnp.bfloat16)

    pl.when(group[0] == 0)(lambda: run(own, other))
    pl.when(group[0] != 0)(lambda: run(other, own))


def places(routes, slots):
    return jnp.max(jnp.where(slots >= 0, routes * PAD + slots, -1), axis=1)


def expert_rows(hidden, norm_gain, router, w_in, w_out, routes, slots):
    experts = lax.axis_size("ep") // SPLIT
    count = experts * PAD
    width = hidden.shape[1]
    table = jnp.arange(count)[:, None] == places(routes, slots)[None, :]
    rows = dot(table.astype(jnp.bfloat16), hidden)
    normed = normalize(rows, norm_gain).astype(jnp.bfloat16)
    outgoing = jnp.broadcast_to(normed.reshape(experts, 1, PAD, width), (experts, SPLIT, PAD, width))
    arrived = lax.all_to_all(
        outgoing.reshape(experts * SPLIT, PAD, width), "ep", split_axis=0, concat_axis=0, tiled=True
    ).reshape(-1, width)
    inner = jax.nn.relu(dot(arrived, w_in)).astype(jnp.bfloat16)
    piece = dot(inner, w_out).astype(jnp.bfloat16)
    back = lax.all_to_all(
        piece.reshape(-1, PAD, width), "ep", split_axis=0, concat_axis=0, tiled=True
    )
    summed = jnp.sum(back.reshape(experts, SPLIT, PAD, width).astype(jnp.float32), axis=1)
    logits = dot(normed, router)
    mine = jnp.arange(count) // PAD
    both = jnp.sum(routes, axis=1)
    others = jnp.sum(jnp.where(table, both[None, :], 0), axis=1) - mine
    ids = jnp.arange(router.shape[1])[None, :]
    sign = (ids == mine[:, None]).astype(jnp.float32) - (ids == others[:, None]).astype(jnp.float32)
    gate = jax.nn.sigmoid(jnp.sum(logits * sign, axis=1, keepdims=True))
    return gate * summed.reshape(count, width)


def expert_layer(marks, hidden, norm_gain, router, w_in, w_out, routes, slots):
    devices = lax.axis_size("ep")
    held = [device // SPLIT for device in range(devices)]
    width = hidden.shape[1]

    def exchanged(values):
        parts = values.reshape(devices, PAD, width)
        parts = lax.all_to_all(parts, "ep", split_axis=0, concat_axis=0, tiled=True)
        return parts.reshape(values.shape)

    gate, send = local(
        functools.partial(pack_kernel, held),
        "pack",
        [((devices // SPLIT * PAD, 1), jnp.float32), ((devices * PAD, width), jnp.bfloat16)],
        (
            places(routes, slots)[None, :],
            jnp.sum(routes, axis=1)[None, :],
            hidden,
            norm_gain[None, :],
            router,
        ),
    )
    (pieces,) = local(
        mlp_kernel,
        "mlp",
        [(send.shape, jnp.bfloat16)],
        (exchanged(send), w_in, w_out),
        after=[marks[0]],
    )
    (rows,) = local(
        functools.partial(rows_kernel, held),
        "rows",
        [((gate.shape[0], width), jnp.float32)],
        (gate, exchanged(pieces)),
        after=[marks[1]],
    )
    return rows


def both_norms(hidden, others, small, final_gain, rows, targets):
    other_hidden, other_small = others
    other_rows = lax.ppermute(rows, "grp", [(0, 1), (1, 0)])
    size, width = hidden.shape
    own = (hidden, small[1, :size][:, None], rows, small[:1])
    other = (other_hidden, other_small[1, :size][:, None], other_rows, other_small[:1])
    return local(
        norm_kernel,
        "norm",
        [
            ((size, width), jnp.bfloat16),
            ((targets, width), jnp.bfloat16),
            ((size, width), jnp.float32),
        ],
        (*own, *other),
        order=lax.axis_index("grp")[None],
        mib=12,
    )


def collect_kernel(order, *refs):
    blocks, gathered = refs[:-1], refs[-1]
    rows = blocks[0].shape[0]
    for i, block in enumerate(blocks):
        gathered[pl.ds(pl.multiple_of(order[i] * rows, rows), rows)] = block[...]


def first_kernel(count, order, *refs):
    collect_kernel(order, *refs)
    gathered, rows = refs[-1], refs[0].shape[0]
    for i in range(count, order.shape[0]):
        empty = jnp.zeros((rows, gathered.shape[1]), gathered.dtype)
        gathered[pl.ds(pl.multiple_of(order[i] * rows, rows), rows)] = empty


def gather(part):
    z, y, x = place_of(lax.axis_index("ep"))

    def order(*steps):
        return jnp.stack([index_of(z - dz, y ^ dy, x ^ dx) for dz, dy, dx in steps])

    def once(there, *blocks, near=()):
        return local(gate_kernel, "gate", [], near, after=there, onward=blocks)

    def collected(gathered, blocks, *steps):
        return local(
            collect_kernel, "collect", [], blocks, order=order(*steps), updated=[gathered]
        )[0]

    last = ((3, 0, 1), (3, 1, 1), (2, 1, 1))
    z1, x0, y0 = moved(part, dz=1), moved(part, dx=1), moved(part, dy=1)
    z1, y0 = once([x0], z1, y0)
    z2, far0, y1 = moved(z1, dz=1), moved(y0, dx=1), moved(z1, dy=1)
    (gathered,) = local(
        functools.partial(first_kernel, 4),
        "first",
        [((part.shape[0] * lax.axis_size("ep"), part.shape[1]), part.dtype)],
        (part, z1, x0, y0),
        order=order((0, 0, 0), (1, 0, 0), (0, 0, 1), (0, 1, 0), *last),
    )
    z1, z2, far0 = once([y1], z1, z2, far0, near=[gathered])
    z3, x1, y2 = moved(z2, dz=1), moved(z1, dx=1), moved(z2, dy=1)
    marks = [z2]
    gathered = collected(gathered, (z2, far0, y1), (2, 0, 0), (0, 1, 1), (1, 1, 0))
    z2, z3, far0 = once([x1, y2], z2, z3, far0, near=[gathered])
    far1, x2, y3 = moved(far0, dz=1), moved(z2, dx=1), moved(z3, dy=1)
    gathered = collected(gathered, (z3, x1, y2), (3, 0, 0), (1, 0, 1), (2, 1, 0))
    z3, far0, x2 = once([far1, y3], z3, far0, x2, near=[gathered])
    marks.append(x2)
    far3, x3, far2 = moved(far0, dz=-1), moved(z3, dx=1), moved(x2, dy=1)
    gathered = collected(gathered, (far1, x2, y3), (1, 1, 1), (2, 0, 1), (3, 1, 0))
    return gathered, (x3, far3, far2), order(*last), marks


def project_kernel(memory, target, gathered, kv, q):
    half = q.shape[1]
    for low in range(0, gathered.shape[0], 256):
        rows = slice(low, low + 256)
        kv_part = dot(memory[:, rows], gathered[rows, : 2 * half])
        q_part = dot(target[:, rows], gathered[rows, 2 * half : 3 * half])
        if low == 0:
            kv[...] = kv_part
            q[...] = q_part
        else:
            kv[...] += kv_part
            q[...] += q_part


def attend_kernel(count, order, seg_q, seg_k, memory, target, gathered, *refs):
    blocks, (sent, kv, q, mixed, context) = refs[:count], refs[count:]
    half = q.shape[1]
    rows = blocks[0].shape[0] if blocks else 0
    targets = target.shape[0]
    places = [pl.ds(pl.multiple_of(order[i] * rows, 128), rows) for i in range(count)]
    for block, columns in zip(blocks, places):
        kv[...] += dot(memory[:, columns], block[:, : 2 * half])
        q[...] += dot(target[:, columns], block[:, 2 * half : 3 * half])
    allowed = seg_q[...] == seg_k[...]
    for low in range(0, half, HD):
        query = q[:, low : low + HD].astype(jnp.bfloat16)
        keys = kv[:, low : low + HD].astype(jnp.bfloat16)
        values = kv[:, half + low : half + low + HD].astype(jnp.bfloat16)
        scores = jnp.where(allowed, dot_rows(query, keys) * HD ** (-0.5), -1e30)
        expd = jnp.exp(scores - jnp.max(scores, axis=-1, keepdims=True))
        prob = (expd / jnp.sum(expd, axis=-1, keepdims=True)).astype(jnp.bfloat16)
        context[:, low : low + HD] = dot(prob, values).astype(jnp.bfloat16)
    valid = (seg_q[...] < SENT).astype(jnp.float32)
    for low in range(0, gathered.shape[0], 256):
        part = dot_rows(context[...], gathered[low : low + 256, 3 * half :]) * valid
        sent[:, low : low + 256] = part.astype(jnp.bfloat16)
        mixed[:targets, low : low + 256] += part
    for block, columns in zip(blocks, places):
        part = dot_rows(context[...], block[:, 3 * half :]) * valid
        sent[:, columns] = part.astype(jnp.bfloat16)
        mixed[:targets, columns] += part


def attended(order, seg_q, seg_k, memory, target, gathered, late, kv, q, mixed):
    return local(
        functools.partial(attend_kernel, len(late)),
        "attend",
        [(target.shape, jnp.bfloat16)],
        (seg_q[:, None], seg_k[None, :], memory, target, gathered, *late),
        order=order,
        updated=[kv, q, mixed],
        scratch=[pltpu.VMEM(q.shape, jnp.bfloat16)],
    )


def finish_kernel(group, memory, mixed, received, out):
    count = received.shape[0]

    @pl.when(group[0] == 0)
    def _():
        out[...] = memory[...]

    @pl.when(group[0] != 0)
    def _():
        out[:count] = (mixed[:count] + received[...].astype(jnp.float32)).astype(jnp.bfloat16)
        out[count:] = mixed[count:].astype(jnp.bfloat16)


def body(
    hidden,
    norm_gain,
    final_gain,
    router,
    w_in,
    w_out,
    expert_ids,
    slot_ids,
    src_len,
    tgt_len,
    wq,
    wk,
    wv,
    wo,
):
    group = lax.axis_index("grp")
    rows_here, width = hidden.shape[1:]
    half = wq.shape[1] // lax.axis_size("grp")
    targets = min(rows_here, -(-TGT_TOTAL // 16) * 16)

    def mine(*weights):
        return jnp.concatenate(
            [lax.dynamic_slice_in_dim(weight, group * half, half, 1) for weight in weights], axis=1
        )

    tokens, routes, slots = hidden[0], expert_ids[0], slot_ids[0]
    place = places(routes, slots).astype(jnp.float32)
    small = jnp.stack([final_gain[0], jnp.pad(place, (0, width - rows_here))])
    part = mine(wk, wv, wq, wo)
    if chips() is None:
        gathered, late = lax.all_gather(part, "ep", axis=0, tiled=True), ()
        late_order = jnp.zeros((1,), jnp.int32)
        rows = expert_rows(tokens, norm_gain[0], router[0], w_in[0], w_out[0], routes, slots)
    else:
        gathered, late, late_order, marks = gather(part)
        rows = expert_layer(
            marks, tokens, norm_gain[0], router[0], w_in[0], w_out[0], routes, slots
        )
    others = [lax.ppermute(value, "grp", [(0, 1), (1, 0)]) for value in (tokens, small)]
    memory, target, mixed = both_norms(tokens, others, small, final_gain[0], rows, targets)

    seg_q = positions(tgt_len[0], targets)
    seg_k = positions(src_len[0], rows_here)
    kv, q = local(
        project_kernel,
        "project",
        [((rows_here, 2 * half), jnp.float32), ((targets, half), jnp.float32)],
        (memory, target, gathered),
    )
    sent, _, _, mixed = attended(
        late_order, seg_q, seg_k, memory, target, gathered, late, kv, q, mixed
    )
    received = lax.ppermute(sent, "grp", [(0, 1)])
    (out,) = local(
        finish_kernel,
        "finish",
        [((rows_here, width), jnp.bfloat16)],
        (memory, mixed, received),
        order=group[None],
    )
    return out[None]


def solution(mesh):
    in_specs = (
        P("grp", "ep", None),
        P("grp", None),
        P("grp", None),
        P("grp", None, None),
        P("grp", None, "ep"),
        P("grp", "ep", None),
        P("grp", "ep", None),
        P("grp", "ep", None),
        P("ep", None),
        P("ep", None),
        P("ep", None),
        P("ep", None),
        P("ep", None),
        P("ep", None),
    )
    out_specs = P("grp", "ep", None)
    return jax.shard_map(body, mesh=mesh, in_specs=in_specs, out_specs=out_specs, check_vma=False)
```

```python
import functools

import jax
import jax.numpy as jnp
from jax import lax
from jax.experimental import pallas as pl
from jax.experimental.pallas import tpu as pltpu
from jax.sharding import PartitionSpec as P

HD = 128
SPLIT = 8
C = 6
PAD = 8
SENT = 4
TGT_TOTAL = 171
MIB = 1 << 20


def normalize(values, gain):
    mean = jnp.mean(values, -1, keepdims=True)
    centred = values - mean
    spread = jnp.mean(centred * centred, -1, keepdims=True)
    return centred * lax.rsqrt(spread + 1e-05) * gain


def positions(lengths, count):
    upto = jnp.arange(SENT)[:, None] <= jnp.arange(SENT)[None, :]
    ends = jnp.sum(jnp.where(upto, lengths[:, None], 0), axis=0)
    above = (jnp.arange(count, dtype=jnp.int32)[:, None] >= ends[None, :]).astype(jnp.int32)
    return jnp.sum(above, axis=1)


def dot(left, right):
    return jnp.dot(left, right, preferred_element_type=jnp.float32)


def dot_rows(left, right):
    return lax.dot_general(
        left, right, (((1,), (1,)), ((), ())), preferred_element_type=jnp.float32
    )


def chips():
    return (4, 2, 2) if lax.axis_size("ep") == 16 else None


def place_of(index):
    depth, high, wide = chips()
    return index // (high * wide), index // wide % high, index % wide


def index_of(z, y, x):
    depth, high, wide = chips()
    return (z % depth * high + y) * wide + x


def moved(value, dz=0, dy=0, dx=0):
    pairs = []
    for source in range(lax.axis_size("ep")):
        z, y, x = place_of(source)
        pairs.append((source, index_of(z + dz, y ^ dy, x ^ dx)))
    return lax.ppermute(value, "ep", pairs)


def specs(smem, vmem, unread=0):
    return (
        [pl.BlockSpec(memory_space=pltpu.SMEM)] * smem
        + [pl.BlockSpec(memory_space=pltpu.VMEM)] * vmem
        + [pl.BlockSpec(memory_space=pltpu.HBM)] * unread
    )


def local(kernel, name, outs, vmem, after=(), onward=(), order=None, far=(), scratch=(), mib=6):
    scalars = () if order is None else (order,)
    read = len(scalars) + len(vmem) + len(far)
    unread = len(after) + len(onward)

    def run(*refs):
        results = refs[read + unread :]
        kernel(*refs[:read], *results[: len(outs)], *results[len(outs) + len(onward) :])

    first = read + len(after)
    return pl.pallas_call(
        run,
        out_shape=[jax.ShapeDtypeStruct(shape, dtype) for shape, dtype in outs]
        + [jax.ShapeDtypeStruct(array.shape, array.dtype) for array in onward],
        in_specs=specs(len(scalars), len(vmem), len(far) + unread),
        out_specs=specs(0, len(outs), len(onward)),
        scratch_shapes=list(scratch),
        input_output_aliases={first + i: len(outs) + i for i in range(len(onward))},
        compiler_params=pltpu.CompilerParams(vmem_limit_bytes=mib * MIB),
        name=name,
    )(*scalars, *vmem, *far, *after, *onward)


def pack_kernel(held, place, both, hidden, gain, router, gate, own, other):
    count = gate.shape[0]
    slot = lax.broadcasted_iota(jnp.int32, (count, hidden.shape[0]), 0)
    table = slot == place[...]
    rows = dot(table.astype(jnp.bfloat16), hidden[...])
    normed = normalize(rows, gain[...])
    near, far = halves(held, normed)
    own[...] = near.astype(jnp.bfloat16)
    other[...] = far.astype(jnp.bfloat16)
    logits = dot(normed.astype(jnp.bfloat16), router[...])
    mine = lax.broadcasted_iota(jnp.int32, (count, 1), 0) // PAD
    others = jnp.sum(jnp.where(table, both[...], 0), axis=1, keepdims=True) - mine
    expert = lax.broadcasted_iota(jnp.int32, logits.shape, 1)
    lead = jnp.where(expert == mine, logits, 0.0) - jnp.where(expert == others, logits, 0.0)
    gate[...] = 1.0 / (1.0 + jnp.exp(-jnp.sum(lead, axis=1, keepdims=True)))


def halves(held, rows):
    first = held[0] == 0
    return jnp.where(first, rows[:PAD], rows[PAD:]), jnp.where(first, rows[PAD:], rows[:PAD])


def copies_kernel(own, arrived, out):
    rows = jnp.concatenate([ref[...].astype(jnp.float32) for ref in (own, arrived)], axis=0)
    rows = rows.astype(jnp.bfloat16)
    for low in range(0, out.shape[0], 2 * PAD):
        out[low : low + 2 * PAD] = rows


def sum_kernel(pieces, own, other):
    total = pieces[: 2 * PAD].astype(jnp.float32)
    for low in range(2 * PAD, pieces.shape[0], 2 * PAD):
        total = total + pieces[low : low + 2 * PAD].astype(jnp.float32)
    own[...] = total[:PAD]
    other[...] = total[PAD:]


def gate_kernel():
    pass


def mlp_kernel(rows, w_in, w_out, pieces, near_in, near_out, inner, sems):
    steps = sems.shape[1]
    wide = w_in.shape[1] // steps
    copies = []
    for i in range(steps):
        part = pl.ds(i * wide, wide)
        copies.append(pltpu.make_async_copy(w_in.at[:, part], near_in.at[:, part], sems.at[0, i]))
    for i in range(steps):
        part = pl.ds(i * wide, wide)
        copies.append(pltpu.make_async_copy(w_out.at[part], near_out.at[part], sems.at[1, i]))
    for copy in copies:
        copy.start()
    for i in range(steps):
        copies[i].wait()
        part = slice(i * wide, (i + 1) * wide)
        inner[:, part] = jnp.maximum(dot(rows[...], near_in[:, part]), 0.0).astype(jnp.bfloat16)
    for i in range(steps):
        copies[steps + i].wait()
    pieces[...] = dot(inner[...], near_out[...]).astype(jnp.bfloat16)


def rows_kernel(held, gate, own, arrived, rows):
    both = jnp.concatenate([own[...], arrived[...]], axis=0)
    rows[...] = gate[...] * jnp.concatenate(halves(held, both), axis=0)


def mixed_rows(hidden, place, rows_ref):
    rows = rows_ref[...]
    count, size = rows.shape[0], hidden.shape[0]
    high = rows.astype(jnp.bfloat16)
    rest = rows - high.astype(jnp.float32)
    middle = rest.astype(jnp.bfloat16)
    low = (rest - middle.astype(jnp.float32)).astype(jnp.bfloat16)
    slot = lax.broadcasted_iota(jnp.int32, (size, 3 * count), 1) % count
    picks = (slot.astype(jnp.float32) == place[...]).astype(jnp.bfloat16)
    added = dot(picks, jnp.concatenate([high, middle, low], axis=0))
    return hidden[...].astype(jnp.float32) + added


def norm_kernel(group, *refs):
    own, other, (memory, target, mixed) = refs[:4], refs[4:8], refs[8:]

    def run(source, wanted):
        hidden, place, rows, gain = source
        values = mixed_rows(hidden, place, rows)
        memory[...] = normalize(values, gain[...]).astype(jnp.bfloat16)
        hidden, place, rows, gain = wanted
        mixed[...] = mixed_rows(hidden, place, rows)
        target[...] = normalize(mixed[: target.shape[0]], gain[...]).astype(jnp.bfloat16)

    pl.when(group[0] == 0)(lambda: run(own, other))
    pl.when(group[0] != 0)(lambda: run(other, own))


def places(routes, slots):
    return jnp.max(jnp.where(slots >= 0, routes * PAD + slots, -1), axis=1)


def expert_rows(hidden, norm_gain, router, w_in, w_out, routes, slots):
    experts = lax.axis_size("ep") // SPLIT
    count = experts * PAD
    width = hidden.shape[1]
    table = jnp.arange(count)[:, None] == places(routes, slots)[None, :]
    rows = dot(table.astype(jnp.bfloat16), hidden)
    normed = normalize(rows, norm_gain).astype(jnp.bfloat16)
    outgoing = jnp.broadcast_to(normed.reshape(experts, 1, PAD, width), (experts, SPLIT, PAD, width))
    arrived = lax.all_to_all(
        outgoing.reshape(experts * SPLIT, PAD, width), "ep", split_axis=0, concat_axis=0, tiled=True
    ).reshape(-1, width)
    inner = jax.nn.relu(dot(arrived, w_in)).astype(jnp.bfloat16)
    piece = dot(inner, w_out).astype(jnp.bfloat16)
    back = lax.all_to_all(
        piece.reshape(-1, PAD, width), "ep", split_axis=0, concat_axis=0, tiled=True
    )
    summed = jnp.sum(back.reshape(experts, SPLIT, PAD, width).astype(jnp.float32), axis=1)
    logits = dot(normed, router)
    mine = jnp.arange(count) // PAD
    both = jnp.sum(routes, axis=1)
    others = jnp.sum(jnp.where(table, both[None, :], 0), axis=1) - mine
    ids = jnp.arange(router.shape[1])[None, :]
    sign = (ids == mine[:, None]).astype(jnp.float32) - (ids == others[:, None]).astype(jnp.float32)
    gate = jax.nn.sigmoid(jnp.sum(logits * sign, axis=1, keepdims=True))
    return gate * summed.reshape(count, width)


def expert_layer(marks, hidden, norm_gain, router, w_in, w_out, routes, slots):
    devices = lax.axis_size("ep")
    width = hidden.shape[1]
    depth = chips()[0]
    held = (place_of(lax.axis_index("ep"))[0] // (depth // 2))[None]
    groups = [list(range(low, low + SPLIT)) for low in range(0, devices, SPLIT)]
    small, wide = (PAD, width), (2 * PAD * SPLIT, width)

    def exchanged(values):
        parts = values.reshape(SPLIT, 2 * PAD, width)
        parts = lax.all_to_all(
            parts, "ep", split_axis=0, concat_axis=0, tiled=True, axis_index_groups=groups
        )
        return parts.reshape(values.shape)

    gate, own, other = local(
        pack_kernel,
        "pack",
        [((2 * PAD, 1), jnp.float32), (small, jnp.bfloat16), (small, jnp.bfloat16)],
        (
            places(routes, slots)[None, :],
            jnp.sum(routes, axis=1)[None, :],
            hidden,
            norm_gain[None, :],
            router,
        ),
        order=held,
    )
    (send,) = local(
        copies_kernel, "copies", [(wide, jnp.bfloat16)], (own, moved(other, dz=depth // 2))
    )
    (pieces,) = local(
        mlp_kernel,
        "mlp",
        [(wide, jnp.bfloat16)],
        (exchanged(send),),
        marks[0],
        far=(w_in, w_out),
        scratch=[
            pltpu.VMEM(w_in.shape, w_in.dtype),
            pltpu.VMEM(w_out.shape, w_out.dtype),
            pltpu.VMEM((wide[0], w_in.shape[1]), jnp.bfloat16),
            pltpu.SemaphoreType.DMA((2, 4)),
        ],
        mib=16,
    )
    own, other = local(
        sum_kernel, "sum", [(small, jnp.float32)] * 2, (exchanged(pieces),), marks[1]
    )
    (rows,) = local(
        rows_kernel,
        "rows",
        [((2 * PAD, width), jnp.float32)],
        (gate, own, moved(other, dz=depth // 2)),
        order=held,
    )
    return rows


def both_norms(hidden, other_hidden, final_gain, place, rows, targets):
    swap = [(0, 1), (1, 0)]
    place = place[:, None].astype(jnp.float32)
    gain = final_gain[None, :]
    small = jnp.concatenate([gain, jnp.pad(place.T, ((0, 0), (0, gain.shape[1] - place.shape[0])))])
    small = lax.ppermute(small, "grp", swap)
    other_rows = lax.ppermute(rows, "grp", swap)
    own = (hidden, place, rows, gain)
    other = (other_hidden, small[1, : place.shape[0]][:, None], other_rows, small[:1])
    size, width = hidden.shape
    return local(
        norm_kernel,
        "norm",
        [
            ((size, width), jnp.bfloat16),
            ((targets, width), jnp.bfloat16),
            ((size, width), jnp.float32),
        ],
        (*own[:4], *other[:4]),
        order=lax.axis_index("grp")[None],
        mib=12,
    )


EARLY = [
    (0, 0, 0), (1, 0, 0), (2, 0, 0), (3, 0, 0), (0, 0, 1), (1, 0, 1), (0, 1, 0), (1, 1, 0),
    (2, 1, 0), (3, 1, 0), (0, 1, 1), (1, 1, 1), (2, 0, 1),
]
LATE = [(3, 0, 1), (3, 1, 1), (2, 1, 1)]


def gather(part):
    def once(there, *blocks):
        return local(gate_kernel, "gate", [], (), there, blocks)

    z1, x0, y0 = moved(part, dz=1), moved(part, dx=1), moved(part, dy=1)
    z1, y0 = once([x0], z1, y0)
    z2, far0, y1 = moved(z1, dz=1), moved(y0, dx=1), moved(z1, dy=1)
    z1, z2, far0 = once([y1], z1, z2, far0)
    second = [z2]
    z3, x1, y2 = moved(z2, dz=1), moved(z1, dx=1), moved(z2, dy=1)
    z2, z3, far0 = once([x1, y2], z2, z3, far0)
    far1, x2, y3 = moved(far0, dz=1), moved(z2, dx=1), moved(z3, dy=1)
    z3, far0, x2 = once([far1, y3], z3, far0, x2)
    fourth = [x2]
    far3, x3, far2 = moved(far0, dz=-1), moved(z3, dx=1), moved(x2, dy=1)
    early = [part, z1, z2, z3, x0, x1, y0, y1, y2, y3, far0, far1, x2]
    return early, [x3, far3, far2], (second, fourth)


def pairs_of(refs):
    return [tuple(range(low, min(low + 2, len(refs)))) for low in range(0, len(refs), 2)]


def joined(parts, axis):
    return parts[0] if len(parts) == 1 else jnp.concatenate(parts, axis=axis)


def fetched(blocks, columns, near, sems):
    rows = blocks[0].shape[0]
    copies = [
        pltpu.make_async_copy(
            block.at[:, columns], near.at[pl.ds(i * rows, rows)], sems.at[i]
        )
        for i, block in enumerate(blocks)
    ]
    for copy in copies:
        copy.start()
    return copies


def add_blocks(order, memory, target, near, copies, kv, q, fresh):
    rows = near.shape[0] // len(copies)
    half = q.shape[1]

    def columns(ref, members):
        return joined(
            [ref[:, pl.ds(pl.multiple_of(order[i] * rows, 128), rows)] for i in members], 1
        )

    for step, members in enumerate(pairs_of(copies)):
        for i in members:
            copies[i].wait()
        weights = near[members[0] * rows : (members[-1] + 1) * rows]
        kv_part = dot(columns(memory, members), weights[:, : 2 * half])
        q_part = dot(columns(target, members), weights[:, 2 * half :])
        if fresh and step == 0:
            kv[...] = kv_part
            q[...] = q_part
        else:
            kv[...] += kv_part
            q[...] += q_part


def project_kernel(count, order, memory, target, *refs):
    blocks, (kv, q, near, sems) = refs[:count], refs[count:]
    copies = fetched(blocks, pl.ds(0, near.shape[1]), near, sems)
    add_blocks(order, memory, target, near, copies, kv, q, True)


def attend_kernel(early, late, order, seg_q, seg_k, memory, target, kv_sum, q_sum, *refs):
    blocks = refs[: early + late]
    own, sent, kv, q, context, near, near_out, sems, sems_out = refs[early + late :]
    half = q.shape[1]
    rows = blocks[0].shape[0]
    kv[...] = kv_sum[...]
    q[...] = q_sum[...]
    if late:
        copies = fetched(blocks[early:], pl.ds(0, 3 * half), near, sems)
    copies_out = fetched(blocks, pl.ds(3 * half, half), near_out, sems_out)
    if late:
        late_order = [order[early + i] for i in range(late)]
        add_blocks(late_order, memory, target, near, copies, kv, q, False)
    allowed = seg_q[...] == seg_k[...]
    for low in range(0, half, HD):
        query = q[:, low : low + HD].astype(jnp.bfloat16)
        keys = kv[:, low : low + HD].astype(jnp.bfloat16)
        values = kv[:, half + low : half + low + HD].astype(jnp.bfloat16)
        scores = jnp.where(allowed, dot_rows(query, keys) * HD ** (-0.5), -1e30)
        expd = jnp.exp(scores - jnp.max(scores, axis=-1, keepdims=True))
        prob = (expd / jnp.sum(expd, axis=-1, keepdims=True)).astype(jnp.bfloat16)
        context[:, low : low + HD] = dot(prob, values).astype(jnp.bfloat16)
    for copy in copies_out:
        copy.wait()
    for members in pairs_of(blocks):
        part = dot_rows(context[...], near_out[members[0] * rows : (members[-1] + 1) * rows])
        for place, i in enumerate(members):
            columns = pl.ds(pl.multiple_of(order[i] * rows, 128), rows)
            value = part[:, place * rows : (place + 1) * rows]
            own[:, columns] = value
            sent[:, columns] = value.astype(jnp.bfloat16)


def finish_kernel(group, memory, mixed, own, received, valid, out):
    count = own.shape[0]

    @pl.when(group[0] == 0)
    def _():
        out[...] = memory[...]

    @pl.when(group[0] != 0)
    def _():
        total = own[...] + received[...].astype(jnp.float32)
        attended = jnp.where(valid[...] > 0.0, total, 0.0)
        out[:count] = (mixed[:count] + attended).astype(jnp.bfloat16)
        out[count:] = mixed[count:].astype(jnp.bfloat16)


def project(order, memory, target, blocks):
    rows, half = blocks[0].shape[0], blocks[0].shape[1] // 4
    return local(
        functools.partial(project_kernel, len(blocks)),
        "project",
        [((memory.shape[0], 2 * half), jnp.float32), ((target.shape[0], half), jnp.float32)],
        (memory, target),
        order=order,
        far=blocks,
        scratch=[
            pltpu.VMEM((len(blocks) * rows, 3 * half), jnp.bfloat16),
            pltpu.SemaphoreType.DMA((len(blocks),)),
        ],
        mib=14,
    )


def attend(order, seg_q, seg_k, memory, target, sums, early, late):
    rows, half = early[0].shape[0], early[0].shape[1] // 4
    count, width = target.shape
    blocks = len(early) + len(late)
    return local(
        functools.partial(attend_kernel, len(early), len(late)),
        "attend",
        [((count, width), jnp.float32), ((count, width), jnp.bfloat16)],
        (seg_q[:, None], seg_k[None, :], memory, target, *sums),
        order=order,
        far=(*early, *late),
        scratch=[
            pltpu.VMEM((memory.shape[0], 2 * half), jnp.float32),
            pltpu.VMEM((count, half), jnp.float32),
            pltpu.VMEM((count, half), jnp.bfloat16),
            pltpu.VMEM((max(len(late), 1) * rows, 3 * half), jnp.bfloat16),
            pltpu.VMEM((blocks * rows, half), jnp.bfloat16),
            pltpu.SemaphoreType.DMA((max(len(late), 1),)),
            pltpu.SemaphoreType.DMA((blocks,)),
        ],
        mib=14,
    )


def body(
    hidden,
    norm_gain,
    final_gain,
    router,
    w_in,
    w_out,
    expert_ids,
    slot_ids,
    src_len,
    tgt_len,
    wq,
    wk,
    wv,
    wo,
):
    group = lax.axis_index("grp")
    rows_here, width = hidden.shape[1:]
    half = wq.shape[1] // lax.axis_size("grp")
    targets = min(rows_here, -(-TGT_TOTAL // 16) * 16)

    def mine(*weights):
        return jnp.concatenate(
            [lax.dynamic_slice_in_dim(weight, group * half, half, 1) for weight in weights], axis=1
        )

    part = mine(wk, wv, wq, wo)
    other_hidden = lax.ppermute(hidden[0], "grp", [(0, 1), (1, 0)])
    layer = (norm_gain[0], router[0], w_in[0], w_out[0], expert_ids[0], slot_ids[0])
    if chips() is None:
        early, late = [lax.all_gather(part, "ep", axis=0, tiled=True)], []
        order = jnp.zeros((1,), jnp.int32)
        rows = expert_rows(hidden[0], *layer)
    else:
        early, late, marks = gather(part)
        z, y, x = place_of(lax.axis_index("ep"))
        order = jnp.stack([index_of(z - dz, y ^ dy, x ^ dx) for dz, dy, dx in EARLY + LATE])
        rows = expert_layer(marks, hidden[0], *layer)
    memory, target, mixed = both_norms(
        hidden[0], other_hidden, final_gain[0], places(expert_ids[0], slot_ids[0]), rows, targets
    )

    seg_q = positions(tgt_len[0], targets)
    seg_k = positions(src_len[0], rows_here)
    sums = project(order, memory, target, early)
    own, sent = attend(order, seg_q, seg_k, memory, target, sums, early, late)
    received = lax.ppermute(sent, "grp", [(0, 1)])
    (out,) = local(
        finish_kernel,
        "finish",
        [((rows_here, width), jnp.bfloat16)],
        (memory, mixed, own, received, (seg_q < SENT).astype(jnp.float32)[:, None]),
        order=group[None],
        mib=8,
    )
    return out[None]


def solution(mesh):
    in_specs = (
        P("grp", "ep", None),
        P("grp", None),
        P("grp", None),
        P("grp", None, None),
        P("grp", None, "ep"),
        P("grp", "ep", None),
        P("grp", "ep", None),
        P("grp", "ep", None),
        P("ep", None),
        P("ep", None),
        P("ep", None),
        P("ep", None),
        P("ep", None),
        P("ep", None),
    )
    out_specs = P("grp", "ep", None)
    return jax.shard_map(body, mesh=mesh, in_specs=in_specs, out_specs=out_specs, check_vma=False)
```

```python
import functools

import jax
import jax.numpy as jnp
from jax import lax
from jax.experimental import pallas as pl
from jax.experimental.pallas import tpu as pltpu
from jax.sharding import PartitionSpec as P

HD = 128
SPLIT = 8
C = 6
PAD = 8
SENT = 4
TGT_TOTAL = 171
MIB = 1 << 20


def normalize(values, gain):
    mean = jnp.mean(values, -1, keepdims=True)
    centred = values - mean
    spread = jnp.mean(centred * centred, -1, keepdims=True)
    return centred * lax.rsqrt(spread + 1e-05) * gain


def positions(lengths, count):
    upto = jnp.arange(SENT)[:, None] <= jnp.arange(SENT)[None, :]
    ends = jnp.sum(jnp.where(upto, lengths[:, None], 0), axis=0)
    above = (jnp.arange(count, dtype=jnp.int32)[:, None] >= ends[None, :]).astype(jnp.int32)
    return jnp.sum(above, axis=1)


def dot(left, right):
    return jnp.dot(left, right, preferred_element_type=jnp.float32)


def dot_rows(left, right):
    return lax.dot_general(
        left, right, (((1,), (1,)), ((), ())), preferred_element_type=jnp.float32
    )


def chips():
    return (4, 2, 2) if lax.axis_size("ep") == 16 else None


def place_of(index):
    depth, high, wide = chips()
    return index // (high * wide), index // wide % high, index % wide


def index_of(z, y, x):
    depth, high, wide = chips()
    return (z % depth * high + y) * wide + x


def moved(value, dz=0, dy=0, dx=0):
    pairs = []
    for source in range(lax.axis_size("ep")):
        z, y, x = place_of(source)
        pairs.append((source, index_of(z + dz, y ^ dy, x ^ dx)))
    return lax.ppermute(value, "ep", pairs)


def specs(smem, vmem, unread=0):
    return (
        [pl.BlockSpec(memory_space=pltpu.SMEM)] * smem
        + [pl.BlockSpec(memory_space=pltpu.VMEM)] * vmem
        + [pl.BlockSpec(memory_space=pltpu.HBM)] * unread
    )


def local(kernel, name, outs, vmem, after=(), onward=(), order=None, far=(), scratch=(), mib=6):
    scalars = () if order is None else (order,)
    read = len(scalars) + len(vmem) + len(far)
    unread = len(after) + len(onward)

    def run(*refs):
        results = refs[read + unread :]
        kernel(*refs[:read], *results[: len(outs)], *results[len(outs) + len(onward) :])

    first = read + len(after)
    return pl.pallas_call(
        run,
        out_shape=[jax.ShapeDtypeStruct(shape, dtype) for shape, dtype in outs]
        + [jax.ShapeDtypeStruct(array.shape, array.dtype) for array in onward],
        in_specs=specs(len(scalars), len(vmem), len(far) + unread),
        out_specs=specs(0, len(outs), len(onward)),
        scratch_shapes=list(scratch),
        input_output_aliases={first + i: len(outs) + i for i in range(len(onward))},
        compiler_params=pltpu.CompilerParams(vmem_limit_bytes=mib * MIB),
        name=name,
    )(*scalars, *vmem, *far, *after, *onward)


def pack_kernel(experts, place, both, hidden, gain, router, gate, send):
    count = gate.shape[0]
    slot = lax.broadcasted_iota(jnp.int32, (count, hidden.shape[0]), 0)
    table = slot == place[...]
    rows = dot(table.astype(jnp.bfloat16), hidden[...])
    normed = normalize(rows, gain[...])
    send[...] = jnp.concatenate(
        [normed[e * PAD : (e + 1) * PAD] for e in experts], axis=0
    ).astype(jnp.bfloat16)
    logits = dot(normed.astype(jnp.bfloat16), router[...])
    mine = lax.broadcasted_iota(jnp.int32, (count, 1), 0) // PAD
    others = jnp.sum(jnp.where(table, both[...], 0), axis=1, keepdims=True) - mine
    expert = lax.broadcasted_iota(jnp.int32, logits.shape, 1)
    lead = jnp.where(expert == mine, logits, 0.0) - jnp.where(expert == others, logits, 0.0)
    gate[...] = 1.0 / (1.0 + jnp.exp(-jnp.sum(lead, axis=1, keepdims=True)))


def gate_kernel():
    pass


def mlp_kernel(rows, w_in, w_out, pieces):
    inner = jnp.maximum(dot(rows[...], w_in[...]), 0.0).astype(jnp.bfloat16)
    pieces[...] = dot(inner, w_out[...]).astype(jnp.bfloat16)


def rows_kernel(experts, gate, parts, rows):
    count = gate.shape[0]
    summed = [None] * (count // PAD)
    for i, e in enumerate(experts):
        part = parts[i * PAD : (i + 1) * PAD].astype(jnp.float32)
        summed[e] = part if summed[e] is None else summed[e] + part
    rows[...] = gate[...] * jnp.concatenate(summed, axis=0)


def mixed_rows(hidden, place, rows_ref):
    rows = rows_ref[...]
    count, size = rows.shape[0], hidden.shape[0]
    high = rows.astype(jnp.bfloat16)
    rest = rows - high.astype(jnp.float32)
    middle = rest.astype(jnp.bfloat16)
    low = (rest - middle.astype(jnp.float32)).astype(jnp.bfloat16)
    slot = lax.broadcasted_iota(jnp.int32, (size, 3 * count), 1) % count
    picks = (slot.astype(jnp.float32) == place[...]).astype(jnp.bfloat16)
    added = dot(picks, jnp.concatenate([high, middle, low], axis=0))
    return hidden[...].astype(jnp.float32) + added


def norm_kernel(group, *refs):
    own, other, (memory, target, mixed) = refs[:4], refs[4:8], refs[8:]

    def run(source, wanted):
        hidden, place, rows, gain = source
        values = mixed_rows(hidden, place, rows)
        memory[...] = normalize(values, gain[...]).astype(jnp.bfloat16)
        hidden, place, rows, gain = wanted
        mixed[...] = mixed_rows(hidden, place, rows)
        target[...] = normalize(mixed[: target.shape[0]], gain[...]).astype(jnp.bfloat16)

    pl.when(group[0] == 0)(lambda: run(own, other))
    pl.when(group[0] != 0)(lambda: run(other, own))


def places(routes, slots):
    return jnp.max(jnp.where(slots >= 0, routes * PAD + slots, -1), axis=1)


def expert_rows(hidden, norm_gain, router, w_in, w_out, routes, slots):
    experts = lax.axis_size("ep") // SPLIT
    count = experts * PAD
    width = hidden.shape[1]
    table = jnp.arange(count)[:, None] == places(routes, slots)[None, :]
    rows = dot(table.astype(jnp.bfloat16), hidden)
    normed = normalize(rows, norm_gain).astype(jnp.bfloat16)
    outgoing = jnp.broadcast_to(normed.reshape(experts, 1, PAD, width), (experts, SPLIT, PAD, width))
    arrived = lax.all_to_all(
        outgoing.reshape(experts * SPLIT, PAD, width), "ep", split_axis=0, concat_axis=0, tiled=True
    ).reshape(-1, width)
    inner = jax.nn.relu(dot(arrived, w_in)).astype(jnp.bfloat16)
    piece = dot(inner, w_out).astype(jnp.bfloat16)
    back = lax.all_to_all(
        piece.reshape(-1, PAD, width), "ep", split_axis=0, concat_axis=0, tiled=True
    )
    summed = jnp.sum(back.reshape(experts, SPLIT, PAD, width).astype(jnp.float32), axis=1)
    logits = dot(normed, router)
    mine = jnp.arange(count) // PAD
    both = jnp.sum(routes, axis=1)
    others = jnp.sum(jnp.where(table, both[None, :], 0), axis=1) - mine
    ids = jnp.arange(router.shape[1])[None, :]
    sign = (ids == mine[:, None]).astype(jnp.float32) - (ids == others[:, None]).astype(jnp.float32)
    gate = jax.nn.sigmoid(jnp.sum(logits * sign, axis=1, keepdims=True))
    return gate * summed.reshape(count, width)


def expert_layer(marks, hidden, norm_gain, router, w_in, w_out, routes, slots):
    devices = lax.axis_size("ep")
    experts = devices // SPLIT
    width = hidden.shape[1]
    place = places(routes, slots)
    held = [device // SPLIT for device in range(devices)]
    blocks = (devices * PAD, width)

    def exchanged(values):
        parts = values.reshape(devices, PAD, width)
        parts = lax.all_to_all(parts, "ep", split_axis=0, concat_axis=0, tiled=True)
        return parts.reshape(values.shape)

    gate, send = local(
        functools.partial(pack_kernel, held),
        "pack",
        [((experts * PAD, 1), jnp.float32), (blocks, jnp.bfloat16)],
        (place[None, :], jnp.sum(routes, axis=1)[None, :], hidden, norm_gain[None, :], router),
    )
    (pieces,) = local(
        mlp_kernel,
        "mlp",
        [(blocks, jnp.bfloat16)],
        (exchanged(send), w_in, w_out),
        marks[0],
    )
    (rows,) = local(
        functools.partial(rows_kernel, held),
        "rows",
        [((experts * PAD, width), jnp.float32)],
        (gate, exchanged(pieces)),
        marks[1],
    )
    return rows


def both_norms(hidden, other_hidden, final_gain, place, rows, targets):
    swap = [(0, 1), (1, 0)]
    place = place[:, None].astype(jnp.float32)
    gain = final_gain[None, :]
    small = jnp.concatenate([gain, jnp.pad(place.T, ((0, 0), (0, gain.shape[1] - place.shape[0])))])
    small = lax.ppermute(small, "grp", swap)
    other_rows = lax.ppermute(rows, "grp", swap)
    own = (hidden, place, rows, gain)
    other = (other_hidden, small[1, : place.shape[0]][:, None], other_rows, small[:1])
    size, width = hidden.shape
    return local(
        norm_kernel,
        "norm",
        [
            ((size, width), jnp.bfloat16),
            ((targets, width), jnp.bfloat16),
            ((size, width), jnp.float32),
        ],
        (*own[:4], *other[:4]),
        order=lax.axis_index("grp")[None],
        mib=12,
    )


EARLY = [
    (0, 0, 0), (1, 0, 0), (2, 0, 0), (3, 0, 0), (0, 0, 1), (1, 0, 1), (0, 1, 0), (1, 1, 0),
    (2, 1, 0), (3, 1, 0), (0, 1, 1), (1, 1, 1), (2, 0, 1),
]
LATE = [(3, 0, 1), (3, 1, 1), (2, 1, 1)]


def gather(part):
    def once(there, *blocks):
        return local(gate_kernel, "gate", [], (), there, blocks)

    z1, x0, y0 = moved(part, dz=1), moved(part, dx=1), moved(part, dy=1)
    z1, y0 = once([x0], z1, y0)
    z2, far0, y1 = moved(z1, dz=1), moved(y0, dx=1), moved(z1, dy=1)
    z1, z2, far0 = once([y1], z1, z2, far0)
    second = [z2]
    z3, x1, y2 = moved(z2, dz=1), moved(z1, dx=1), moved(z2, dy=1)
    z2, z3, far0 = once([x1, y2], z2, z3, far0)
    far1, x2, y3 = moved(far0, dz=1), moved(z2, dx=1), moved(z3, dy=1)
    z3, far0, x2 = once([far1, y3], z3, far0, x2)
    fourth = [x2]
    far3, x3, far2 = moved(far0, dz=-1), moved(z3, dx=1), moved(x2, dy=1)
    early = [part, z1, z2, z3, x0, x1, y0, y1, y2, y3, far0, far1, x2]
    return early, [x3, far3, far2], (second, fourth)


def pairs_of(refs):
    return [tuple(range(low, min(low + 2, len(refs)))) for low in range(0, len(refs), 2)]


def joined(parts, axis):
    return parts[0] if len(parts) == 1 else jnp.concatenate(parts, axis=axis)


AHEAD = 4


def fetched(blocks, columns, near, sems):
    rows = blocks[0].shape[0]
    copies = [
        pltpu.make_async_copy(
            block.at[:, columns], near.at[pl.ds(i * rows, rows)], sems.at[i]
        )
        for i, block in enumerate(blocks)
    ]
    for copy in copies[:AHEAD]:
        copy.start()
    return copies


def arrived(copies, members):
    for i in members:
        copies[i].wait()
        if i + AHEAD < len(copies):
            copies[i + AHEAD].start()


def add_blocks(order, memory, target, near, copies, kv, q, fresh):
    rows = near.shape[0] // len(copies)
    half = q.shape[1]

    def columns(ref, members):
        return joined(
            [ref[:, pl.ds(pl.multiple_of(order[i] * rows, 128), rows)] for i in members], 1
        )

    for step, members in enumerate(pairs_of(copies)):
        arrived(copies, members)
        weights = near[members[0] * rows : (members[-1] + 1) * rows]
        kv_part = dot(columns(memory, members), weights[:, : 2 * half])
        q_part = dot(columns(target, members), weights[:, 2 * half :])
        if fresh and step == 0:
            kv[...] = kv_part
            q[...] = q_part
        else:
            kv[...] += kv_part
            q[...] += q_part


def project_kernel(count, order, memory, target, *refs):
    blocks, (kv, q, near, sems) = refs[:count], refs[count:]
    copies = fetched(blocks, pl.ds(0, near.shape[1]), near, sems)
    add_blocks(order, memory, target, near, copies, kv, q, True)


def attend_kernel(early, late, order, seg_q, seg_k, memory, target, kv_sum, q_sum, *refs):
    blocks = refs[: early + late]
    own, sent, kv, q, context, near, near_out, sems, sems_out = refs[early + late :]
    half = q.shape[1]
    rows = blocks[0].shape[0]
    kv[...] = kv_sum[...]
    q[...] = q_sum[...]
    if late:
        copies = fetched(blocks[early:], pl.ds(0, 3 * half), near, sems)
        late_order = [order[early + i] for i in range(late)]
        add_blocks(late_order, memory, target, near, copies, kv, q, False)
    copies_out = fetched(blocks, pl.ds(3 * half, half), near_out, sems_out)
    allowed = seg_q[...] == seg_k[...]
    for low in range(0, half, HD):
        query = q[:, low : low + HD].astype(jnp.bfloat16)
        keys = kv[:, low : low + HD].astype(jnp.bfloat16)
        values = kv[:, half + low : half + low + HD].astype(jnp.bfloat16)
        scores = jnp.where(allowed, dot_rows(query, keys) * HD ** (-0.5), -1e30)
        expd = jnp.exp(scores - jnp.max(scores, axis=-1, keepdims=True))
        prob = (expd / jnp.sum(expd, axis=-1, keepdims=True)).astype(jnp.bfloat16)
        context[:, low : low + HD] = dot(prob, values).astype(jnp.bfloat16)
    for members in pairs_of(blocks):
        arrived(copies_out, members)
        part = dot_rows(context[...], near_out[members[0] * rows : (members[-1] + 1) * rows])
        for place, i in enumerate(members):
            columns = pl.ds(pl.multiple_of(order[i] * rows, 128), rows)
            value = part[:, place * rows : (place + 1) * rows]
            own[:, columns] = value
            sent[:, columns] = value.astype(jnp.bfloat16)


def finish_kernel(group, memory, mixed, own, received, valid, out):
    count = own.shape[0]

    @pl.when(group[0] == 0)
    def _():
        out[...] = memory[...]

    @pl.when(group[0] != 0)
    def _():
        total = own[...] + received[...].astype(jnp.float32)
        attended = jnp.where(valid[...] > 0.0, total, 0.0)
        out[:count] = (mixed[:count] + attended).astype(jnp.bfloat16)
        out[count:] = mixed[count:].astype(jnp.bfloat16)


def project(order, memory, target, blocks):
    rows, half = blocks[0].shape[0], blocks[0].shape[1] // 4
    return local(
        functools.partial(project_kernel, len(blocks)),
        "project",
        [((memory.shape[0], 2 * half), jnp.float32), ((target.shape[0], half), jnp.float32)],
        (memory, target),
        order=order,
        far=blocks,
        scratch=[
            pltpu.VMEM((len(blocks) * rows, 3 * half), jnp.bfloat16),
            pltpu.SemaphoreType.DMA((len(blocks),)),
        ],
        mib=52,
    )


def attend(order, seg_q, seg_k, memory, target, sums, early, late):
    rows, half = early[0].shape[0], early[0].shape[1] // 4
    count, width = target.shape
    blocks = len(early) + len(late)
    return local(
        functools.partial(attend_kernel, len(early), len(late)),
        "attend",
        [((count, width), jnp.float32), ((count, width), jnp.bfloat16)],
        (seg_q[:, None], seg_k[None, :], memory, target, *sums),
        order=order,
        far=(*early, *late),
        scratch=[
            pltpu.VMEM((memory.shape[0], 2 * half), jnp.float32),
            pltpu.VMEM((count, half), jnp.float32),
            pltpu.VMEM((count, half), jnp.bfloat16),
            pltpu.VMEM((max(len(late), 1) * rows, 3 * half), jnp.bfloat16),
            pltpu.VMEM((blocks * rows, half), jnp.bfloat16),
            pltpu.SemaphoreType.DMA((max(len(late), 1),)),
            pltpu.SemaphoreType.DMA((blocks,)),
        ],
        mib=52,
    )


def body(
    hidden,
    norm_gain,
    final_gain,
    router,
    w_in,
    w_out,
    expert_ids,
    slot_ids,
    src_len,
    tgt_len,
    wq,
    wk,
    wv,
    wo,
):
    group = lax.axis_index("grp")
    rows_here, width = hidden.shape[1:]
    half = wq.shape[1] // lax.axis_size("grp")
    targets = min(rows_here, -(-TGT_TOTAL // 16) * 16)

    def mine(*weights):
        return jnp.concatenate(
            [lax.dynamic_slice_in_dim(weight, group * half, half, 1) for weight in weights], axis=1
        )

    part = mine(wk, wv, wq, wo)
    other_hidden = lax.ppermute(hidden[0], "grp", [(0, 1), (1, 0)])
    layer = (norm_gain[0], router[0], w_in[0], w_out[0], expert_ids[0], slot_ids[0])
    if chips() is None:
        early, late = [lax.all_gather(part, "ep", axis=0, tiled=True)], []
        order = jnp.zeros((1,), jnp.int32)
        rows = expert_rows(hidden[0], *layer)
    else:
        early, late, marks = gather(part)
        z, y, x = place_of(lax.axis_index("ep"))
        order = jnp.stack([index_of(z - dz, y ^ dy, x ^ dx) for dz, dy, dx in EARLY + LATE])
        rows = expert_layer(marks, hidden[0], *layer)
    memory, target, mixed = both_norms(
        hidden[0], other_hidden, final_gain[0], places(expert_ids[0], slot_ids[0]), rows, targets
    )

    seg_q = positions(tgt_len[0], targets)
    seg_k = positions(src_len[0], rows_here)
    sums = project(order, memory, target, early)
    own, sent = attend(order, seg_q, seg_k, memory, target, sums, early, late)
    received = lax.ppermute(sent, "grp", [(0, 1)])
    (out,) = local(
        finish_kernel,
        "finish",
        [((rows_here, width), jnp.bfloat16)],
        (memory, mixed, own, received, (seg_q < SENT).astype(jnp.float32)[:, None]),
        order=group[None],
        mib=8,
    )
    return out[None]


def solution(mesh):
    in_specs = (
        P("grp", "ep", None),
        P("grp", None),
        P("grp", None),
        P("grp", None, None),
        P("grp", None, "ep"),
        P("grp", "ep", None),
        P("grp", "ep", None),
        P("grp", "ep", None),
        P("ep", None),
        P("ep", None),
        P("ep", None),
        P("ep", None),
        P("ep", None),
        P("ep", None),
    )
    out_specs = P("grp", "ep", None)
    return jax.shard_map(body, mesh=mesh, in_specs=in_specs, out_specs=out_specs, check_vma=False)
```

```python
import functools

import jax
import jax.numpy as jnp
from jax import lax
from jax.experimental import pallas as pl
from jax.experimental.pallas import tpu as pltpu
from jax.sharding import PartitionSpec as P

HD = 128
SPLIT = 8
C = 6
PAD = 8
SENT = 4
TGT_TOTAL = 171
MIB = 1 << 20


def normalize(values, gain):
    mean = jnp.mean(values, -1, keepdims=True)
    centred = values - mean
    spread = jnp.mean(centred * centred, -1, keepdims=True)
    return centred * lax.rsqrt(spread + 1e-05) * gain


def positions(lengths, count):
    upto = jnp.arange(SENT)[:, None] <= jnp.arange(SENT)[None, :]
    ends = jnp.sum(jnp.where(upto, lengths[:, None], 0), axis=0)
    above = (jnp.arange(count, dtype=jnp.int32)[:, None] >= ends[None, :]).astype(jnp.int32)
    return jnp.sum(above, axis=1)


def dot(left, right):
    return jnp.dot(left, right, preferred_element_type=jnp.float32)


def dot_rows(left, right):
    return lax.dot_general(
        left, right, (((1,), (1,)), ((), ())), preferred_element_type=jnp.float32
    )


def chips():
    return (4, 2, 2) if lax.axis_size("ep") == 16 else None


def place_of(index):
    depth, high, wide = chips()
    return index // (high * wide), index // wide % high, index % wide


def index_of(z, y, x):
    depth, high, wide = chips()
    return (z % depth * high + y) * wide + x


def moved(value, dz=0, dy=0, dx=0):
    pairs = []
    for source in range(lax.axis_size("ep")):
        z, y, x = place_of(source)
        pairs.append((source, index_of(z + dz, y ^ dy, x ^ dx)))
    return lax.ppermute(value, "ep", pairs)


def specs(smem, vmem, unread=0):
    return (
        [pl.BlockSpec(memory_space=pltpu.SMEM)] * smem
        + [pl.BlockSpec(memory_space=pltpu.VMEM)] * vmem
        + [pl.BlockSpec(memory_space=pltpu.HBM)] * unread
    )


def local(kernel, name, outs, vmem, after=(), onward=(), order=None, far=(), scratch=(), mib=6):
    scalars = () if order is None else (order,)
    read = len(scalars) + len(vmem) + len(far)
    unread = len(after) + len(onward)

    def run(*refs):
        results = refs[read + unread :]
        kernel(*refs[:read], *results[: len(outs)], *results[len(outs) + len(onward) :])

    first = read + len(after)
    return pl.pallas_call(
        run,
        out_shape=[jax.ShapeDtypeStruct(shape, dtype) for shape, dtype in outs]
        + [jax.ShapeDtypeStruct(array.shape, array.dtype) for array in onward],
        in_specs=specs(len(scalars), len(vmem), len(far) + unread),
        out_specs=specs(0, len(outs), len(onward)),
        scratch_shapes=list(scratch),
        input_output_aliases={first + i: len(outs) + i for i in range(len(onward))},
        compiler_params=pltpu.CompilerParams(vmem_limit_bytes=mib * MIB),
        name=name,
    )(*scalars, *vmem, *far, *after, *onward)


def pack_kernel(experts, place, both, hidden, gain, router, gate, send):
    count = gate.shape[0]
    slot = lax.broadcasted_iota(jnp.int32, (count, hidden.shape[0]), 0)
    table = slot == place[...]
    rows = dot(table.astype(jnp.bfloat16), hidden[...])
    normed = normalize(rows, gain[...])
    send[...] = jnp.concatenate(
        [normed[e * PAD : (e + 1) * PAD] for e in experts], axis=0
    ).astype(jnp.bfloat16)
    logits = dot(normed.astype(jnp.bfloat16), router[...])
    mine = lax.broadcasted_iota(jnp.int32, (count, 1), 0) // PAD
    others = jnp.sum(jnp.where(table, both[...], 0), axis=1, keepdims=True) - mine
    expert = lax.broadcasted_iota(jnp.int32, logits.shape, 1)
    lead = jnp.where(expert == mine, logits, 0.0) - jnp.where(expert == others, logits, 0.0)
    gate[...] = 1.0 / (1.0 + jnp.exp(-jnp.sum(lead, axis=1, keepdims=True)))


def gate_kernel():
    pass


def mlp_kernel(rows, w_in, w_out, pieces):
    inner = jnp.maximum(dot(rows[...], w_in[...]), 0.0).astype(jnp.bfloat16)
    pieces[...] = dot(inner, w_out[...]).astype(jnp.bfloat16)


def rows_kernel(experts, gate, parts, rows):
    count = gate.shape[0]
    summed = [None] * (count // PAD)
    for i, e in enumerate(experts):
        part = parts[i * PAD : (i + 1) * PAD].astype(jnp.float32)
        summed[e] = part if summed[e] is None else summed[e] + part
    rows[...] = gate[...] * jnp.concatenate(summed, axis=0)


def mixed_rows(hidden, place, rows_ref):
    rows = rows_ref[...]
    count, size = rows.shape[0], hidden.shape[0]
    high = rows.astype(jnp.bfloat16)
    rest = rows - high.astype(jnp.float32)
    middle = rest.astype(jnp.bfloat16)
    low = (rest - middle.astype(jnp.float32)).astype(jnp.bfloat16)
    slot = lax.broadcasted_iota(jnp.int32, (size, 3 * count), 1) % count
    picks = (slot.astype(jnp.float32) == place[...]).astype(jnp.bfloat16)
    added = dot(picks, jnp.concatenate([high, middle, low], axis=0))
    return hidden[...].astype(jnp.float32) + added


def norm_kernel(group, *refs):
    own, other, (memory, target, mixed) = refs[:4], refs[4:8], refs[8:]

    def run(source, wanted):
        hidden, place, rows, gain = source
        values = mixed_rows(hidden, place, rows)
        memory[...] = normalize(values, gain[...]).astype(jnp.bfloat16)
        hidden, place, rows, gain = wanted
        mixed[...] = mixed_rows(hidden, place, rows)
        target[...] = normalize(mixed[: target.shape[0]], gain[...]).astype(jnp.bfloat16)

    pl.when(group[0] == 0)(lambda: run(own, other))
    pl.when(group[0] != 0)(lambda: run(other, own))


def places(routes, slots):
    return jnp.max(jnp.where(slots >= 0, routes * PAD + slots, -1), axis=1)


def expert_rows(hidden, norm_gain, router, w_in, w_out, routes, slots):
    experts = lax.axis_size("ep") // SPLIT
    count = experts * PAD
    width = hidden.shape[1]
    table = jnp.arange(count)[:, None] == places(routes, slots)[None, :]
    rows = dot(table.astype(jnp.bfloat16), hidden)
    normed = normalize(rows, norm_gain).astype(jnp.bfloat16)
    outgoing = jnp.broadcast_to(normed.reshape(experts, 1, PAD, width), (experts, SPLIT, PAD, width))
    arrived = lax.all_to_all(
        outgoing.reshape(experts * SPLIT, PAD, width), "ep", split_axis=0, concat_axis=0, tiled=True
    ).reshape(-1, width)
    inner = jax.nn.relu(dot(arrived, w_in)).astype(jnp.bfloat16)
    piece = dot(inner, w_out).astype(jnp.bfloat16)
    back = lax.all_to_all(
        piece.reshape(-1, PAD, width), "ep", split_axis=0, concat_axis=0, tiled=True
    )
    summed = jnp.sum(back.reshape(experts, SPLIT, PAD, width).astype(jnp.float32), axis=1)
    logits = dot(normed, router)
    mine = jnp.arange(count) // PAD
    both = jnp.sum(routes, axis=1)
    others = jnp.sum(jnp.where(table, both[None, :], 0), axis=1) - mine
    ids = jnp.arange(router.shape[1])[None, :]
    sign = (ids == mine[:, None]).astype(jnp.float32) - (ids == others[:, None]).astype(jnp.float32)
    gate = jax.nn.sigmoid(jnp.sum(logits * sign, axis=1, keepdims=True))
    return gate * summed.reshape(count, width)


def expert_layer(marks, hidden, norm_gain, router, w_in, w_out, routes, slots):
    devices = lax.axis_size("ep")
    experts = devices // SPLIT
    width = hidden.shape[1]
    place = places(routes, slots)
    held = [device // SPLIT for device in range(devices)]
    blocks = (devices * PAD, width)

    def exchanged(values):
        parts = values.reshape(devices, PAD, width)
        parts = lax.all_to_all(parts, "ep", split_axis=0, concat_axis=0, tiled=True)
        return parts.reshape(values.shape)

    gate, send = local(
        functools.partial(pack_kernel, held),
        "pack",
        [((experts * PAD, 1), jnp.float32), (blocks, jnp.bfloat16)],
        (place[None, :], jnp.sum(routes, axis=1)[None, :], hidden, norm_gain[None, :], router),
    )
    (pieces,) = local(
        mlp_kernel,
        "mlp",
        [(blocks, jnp.bfloat16)],
        (exchanged(send), w_in, w_out),
        marks[0],
    )
    (rows,) = local(
        functools.partial(rows_kernel, held),
        "rows",
        [((experts * PAD, width), jnp.float32)],
        (gate, exchanged(pieces)),
        marks[1],
    )
    return rows


def both_norms(hidden, other_hidden, final_gain, place, rows, targets):
    swap = [(0, 1), (1, 0)]
    place = place[:, None].astype(jnp.float32)
    gain = final_gain[None, :]
    small = jnp.concatenate([gain, jnp.pad(place.T, ((0, 0), (0, gain.shape[1] - place.shape[0])))])
    small = lax.ppermute(small, "grp", swap)
    other_rows = lax.ppermute(rows, "grp", swap)
    own = (hidden, place, rows, gain)
    other = (other_hidden, small[1, : place.shape[0]][:, None], other_rows, small[:1])
    size, width = hidden.shape
    return local(
        norm_kernel,
        "norm",
        [
            ((size, width), jnp.bfloat16),
            ((targets, width), jnp.bfloat16),
            ((size, width), jnp.float32),
        ],
        (*own[:4], *other[:4]),
        order=lax.axis_index("grp")[None],
        mib=12,
    )


EARLY = [
    (0, 0, 0), (1, 0, 0), (2, 0, 0), (3, 0, 0), (0, 0, 1), (1, 0, 1), (0, 1, 0), (1, 1, 0),
    (2, 1, 0), (3, 1, 0), (0, 1, 1), (1, 1, 1), (2, 0, 1),
]
LATE = [(3, 0, 1), (3, 1, 1), (2, 1, 1)]


def gather(part):
    def once(there, *blocks):
        return local(gate_kernel, "gate", [], (), there, blocks)

    z1, x0, y0 = moved(part, dz=1), moved(part, dx=1), moved(part, dy=1)
    z1, y0 = once([x0], z1, y0)
    z2, far0, y1 = moved(z1, dz=1), moved(y0, dx=1), moved(z1, dy=1)
    z1, z2, far0 = once([y1], z1, z2, far0)
    second = [z2]
    z3, x1, y2 = moved(z2, dz=1), moved(z1, dx=1), moved(z2, dy=1)
    z2, z3, far0 = once([x1, y2], z2, z3, far0)
    far1, x2, y3 = moved(far0, dz=1), moved(z2, dx=1), moved(z3, dy=1)
    z3, far0, x2 = once([far1, y3], z3, far0, x2)
    fourth = [x2]
    far3, x3, far2 = moved(far0, dz=-1), moved(z3, dx=1), moved(x2, dy=1)
    early = [part, z1, z2, z3, x0, x1, y0, y1, y2, y3, far0, far1, x2]
    return early, [x3, far3, far2], (second, fourth)


def pairs_of(refs):
    return [tuple(range(low, min(low + 2, len(refs)))) for low in range(0, len(refs), 2)]


def joined(parts, axis):
    return parts[0] if len(parts) == 1 else jnp.concatenate(parts, axis=axis)


def fetched(blocks, columns, near, sems):
    rows = blocks[0].shape[0]
    copies = [
        pltpu.make_async_copy(
            block.at[:, columns], near.at[pl.ds(i * rows, rows)], sems.at[i]
        )
        for i, block in enumerate(blocks)
    ]
    for copy in copies:
        copy.start()
    return copies


def add_blocks(order, memory, target, near, copies, kv, q, fresh):
    rows = near.shape[0] // len(copies)
    half = q.shape[1]

    def columns(ref, members):
        return joined(
            [ref[:, pl.ds(pl.multiple_of(order[i] * rows, 128), rows)] for i in members], 1
        )

    for step, members in enumerate(pairs_of(copies)):
        for i in members:
            copies[i].wait()
        weights = near[members[0] * rows : (members[-1] + 1) * rows]
        kv_part = dot(columns(memory, members), weights[:, : 2 * half])
        q_part = dot(columns(target, members), weights[:, 2 * half :])
        if fresh and step == 0:
            kv[...] = kv_part
            q[...] = q_part
        else:
            kv[...] += kv_part
            q[...] += q_part


def project_kernel(count, order, memory, target, *refs):
    blocks, (kv, q, near, sems) = refs[:count], refs[count:]
    copies = fetched(blocks, pl.ds(0, near.shape[1]), near, sems)
    add_blocks(order, memory, target, near, copies, kv, q, True)


def attend_kernel(early, late, order, seg_q, seg_k, memory, target, kv_sum, q_sum, *refs):
    blocks = refs[: early + late]
    own, sent, kv, q, context, near, near_out, sems, sems_out = refs[early + late :]
    half = q.shape[1]
    rows = blocks[0].shape[0]
    kv[...] = kv_sum[...]
    q[...] = q_sum[...]
    if late:
        copies = fetched(blocks[early:], pl.ds(0, 3 * half), near, sems)
    copies_out = fetched(blocks, pl.ds(3 * half, half), near_out, sems_out)
    if late:
        late_order = [order[early + i] for i in range(late)]
        add_blocks(late_order, memory, target, near, copies, kv, q, False)
    allowed = seg_q[...] == seg_k[...]
    for low in range(0, half, HD):
        query = q[:, low : low + HD].astype(jnp.bfloat16)
        keys = kv[:, low : low + HD].astype(jnp.bfloat16)
        values = kv[:, half + low : half + low + HD].astype(jnp.bfloat16)
        scores = jnp.where(allowed, dot_rows(query, keys) * HD ** (-0.5), -1e30)
        expd = jnp.exp(scores - jnp.max(scores, axis=-1, keepdims=True))
        prob = (expd / jnp.sum(expd, axis=-1, keepdims=True)).astype(jnp.bfloat16)
        context[:, low : low + HD] = dot(prob, values).astype(jnp.bfloat16)
    for copy in copies_out:
        copy.wait()
    for members in pairs_of(blocks):
        part = dot_rows(context[...], near_out[members[0] * rows : (members[-1] + 1) * rows])
        for place, i in enumerate(members):
            columns = pl.ds(pl.multiple_of(order[i] * rows, 128), rows)
            value = part[:, place * rows : (place + 1) * rows]
            own[:, columns] = value
            sent[:, columns] = value.astype(jnp.bfloat16)


def finish_kernel(group, memory, mixed, own, received, valid, out):
    count = own.shape[0]

    @pl.when(group[0] == 0)
    def _():
        out[...] = memory[...]

    @pl.when(group[0] != 0)
    def _():
        total = own[...] + received[...].astype(jnp.float32)
        attended = jnp.where(valid[...] > 0.0, total, 0.0)
        out[:count] = (mixed[:count] + attended).astype(jnp.bfloat16)
        out[count:] = mixed[count:].astype(jnp.bfloat16)


def project(order, memory, target, blocks):
    rows, half = blocks[0].shape[0], blocks[0].shape[1] // 4
    return local(
        functools.partial(project_kernel, len(blocks)),
        "project",
        [((memory.shape[0], 2 * half), jnp.float32), ((target.shape[0], half), jnp.float32)],
        (memory, target),
        order=order,
        far=blocks,
        scratch=[
            pltpu.VMEM((len(blocks) * rows, 3 * half), jnp.bfloat16),
            pltpu.SemaphoreType.DMA((len(blocks),)),
        ],
        mib=52,
    )


def attend(order, seg_q, seg_k, memory, target, sums, early, late):
    rows, half = early[0].shape[0], early[0].shape[1] // 4
    count, width = target.shape
    blocks = len(early) + len(late)
    return local(
        functools.partial(attend_kernel, len(early), len(late)),
        "attend",
        [((count, width), jnp.float32), ((count, width), jnp.bfloat16)],
        (seg_q[:, None], seg_k[None, :], memory, target, *sums),
        order=order,
        far=(*early, *late),
        scratch=[
            pltpu.VMEM((memory.shape[0], 2 * half), jnp.float32),
            pltpu.VMEM((count, half), jnp.float32),
            pltpu.VMEM((count, half), jnp.bfloat16),
            pltpu.VMEM((max(len(late), 1) * rows, 3 * half), jnp.bfloat16),
            pltpu.VMEM((blocks * rows, half), jnp.bfloat16),
            pltpu.SemaphoreType.DMA((max(len(late), 1),)),
            pltpu.SemaphoreType.DMA((blocks,)),
        ],
        mib=14,
    )


def body(
    hidden,
    norm_gain,
    final_gain,
    router,
    w_in,
    w_out,
    expert_ids,
    slot_ids,
    src_len,
    tgt_len,
    wq,
    wk,
    wv,
    wo,
):
    group = lax.axis_index("grp")
    rows_here, width = hidden.shape[1:]
    half = wq.shape[1] // lax.axis_size("grp")
    targets = min(rows_here, -(-TGT_TOTAL // 16) * 16)

    def mine(*weights):
        return jnp.concatenate(
            [lax.dynamic_slice_in_dim(weight, group * half, half, 1) for weight in weights], axis=1
        )

    part = mine(wk, wv, wq, wo)
    other_hidden = lax.ppermute(hidden[0], "grp", [(0, 1), (1, 0)])
    layer = (norm_gain[0], router[0], w_in[0], w_out[0], expert_ids[0], slot_ids[0])
    if chips() is None:
        early, late = [lax.all_gather(part, "ep", axis=0, tiled=True)], []
        order = jnp.zeros((1,), jnp.int32)
        rows = expert_rows(hidden[0], *layer)
    else:
        early, late, marks = gather(part)
        z, y, x = place_of(lax.axis_index("ep"))
        order = jnp.stack([index_of(z - dz, y ^ dy, x ^ dx) for dz, dy, dx in EARLY + LATE])
        rows = expert_layer(marks, hidden[0], *layer)
    memory, target, mixed = both_norms(
        hidden[0], other_hidden, final_gain[0], places(expert_ids[0], slot_ids[0]), rows, targets
    )

    seg_q = positions(tgt_len[0], targets)
    seg_k = positions(src_len[0], rows_here)
    sums = project(order, memory, target, early)
    own, sent = attend(order, seg_q, seg_k, memory, target, sums, early, late)
    received = lax.ppermute(sent, "grp", [(0, 1)])
    (out,) = local(
        finish_kernel,
        "finish",
        [((rows_here, width), jnp.bfloat16)],
        (memory, mixed, own, received, (seg_q < SENT).astype(jnp.float32)[:, None]),
        order=group[None],
        mib=8,
    )
    return out[None]


def solution(mesh):
    in_specs = (
        P("grp", "ep", None),
        P("grp", None),
        P("grp", None),
        P("grp", None, None),
        P("grp", None, "ep"),
        P("grp", "ep", None),
        P("grp", "ep", None),
        P("grp", "ep", None),
        P("ep", None),
        P("ep", None),
        P("ep", None),
        P("ep", None),
        P("ep", None),
        P("ep", None),
    )
    out_specs = P("grp", "ep", None)
    return jax.shard_map(body, mesh=mesh, in_specs=in_specs, out_specs=out_specs, check_vma=False)
```

```python
import functools

import jax
import jax.numpy as jnp
from jax import lax
from jax.experimental import pallas as pl
from jax.experimental.pallas import tpu as pltpu
from jax.sharding import PartitionSpec as P

HD = 128
SPLIT = 8
C = 6
PAD = 8
SENT = 4
TGT_TOTAL = 171
MIB = 1 << 20


def normalize(values, gain):
    mean = jnp.mean(values, -1, keepdims=True)
    centred = values - mean
    spread = jnp.mean(centred * centred, -1, keepdims=True)
    return centred * lax.rsqrt(spread + 1e-05) * gain


def positions(lengths, count):
    upto = jnp.arange(SENT)[:, None] <= jnp.arange(SENT)[None, :]
    ends = jnp.sum(jnp.where(upto, lengths[:, None], 0), axis=0)
    above = (jnp.arange(count, dtype=jnp.int32)[:, None] >= ends[None, :]).astype(jnp.int32)
    return jnp.sum(above, axis=1)


def dot(left, right):
    return jnp.dot(left, right, preferred_element_type=jnp.float32)


def dot_rows(left, right):
    return lax.dot_general(
        left, right, (((1,), (1,)), ((), ())), preferred_element_type=jnp.float32
    )


def chips():
    return (4, 2, 2) if lax.axis_size("ep") == 16 else None


def place_of(index):
    depth, high, wide = chips()
    return index // (high * wide), index // wide % high, index % wide


def index_of(z, y, x):
    depth, high, wide = chips()
    return (z % depth * high + y) * wide + x


def moved(value, dz=0, dy=0, dx=0):
    pairs = []
    for source in range(lax.axis_size("ep")):
        z, y, x = place_of(source)
        pairs.append((source, index_of(z + dz, y ^ dy, x ^ dx)))
    return lax.ppermute(value, "ep", pairs)


def specs(smem, vmem, unread=0):
    return (
        [pl.BlockSpec(memory_space=pltpu.SMEM)] * smem
        + [pl.BlockSpec(memory_space=pltpu.VMEM)] * vmem
        + [pl.BlockSpec(memory_space=pl.ANY)] * unread
    )


def local(kernel, name, outs, vmem, after=(), onward=(), order=None, far=(), scratch=(), mib=6):
    scalars = () if order is None else (order,)
    read = len(scalars) + len(vmem) + len(far)
    unread = len(after) + len(onward)

    def run(*refs):
        results = refs[read + unread :]
        kernel(*refs[:read], *results[: len(outs)], *results[len(outs) + len(onward) :])

    first = read + len(after)
    return pl.pallas_call(
        run,
        out_shape=[jax.ShapeDtypeStruct(shape, dtype) for shape, dtype in outs]
        + [jax.ShapeDtypeStruct(array.shape, array.dtype) for array in onward],
        in_specs=specs(len(scalars), len(vmem), len(far) + unread),
        out_specs=specs(0, len(outs), len(onward)),
        scratch_shapes=list(scratch),
        input_output_aliases={first + i: len(outs) + i for i in range(len(onward))},
        compiler_params=pltpu.CompilerParams(vmem_limit_bytes=mib * MIB),
        name=name,
    )(*scalars, *vmem, *far, *after, *onward)


def pack_kernel(experts, place, both, hidden, gain, router, gate, send):
    count = gate.shape[0]
    slot = lax.broadcasted_iota(jnp.int32, (count, hidden.shape[0]), 0)
    table = slot == place[...]
    rows = dot(table.astype(jnp.bfloat16), hidden[...])
    normed = normalize(rows, gain[...])
    send[...] = jnp.concatenate(
        [normed[e * PAD : (e + 1) * PAD] for e in experts], axis=0
    ).astype(jnp.bfloat16)
    logits = dot(normed.astype(jnp.bfloat16), router[...])
    mine = lax.broadcasted_iota(jnp.int32, (count, 1), 0) // PAD
    others = jnp.sum(jnp.where(table, both[...], 0), axis=1, keepdims=True) - mine
    expert = lax.broadcasted_iota(jnp.int32, logits.shape, 1)
    lead = jnp.where(expert == mine, logits, 0.0) - jnp.where(expert == others, logits, 0.0)
    gate[...] = 1.0 / (1.0 + jnp.exp(-jnp.sum(lead, axis=1, keepdims=True)))


def gate_kernel():
    pass


def mlp_kernel(rows, w_in, w_out, pieces):
    inner = jnp.maximum(dot(rows[...], w_in[...]), 0.0).astype(jnp.bfloat16)
    pieces[...] = dot(inner, w_out[...]).astype(jnp.bfloat16)


def rows_kernel(experts, gate, parts, rows):
    count = gate.shape[0]
    summed = [None] * (count // PAD)
    for i, e in enumerate(experts):
        part = parts[i * PAD : (i + 1) * PAD].astype(jnp.float32)
        summed[e] = part if summed[e] is None else summed[e] + part
    rows[...] = gate[...] * jnp.concatenate(summed, axis=0)


def mixed_rows(hidden, place, rows_ref):
    rows = rows_ref[...]
    count, size = rows.shape[0], hidden.shape[0]
    high = rows.astype(jnp.bfloat16)
    rest = rows - high.astype(jnp.float32)
    middle = rest.astype(jnp.bfloat16)
    low = (rest - middle.astype(jnp.float32)).astype(jnp.bfloat16)
    slot = lax.broadcasted_iota(jnp.int32, (size, 3 * count), 1) % count
    picks = (slot.astype(jnp.float32) == place[...]).astype(jnp.bfloat16)
    added = dot(picks, jnp.concatenate([high, middle, low], axis=0))
    return hidden[...].astype(jnp.float32) + added


def norm_kernel(group, *refs):
    own, other, (memory, target, mixed) = refs[:4], refs[4:8], refs[8:]

    def run(source, wanted):
        hidden, place, rows, gain = source
        values = mixed_rows(hidden, place, rows)
        memory[...] = normalize(values, gain[...]).astype(jnp.bfloat16)
        hidden, place, rows, gain = wanted
        mixed[...] = mixed_rows(hidden, place, rows)
        target[...] = normalize(mixed[: target.shape[0]], gain[...]).astype(jnp.bfloat16)

    pl.when(group[0] == 0)(lambda: run(own, other))
    pl.when(group[0] != 0)(lambda: run(other, own))


def places(routes, slots):
    return jnp.max(jnp.where(slots >= 0, routes * PAD + slots, -1), axis=1)


def expert_rows(hidden, norm_gain, router, w_in, w_out, routes, slots):
    experts = lax.axis_size("ep") // SPLIT
    count = experts * PAD
    width = hidden.shape[1]
    table = jnp.arange(count)[:, None] == places(routes, slots)[None, :]
    rows = dot(table.astype(jnp.bfloat16), hidden)
    normed = normalize(rows, norm_gain).astype(jnp.bfloat16)
    outgoing = jnp.broadcast_to(normed.reshape(experts, 1, PAD, width), (experts, SPLIT, PAD, width))
    arrived = lax.all_to_all(
        outgoing.reshape(experts * SPLIT, PAD, width), "ep", split_axis=0, concat_axis=0, tiled=True
    ).reshape(-1, width)
    inner = jax.nn.relu(dot(arrived, w_in)).astype(jnp.bfloat16)
    piece = dot(inner, w_out).astype(jnp.bfloat16)
    back = lax.all_to_all(
        piece.reshape(-1, PAD, width), "ep", split_axis=0, concat_axis=0, tiled=True
    )
    summed = jnp.sum(back.reshape(experts, SPLIT, PAD, width).astype(jnp.float32), axis=1)
    logits = dot(normed, router)
    mine = jnp.arange(count) // PAD
    both = jnp.sum(routes, axis=1)
    others = jnp.sum(jnp.where(table, both[None, :], 0), axis=1) - mine
    ids = jnp.arange(router.shape[1])[None, :]
    sign = (ids == mine[:, None]).astype(jnp.float32) - (ids == others[:, None]).astype(jnp.float32)
    gate = jax.nn.sigmoid(jnp.sum(logits * sign, axis=1, keepdims=True))
    return gate * summed.reshape(count, width)


def expert_layer(mark, hidden, norm_gain, router, w_in, w_out, routes, slots):
    devices = lax.axis_size("ep")
    experts = devices // SPLIT
    width = hidden.shape[1]
    place = places(routes, slots)
    held = [device // SPLIT for device in range(devices)]
    blocks = (devices * PAD, width)

    def exchanged(values):
        parts = values.reshape(devices, PAD, width)
        parts = lax.all_to_all(parts, "ep", split_axis=0, concat_axis=0, tiled=True)
        return parts.reshape(values.shape)

    gate, send = local(
        functools.partial(pack_kernel, held),
        "pack",
        [((experts * PAD, 1), jnp.float32), (blocks, jnp.bfloat16)],
        (place[None, :], jnp.sum(routes, axis=1)[None, :], hidden, norm_gain[None, :], router),
    )
    (pieces,) = local(
        mlp_kernel,
        "mlp",
        [(blocks, jnp.bfloat16)],
        (exchanged(send), w_in, w_out),
        mark,
    )
    (rows,) = local(
        functools.partial(rows_kernel, held),
        "rows",
        [((experts * PAD, width), jnp.float32)],
        (gate, exchanged(pieces)),
    )
    return rows


def both_norms(hidden, other_hidden, final_gain, place, rows, targets):
    swap = [(0, 1), (1, 0)]
    place = place[:, None].astype(jnp.float32)
    gain = final_gain[None, :]
    small = jnp.concatenate([gain, jnp.pad(place.T, ((0, 0), (0, gain.shape[1] - place.shape[0])))])
    small = lax.ppermute(small, "grp", swap)
    other_rows = lax.ppermute(rows, "grp", swap)
    own = (hidden, place, rows, gain)
    other = (other_hidden, small[1, : place.shape[0]][:, None], other_rows, small[:1])
    size, width = hidden.shape
    return local(
        norm_kernel,
        "norm",
        [
            ((size, width), jnp.bfloat16),
            ((targets, width), jnp.bfloat16),
            ((size, width), jnp.float32),
        ],
        (*own[:4], *other[:4]),
        order=lax.axis_index("grp")[None],
        mib=12,
    )


EARLY = [
    (0, 0, 0), (1, 0, 0), (2, 0, 0), (3, 0, 0), (0, 0, 1), (1, 0, 1), (0, 1, 0), (1, 1, 0),
    (2, 1, 0), (3, 1, 0), (0, 1, 1), (1, 1, 1), (2, 0, 1),
]
LATE = [(3, 0, 1), (3, 1, 1), (2, 1, 1)]


def gather(part):
    def once(there, *blocks):
        return local(gate_kernel, "gate", [], (), there, blocks)

    z1, x0, y0 = moved(part, dz=1), moved(part, dx=1), moved(part, dy=1)
    z1, y0 = once([x0], z1, y0)
    z2, far0, y1 = moved(z1, dz=1), moved(y0, dx=1), moved(z1, dy=1)
    z1, z2, far0 = once([y1], z1, z2, far0)
    second = [z2]
    z3, x1, y2 = moved(z2, dz=1), moved(z1, dx=1), moved(z2, dy=1)
    z2, z3, far0 = once([x1, y2], z2, z3, far0)
    far1, x2, y3 = moved(far0, dz=1), moved(z2, dx=1), moved(z3, dy=1)
    return [part, z1, z2, z3, x0, x1, y0, y1, y2, y3, far0, far1, x2], second


def last_round(early, rows):
    part, z1, z2, z3, x0, x1, y0, y1, y2, y3, far0, far1, x2 = early
    z3, far0, x2 = local(gate_kernel, "gate", [], (), [far1, y3, rows], [z3, far0, x2])
    far3, x3, far2 = moved(far0, dz=-1), moved(z3, dx=1), moved(x2, dy=1)
    return [part, z1, z2, z3, x0, x1, y0, y1, y2, y3, far0, far1, x2], [x3, far3, far2]


def pairs_of(refs):
    return [tuple(range(low, min(low + 2, len(refs)))) for low in range(0, len(refs), 2)]


def joined(parts, axis):
    return parts[0] if len(parts) == 1 else jnp.concatenate(parts, axis=axis)


def fetched(blocks, columns, near, sems):
    rows = blocks[0].shape[0]
    copies = [
        pltpu.make_async_copy(
            block.at[:, columns], near.at[pl.ds(i * rows, rows)], sems.at[i]
        )
        for i, block in enumerate(blocks)
    ]
    for copy in copies:
        copy.start()
    return copies


def add_blocks(order, memory, target, near, copies, kv, q, fresh):
    rows = near.shape[0] // len(copies)
    half = q.shape[1]

    def columns(ref, members):
        return joined(
            [ref[:, pl.ds(pl.multiple_of(order[i] * rows, 128), rows)] for i in members], 1
        )

    for step, members in enumerate(pairs_of(copies)):
        for i in members:
            copies[i].wait()
        weights = near[members[0] * rows : (members[-1] + 1) * rows]
        kv_part = dot(columns(memory, members), weights[:, : 2 * half])
        q_part = dot(columns(target, members), weights[:, 2 * half :])
        if fresh and step == 0:
            kv[...] = kv_part
            q[...] = q_part
        else:
            kv[...] += kv_part
            q[...] += q_part


def project_kernel(count, order, memory, target, *refs):
    blocks, (kv, q, near, sems) = refs[:count], refs[count:]
    copies = fetched(blocks, pl.ds(0, near.shape[1]), near, sems)
    add_blocks(order, memory, target, near, copies, kv, q, True)


def attend_kernel(early, late, order, seg_q, seg_k, memory, target, kv_sum, q_sum, *refs):
    blocks = refs[: early + late]
    own, sent, kv, q, context, near, near_out, sems, sems_out = refs[early + late :]
    half = q.shape[1]
    rows = blocks[0].shape[0]
    kv[...] = kv_sum[...]
    q[...] = q_sum[...]
    if late:
        copies = fetched(blocks[early:], pl.ds(0, 3 * half), near, sems)
    copies_out = fetched(blocks, pl.ds(3 * half, half), near_out, sems_out)
    if late:
        late_order = [order[early + i] for i in range(late)]
        add_blocks(late_order, memory, target, near, copies, kv, q, False)
    allowed = seg_q[...] == seg_k[...]
    for low in range(0, half, HD):
        query = q[:, low : low + HD].astype(jnp.bfloat16)
        keys = kv[:, low : low + HD].astype(jnp.bfloat16)
        values = kv[:, half + low : half + low + HD].astype(jnp.bfloat16)
        scores = jnp.where(allowed, dot_rows(query, keys) * HD ** (-0.5), -1e30)
        expd = jnp.exp(scores - jnp.max(scores, axis=-1, keepdims=True))
        prob = (expd / jnp.sum(expd, axis=-1, keepdims=True)).astype(jnp.bfloat16)
        context[:, low : low + HD] = dot(prob, values).astype(jnp.bfloat16)
    for copy in copies_out:
        copy.wait()
    for members in pairs_of(blocks):
        part = dot_rows(context[...], near_out[members[0] * rows : (members[-1] + 1) * rows])
        for place, i in enumerate(members):
            columns = pl.ds(pl.multiple_of(order[i] * rows, 128), rows)
            value = part[:, place * rows : (place + 1) * rows]
            own[:, columns] = value
            sent[:, columns] = value.astype(jnp.bfloat16)


def finish_kernel(group, memory, mixed, own, received, valid, out):
    count = own.shape[0]

    @pl.when(group[0] == 0)
    def _():
        out[...] = memory[...]

    @pl.when(group[0] != 0)
    def _():
        total = own[...] + received[...].astype(jnp.float32)
        attended = jnp.where(valid[...] > 0.0, total, 0.0)
        out[:count] = (mixed[:count] + attended).astype(jnp.bfloat16)
        out[count:] = mixed[count:].astype(jnp.bfloat16)


def project(order, memory, target, blocks):
    rows, half = blocks[0].shape[0], blocks[0].shape[1] // 4
    return local(
        functools.partial(project_kernel, len(blocks)),
        "project",
        [((memory.shape[0], 2 * half), jnp.float32), ((target.shape[0], half), jnp.float32)],
        (memory, target),
        order=order,
        far=blocks,
        scratch=[
            pltpu.VMEM((len(blocks) * rows, 3 * half), jnp.bfloat16),
            pltpu.SemaphoreType.DMA((len(blocks),)),
        ],
        mib=14,
    )


def attend(order, seg_q, seg_k, memory, target, sums, early, late):
    rows, half = early[0].shape[0], early[0].shape[1] // 4
    count, width = target.shape
    blocks = len(early) + len(late)
    return local(
        functools.partial(attend_kernel, len(early), len(late)),
        "attend",
        [((count, width), jnp.float32), ((count, width), jnp.bfloat16)],
        (seg_q[:, None], seg_k[None, :], memory, target, *sums),
        order=order,
        far=(*early, *late),
        scratch=[
            pltpu.VMEM((memory.shape[0], 2 * half), jnp.float32),
            pltpu.VMEM((count, half), jnp.float32),
            pltpu.VMEM((count, half), jnp.bfloat16),
            pltpu.VMEM((max(len(late), 1) * rows, 3 * half), jnp.bfloat16),
            pltpu.VMEM((blocks * rows, half), jnp.bfloat16),
            pltpu.SemaphoreType.DMA((max(len(late), 1),)),
            pltpu.SemaphoreType.DMA((blocks,)),
        ],
        mib=14,
    )


def body(
    hidden,
    norm_gain,
    final_gain,
    router,
    w_in,
    w_out,
    expert_ids,
    slot_ids,
    src_len,
    tgt_len,
    wq,
    wk,
    wv,
    wo,
):
    group = lax.axis_index("grp")
    rows_here, width = hidden.shape[1:]
    half = wq.shape[1] // lax.axis_size("grp")
    targets = min(rows_here, -(-TGT_TOTAL // 16) * 16)

    def mine(*weights):
        return jnp.concatenate(
            [lax.dynamic_slice_in_dim(weight, group * half, half, 1) for weight in weights], axis=1
        )

    part = mine(wk, wv, wq, wo)
    other_hidden = lax.ppermute(hidden[0], "grp", [(0, 1), (1, 0)])
    layer = (norm_gain[0], router[0], w_in[0], w_out[0], expert_ids[0], slot_ids[0])
    if chips() is None:
        early, late = [lax.all_gather(part, "ep", axis=0, tiled=True)], []
        order = jnp.zeros((1,), jnp.int32)
        rows = expert_rows(hidden[0], *layer)
    else:
        early, mark = gather(part)
        z, y, x = place_of(lax.axis_index("ep"))
        order = jnp.stack([index_of(z - dz, y ^ dy, x ^ dx) for dz, dy, dx in EARLY + LATE])
        rows = expert_layer(mark, hidden[0], *layer)
        early, late = last_round(early, rows)
    memory, target, mixed = both_norms(
        hidden[0], other_hidden, final_gain[0], places(expert_ids[0], slot_ids[0]), rows, targets
    )

    seg_q = positions(tgt_len[0], targets)
    seg_k = positions(src_len[0], rows_here)
    sums = project(order, memory, target, early)
    own, sent = attend(order, seg_q, seg_k, memory, target, sums, early, late)
    received = lax.ppermute(sent, "grp", [(0, 1)])
    (out,) = local(
        finish_kernel,
        "finish",
        [((rows_here, width), jnp.bfloat16)],
        (memory, mixed, own, received, (seg_q < SENT).astype(jnp.float32)[:, None]),
        order=group[None],
        mib=8,
    )
    return out[None]


def solution(mesh):
    in_specs = (
        P("grp", "ep", None),
        P("grp", None),
        P("grp", None),
        P("grp", None, None),
        P("grp", None, "ep"),
        P("grp", "ep", None),
        P("grp", "ep", None),
        P("grp", "ep", None),
        P("ep", None),
        P("ep", None),
        P("ep", None),
        P("ep", None),
        P("ep", None),
        P("ep", None),
    )
    out_specs = P("grp", "ep", None)
    return jax.shard_map(body, mesh=mesh, in_specs=in_specs, out_specs=out_specs, check_vma=False)
```

```python
import functools

import jax
import jax.numpy as jnp
from jax import lax
from jax.experimental import pallas as pl
from jax.experimental.pallas import tpu as pltpu
from jax.sharding import PartitionSpec as P

HD = 128
SPLIT = 8
C = 6
PAD = 8
SENT = 4
TGT_TOTAL = 171
MIB = 1 << 20


def normalize(values, gain):
    mean = jnp.mean(values, -1, keepdims=True)
    centred = values - mean
    spread = jnp.mean(centred * centred, -1, keepdims=True)
    return centred * lax.rsqrt(spread + 1e-05) * gain


def positions(lengths, count):
    upto = jnp.arange(SENT)[:, None] <= jnp.arange(SENT)[None, :]
    ends = jnp.sum(jnp.where(upto, lengths[:, None], 0), axis=0)
    above = (jnp.arange(count, dtype=jnp.int32)[:, None] >= ends[None, :]).astype(jnp.int32)
    return jnp.sum(above, axis=1)


def dot(left, right):
    return jnp.dot(left, right, preferred_element_type=jnp.float32)


def dot_rows(left, right):
    return lax.dot_general(
        left, right, (((1,), (1,)), ((), ())), preferred_element_type=jnp.float32
    )


def chips():
    return (4, 2, 2) if lax.axis_size("ep") == 16 else None


def place_of(index):
    depth, high, wide = chips()
    return index // (high * wide), index // wide % high, index % wide


def index_of(z, y, x):
    depth, high, wide = chips()
    return (z % depth * high + y) * wide + x


def moved(value, dz=0, dy=0, dx=0):
    pairs = []
    for source in range(lax.axis_size("ep")):
        z, y, x = place_of(source)
        pairs.append((source, index_of(z + dz, y ^ dy, x ^ dx)))
    return lax.ppermute(value, "ep", pairs)


def specs(smem, vmem, unread=0):
    return (
        [pl.BlockSpec(memory_space=pltpu.SMEM)] * smem
        + [pl.BlockSpec(memory_space=pltpu.VMEM)] * vmem
        + [pl.BlockSpec(memory_space=pl.ANY)] * unread
    )


def local(kernel, name, outs, vmem, after=(), onward=(), order=None, far=(), scratch=(), mib=6):
    scalars = () if order is None else (order,)
    read = len(scalars) + len(vmem) + len(far)
    unread = len(after) + len(onward)

    def run(*refs):
        results = refs[read + unread :]
        kernel(*refs[:read], *results[: len(outs)], *results[len(outs) + len(onward) :])

    first = read + len(after)
    return pl.pallas_call(
        run,
        out_shape=[jax.ShapeDtypeStruct(shape, dtype) for shape, dtype in outs]
        + [jax.ShapeDtypeStruct(array.shape, array.dtype) for array in onward],
        in_specs=specs(len(scalars), len(vmem), len(far) + unread),
        out_specs=specs(0, len(outs), len(onward)),
        scratch_shapes=list(scratch),
        input_output_aliases={first + i: len(outs) + i for i in range(len(onward))},
        compiler_params=pltpu.CompilerParams(vmem_limit_bytes=mib * MIB),
        name=name,
    )(*scalars, *vmem, *far, *after, *onward)


def pack_kernel(experts, place, both, hidden, gain, router, gate, send):
    count = gate.shape[0]
    slot = lax.broadcasted_iota(jnp.int32, (count, hidden.shape[0]), 0)
    table = slot == place[...]
    rows = dot(table.astype(jnp.bfloat16), hidden[...])
    normed = normalize(rows, gain[...])
    send[...] = jnp.concatenate(
        [normed[e * PAD : (e + 1) * PAD] for e in experts], axis=0
    ).astype(jnp.bfloat16)
    logits = dot(normed.astype(jnp.bfloat16), router[...])
    mine = lax.broadcasted_iota(jnp.int32, (count, 1), 0) // PAD
    others = jnp.sum(jnp.where(table, both[...], 0), axis=1, keepdims=True) - mine
    expert = lax.broadcasted_iota(jnp.int32, logits.shape, 1)
    lead = jnp.where(expert == mine, logits, 0.0) - jnp.where(expert == others, logits, 0.0)
    gate[...] = 1.0 / (1.0 + jnp.exp(-jnp.sum(lead, axis=1, keepdims=True)))


def gate_kernel():
    pass


def mlp_kernel(held, rows, w_in, w_out, pieces):
    inner = jnp.maximum(dot(rows[...], w_in[...]), 0.0).astype(jnp.bfloat16)
    piece = dot(inner, w_out[...])
    middle = piece.shape[0] // 2
    first = held[0] == 0
    near = jnp.where(first, piece[:middle], piece[middle:])
    far = jnp.where(first, piece[middle:], piece[:middle])
    for low in range(0, middle, PAD):
        both = jnp.concatenate([near[low : low + PAD], far[low : low + PAD]], axis=0)
        pieces[2 * low : 2 * low + 2 * PAD] = both.astype(jnp.bfloat16)


def sum_kernel(pieces, own, other):
    total = pieces[: 2 * PAD].astype(jnp.float32)
    for low in range(2 * PAD, pieces.shape[0], 2 * PAD):
        total = total + pieces[low : low + 2 * PAD].astype(jnp.float32)
    own[...] = total[:PAD]
    other[...] = total[PAD:]


def rows_kernel(held, gate, own, arrived, rows):
    first = held[0] == 0
    near = jnp.where(first, own[...], arrived[...])
    far = jnp.where(first, arrived[...], own[...])
    rows[...] = gate[...] * jnp.concatenate([near, far], axis=0)


def mixed_rows(hidden, place, rows_ref):
    rows = rows_ref[...]
    count, size = rows.shape[0], hidden.shape[0]
    high = rows.astype(jnp.bfloat16)
    rest = rows - high.astype(jnp.float32)
    middle = rest.astype(jnp.bfloat16)
    low = (rest - middle.astype(jnp.float32)).astype(jnp.bfloat16)
    slot = lax.broadcasted_iota(jnp.int32, (size, 3 * count), 1) % count
    picks = (slot.astype(jnp.float32) == place[...]).astype(jnp.bfloat16)
    added = dot(picks, jnp.concatenate([high, middle, low], axis=0))
    return hidden[...].astype(jnp.float32) + added


def norm_kernel(group, *refs):
    own, other, (memory, target, mixed) = refs[:4], refs[4:8], refs[8:]

    def run(source, wanted):
        hidden, place, rows, gain = source
        values = mixed_rows(hidden, place, rows)
        memory[...] = normalize(values, gain[...]).astype(jnp.bfloat16)
        hidden, place, rows, gain = wanted
        mixed[...] = mixed_rows(hidden, place, rows)
        target[...] = normalize(mixed[: target.shape[0]], gain[...]).astype(jnp.bfloat16)

    pl.when(group[0] == 0)(lambda: run(own, other))
    pl.when(group[0] != 0)(lambda: run(other, own))


def places(routes, slots):
    return jnp.max(jnp.where(slots >= 0, routes * PAD + slots, -1), axis=1)


def expert_rows(hidden, norm_gain, router, w_in, w_out, routes, slots):
    experts = lax.axis_size("ep") // SPLIT
    count = experts * PAD
    width = hidden.shape[1]
    table = jnp.arange(count)[:, None] == places(routes, slots)[None, :]
    rows = dot(table.astype(jnp.bfloat16), hidden)
    normed = normalize(rows, norm_gain).astype(jnp.bfloat16)
    outgoing = jnp.broadcast_to(normed.reshape(experts, 1, PAD, width), (experts, SPLIT, PAD, width))
    arrived = lax.all_to_all(
        outgoing.reshape(experts * SPLIT, PAD, width), "ep", split_axis=0, concat_axis=0, tiled=True
    ).reshape(-1, width)
    inner = jax.nn.relu(dot(arrived, w_in)).astype(jnp.bfloat16)
    piece = dot(inner, w_out).astype(jnp.bfloat16)
    back = lax.all_to_all(
        piece.reshape(-1, PAD, width), "ep", split_axis=0, concat_axis=0, tiled=True
    )
    summed = jnp.sum(back.reshape(experts, SPLIT, PAD, width).astype(jnp.float32), axis=1)
    logits = dot(normed, router)
    mine = jnp.arange(count) // PAD
    both = jnp.sum(routes, axis=1)
    others = jnp.sum(jnp.where(table, both[None, :], 0), axis=1) - mine
    ids = jnp.arange(router.shape[1])[None, :]
    sign = (ids == mine[:, None]).astype(jnp.float32) - (ids == others[:, None]).astype(jnp.float32)
    gate = jax.nn.sigmoid(jnp.sum(logits * sign, axis=1, keepdims=True))
    return gate * summed.reshape(count, width)


def expert_layer(mark, hidden, norm_gain, router, w_in, w_out, routes, slots):
    devices = lax.axis_size("ep")
    experts = devices // SPLIT
    width = hidden.shape[1]
    place = places(routes, slots)
    held = [device // SPLIT for device in range(devices)]
    blocks = (devices * PAD, width)

    depth = chips()[0]
    half = (place_of(lax.axis_index("ep"))[0] // (depth // 2))[None]
    halves = [list(range(low, low + SPLIT)) for low in range(0, devices, SPLIT)]

    def exchanged(values, groups=None):
        parts = values.reshape(len(groups[0]) if groups else devices, -1, width)
        parts = lax.all_to_all(
            parts, "ep", split_axis=0, concat_axis=0, tiled=True, axis_index_groups=groups
        )
        return parts.reshape(values.shape)

    gate, send = local(
        functools.partial(pack_kernel, held),
        "pack",
        [((experts * PAD, 1), jnp.float32), (blocks, jnp.bfloat16)],
        (place[None, :], jnp.sum(routes, axis=1)[None, :], hidden, norm_gain[None, :], router),
    )
    (pieces,) = local(
        mlp_kernel,
        "mlp",
        [(blocks, jnp.bfloat16)],
        (exchanged(send), w_in, w_out),
        mark,
        order=half,
    )
    own, other = local(
        sum_kernel, "sum", [((PAD, width), jnp.float32)] * 2, (exchanged(pieces, halves),)
    )
    (rows,) = local(
        rows_kernel,
        "rows",
        [((2 * PAD, width), jnp.float32)],
        (gate, own, moved(other, dz=depth // 2)),
        order=half,
    )
    return rows


def both_norms(hidden, other_hidden, final_gain, place, rows, targets):
    swap = [(0, 1), (1, 0)]
    place = place[:, None].astype(jnp.float32)
    gain = final_gain[None, :]
    small = jnp.concatenate([gain, jnp.pad(place.T, ((0, 0), (0, gain.shape[1] - place.shape[0])))])
    small = lax.ppermute(small, "grp", swap)
    other_rows = lax.ppermute(rows, "grp", swap)
    own = (hidden, place, rows, gain)
    other = (other_hidden, small[1, : place.shape[0]][:, None], other_rows, small[:1])
    size, width = hidden.shape
    return local(
        norm_kernel,
        "norm",
        [
            ((size, width), jnp.bfloat16),
            ((targets, width), jnp.bfloat16),
            ((size, width), jnp.float32),
        ],
        (*own[:4], *other[:4]),
        order=lax.axis_index("grp")[None],
        mib=12,
    )


EARLY = [
    (0, 0, 0), (1, 0, 0), (2, 0, 0), (3, 0, 0), (0, 0, 1), (1, 0, 1), (0, 1, 0), (1, 1, 0),
    (2, 1, 0), (3, 1, 0), (0, 1, 1), (1, 1, 1), (2, 0, 1),
]
LATE = [(3, 0, 1), (3, 1, 1), (2, 1, 1)]


def gather(part):
    def once(there, *blocks):
        return local(gate_kernel, "gate", [], (), there, blocks)

    z1, x0, y0 = moved(part, dz=1), moved(part, dx=1), moved(part, dy=1)
    z1, y0 = once([x0], z1, y0)
    z2, far0, y1 = moved(z1, dz=1), moved(y0, dx=1), moved(z1, dy=1)
    z1, z2, far0 = once([y1], z1, z2, far0)
    second = [z2]
    z3, x1, y2 = moved(z2, dz=1), moved(z1, dx=1), moved(z2, dy=1)
    z2, z3, far0 = once([x1, y2], z2, z3, far0)
    far1, x2, y3 = moved(far0, dz=1), moved(z2, dx=1), moved(z3, dy=1)
    return [part, z1, z2, z3, x0, x1, y0, y1, y2, y3, far0, far1, x2], second


def last_round(early, rows):
    part, z1, z2, z3, x0, x1, y0, y1, y2, y3, far0, far1, x2 = early
    z3, far0, x2 = local(gate_kernel, "gate", [], (), [far1, y3, rows], [z3, far0, x2])
    far3, x3, far2 = moved(far0, dz=-1), moved(z3, dx=1), moved(x2, dy=1)
    return [part, z1, z2, z3, x0, x1, y0, y1, y2, y3, far0, far1, x2], [x3, far3, far2]


def pairs_of(refs):
    return [tuple(range(low, min(low + 2, len(refs)))) for low in range(0, len(refs), 2)]


def joined(parts, axis):
    return parts[0] if len(parts) == 1 else jnp.concatenate(parts, axis=axis)


def fetched(blocks, columns, near, sems):
    rows = blocks[0].shape[0]
    copies = [
        pltpu.make_async_copy(
            block.at[:, columns], near.at[pl.ds(i * rows, rows)], sems.at[i]
        )
        for i, block in enumerate(blocks)
    ]
    for copy in copies:
        copy.start()
    return copies


def add_blocks(order, memory, target, near, copies, kv, q, fresh):
    rows = near.shape[0] // len(copies)
    half = q.shape[1]

    def columns(ref, members):
        return joined(
            [ref[:, pl.ds(pl.multiple_of(order[i] * rows, 128), rows)] for i in members], 1
        )

    for step, members in enumerate(pairs_of(copies)):
        for i in members:
            copies[i].wait()
        weights = near[members[0] * rows : (members[-1] + 1) * rows]
        kv_part = dot(columns(memory, members), weights[:, : 2 * half])
        q_part = dot(columns(target, members), weights[:, 2 * half :])
        if fresh and step == 0:
            kv[...] = kv_part
            q[...] = q_part
        else:
            kv[...] += kv_part
            q[...] += q_part


def project_kernel(count, order, memory, target, *refs):
    blocks, (kv, q, near, sems) = refs[:count], refs[count:]
    copies = fetched(blocks, pl.ds(0, near.shape[1]), near, sems)
    add_blocks(order, memory, target, near, copies, kv, q, True)


def attend_kernel(early, late, order, seg_q, seg_k, memory, target, kv_sum, q_sum, *refs):
    blocks = refs[: early + late]
    own, sent, kv, q, context, near, near_out, sems, sems_out = refs[early + late :]
    half = q.shape[1]
    rows = blocks[0].shape[0]
    kv[...] = kv_sum[...]
    q[...] = q_sum[...]
    if late:
        copies = fetched(blocks[early:], pl.ds(0, 3 * half), near, sems)
    copies_out = fetched(blocks, pl.ds(3 * half, half), near_out, sems_out)
    if late:
        late_order = [order[early + i] for i in range(late)]
        add_blocks(late_order, memory, target, near, copies, kv, q, False)
    allowed = seg_q[...] == seg_k[...]
    for low in range(0, half, HD):
        query = q[:, low : low + HD].astype(jnp.bfloat16)
        keys = kv[:, low : low + HD].astype(jnp.bfloat16)
        values = kv[:, half + low : half + low + HD].astype(jnp.bfloat16)
        scores = jnp.where(allowed, dot_rows(query, keys) * HD ** (-0.5), -1e30)
        expd = jnp.exp(scores - jnp.max(scores, axis=-1, keepdims=True))
        prob = (expd / jnp.sum(expd, axis=-1, keepdims=True)).astype(jnp.bfloat16)
        context[:, low : low + HD] = dot(prob, values).astype(jnp.bfloat16)
    for copy in copies_out:
        copy.wait()
    for members in pairs_of(blocks):
        part = dot_rows(context[...], near_out[members[0] * rows : (members[-1] + 1) * rows])
        for place, i in enumerate(members):
            columns = pl.ds(pl.multiple_of(order[i] * rows, 128), rows)
            value = part[:, place * rows : (place + 1) * rows]
            own[:, columns] = value
            sent[:, columns] = value.astype(jnp.bfloat16)


def finish_kernel(group, memory, mixed, own, received, valid, out):
    count = own.shape[0]

    @pl.when(group[0] == 0)
    def _():
        out[...] = memory[...]

    @pl.when(group[0] != 0)
    def _():
        total = own[...] + received[...].astype(jnp.float32)
        attended = jnp.where(valid[...] > 0.0, total, 0.0)
        out[:count] = (mixed[:count] + attended).astype(jnp.bfloat16)
        out[count:] = mixed[count:].astype(jnp.bfloat16)


def project(order, memory, target, blocks):
    rows, half = blocks[0].shape[0], blocks[0].shape[1] // 4
    return local(
        functools.partial(project_kernel, len(blocks)),
        "project",
        [((memory.shape[0], 2 * half), jnp.float32), ((target.shape[0], half), jnp.float32)],
        (memory, target),
        order=order,
        far=blocks,
        scratch=[
            pltpu.VMEM((len(blocks) * rows, 3 * half), jnp.bfloat16),
            pltpu.SemaphoreType.DMA((len(blocks),)),
        ],
        mib=14,
    )


def attend(order, seg_q, seg_k, memory, target, sums, early, late):
    rows, half = early[0].shape[0], early[0].shape[1] // 4
    count, width = target.shape
    blocks = len(early) + len(late)
    return local(
        functools.partial(attend_kernel, len(early), len(late)),
        "attend",
        [((count, width), jnp.float32), ((count, width), jnp.bfloat16)],
        (seg_q[:, None], seg_k[None, :], memory, target, *sums),
        order=order,
        far=(*early, *late),
        scratch=[
            pltpu.VMEM((memory.shape[0], 2 * half), jnp.float32),
            pltpu.VMEM((count, half), jnp.float32),
            pltpu.VMEM((count, half), jnp.bfloat16),
            pltpu.VMEM((max(len(late), 1) * rows, 3 * half), jnp.bfloat16),
            pltpu.VMEM((blocks * rows, half), jnp.bfloat16),
            pltpu.SemaphoreType.DMA((max(len(late), 1),)),
            pltpu.SemaphoreType.DMA((blocks,)),
        ],
        mib=14,
    )


def body(
    hidden,
    norm_gain,
    final_gain,
    router,
    w_in,
    w_out,
    expert_ids,
    slot_ids,
    src_len,
    tgt_len,
    wq,
    wk,
    wv,
    wo,
):
    group = lax.axis_index("grp")
    rows_here, width = hidden.shape[1:]
    half = wq.shape[1] // lax.axis_size("grp")
    targets = min(rows_here, -(-TGT_TOTAL // 16) * 16)

    def mine(*weights):
        return jnp.concatenate(
            [lax.dynamic_slice_in_dim(weight, group * half, half, 1) for weight in weights], axis=1
        )

    part = mine(wk, wv, wq, wo)
    other_hidden = lax.ppermute(hidden[0], "grp", [(0, 1), (1, 0)])
    layer = (norm_gain[0], router[0], w_in[0], w_out[0], expert_ids[0], slot_ids[0])
    if chips() is None:
        early, late = [lax.all_gather(part, "ep", axis=0, tiled=True)], []
        order = jnp.zeros((1,), jnp.int32)
        rows = expert_rows(hidden[0], *layer)
    else:
        early, mark = gather(part)
        z, y, x = place_of(lax.axis_index("ep"))
        order = jnp.stack([index_of(z - dz, y ^ dy, x ^ dx) for dz, dy, dx in EARLY + LATE])
        rows = expert_layer(mark, hidden[0], *layer)
        early, late = last_round(early, rows)
    memory, target, mixed = both_norms(
        hidden[0], other_hidden, final_gain[0], places(expert_ids[0], slot_ids[0]), rows, targets
    )

    seg_q = positions(tgt_len[0], targets)
    seg_k = positions(src_len[0], rows_here)
    sums = project(order, memory, target, early)
    own, sent = attend(order, seg_q, seg_k, memory, target, sums, early, late)
    received = lax.ppermute(sent, "grp", [(0, 1)])
    (out,) = local(
        finish_kernel,
        "finish",
        [((rows_here, width), jnp.bfloat16)],
        (memory, mixed, own, received, (seg_q < SENT).astype(jnp.float32)[:, None]),
        order=group[None],
        mib=8,
    )
    return out[None]


def solution(mesh):
    in_specs = (
        P("grp", "ep", None),
        P("grp", None),
        P("grp", None),
        P("grp", None, None),
        P("grp", None, "ep"),
        P("grp", "ep", None),
        P("grp", "ep", None),
        P("grp", "ep", None),
        P("ep", None),
        P("ep", None),
        P("ep", None),
        P("ep", None),
        P("ep", None),
        P("ep", None),
    )
    out_specs = P("grp", "ep", None)
    return jax.shard_map(body, mesh=mesh, in_specs=in_specs, out_specs=out_specs, check_vma=False)
```

```python
import functools

import jax
import jax.numpy as jnp
from jax import lax
from jax.experimental import pallas as pl
from jax.experimental.pallas import tpu as pltpu
from jax.sharding import PartitionSpec as P

HD = 128
SPLIT = 8
C = 6
PAD = 8
SENT = 4
TGT_TOTAL = 171
MIB = 1 << 20


def normalize(values, gain):
    mean = jnp.mean(values, -1, keepdims=True)
    centred = values - mean
    spread = jnp.mean(centred * centred, -1, keepdims=True)
    return centred * lax.rsqrt(spread + 1e-05) * gain


def positions(lengths, count):
    upto = jnp.arange(SENT)[:, None] <= jnp.arange(SENT)[None, :]
    ends = jnp.sum(jnp.where(upto, lengths[:, None], 0), axis=0)
    above = (jnp.arange(count, dtype=jnp.int32)[:, None] >= ends[None, :]).astype(jnp.int32)
    return jnp.sum(above, axis=1)


def dot(left, right):
    return jnp.dot(left, right, preferred_element_type=jnp.float32)


def dot_rows(left, right):
    return lax.dot_general(
        left, right, (((1,), (1,)), ((), ())), preferred_element_type=jnp.float32
    )


def chips():
    return (4, 2, 2) if lax.axis_size("ep") == 16 else None


def place_of(index):
    depth, high, wide = chips()
    return index // (high * wide), index // wide % high, index % wide


def index_of(z, y, x):
    depth, high, wide = chips()
    return (z % depth * high + y) * wide + x


def moved(value, dz=0, dy=0, dx=0):
    pairs = []
    for source in range(lax.axis_size("ep")):
        z, y, x = place_of(source)
        pairs.append((source, index_of(z + dz, y ^ dy, x ^ dx)))
    return lax.ppermute(value, "ep", pairs)


def specs(smem, vmem, unread=0):
    return (
        [pl.BlockSpec(memory_space=pltpu.SMEM)] * smem
        + [pl.BlockSpec(memory_space=pltpu.VMEM)] * vmem
        + [pl.BlockSpec(memory_space=pl.ANY)] * unread
    )


def local(kernel, name, outs, vmem, after=(), onward=(), order=None, far=(), scratch=(), mib=6):
    scalars = () if order is None else (order,)
    read = len(scalars) + len(vmem) + len(far)
    unread = len(after) + len(onward)

    def run(*refs):
        results = refs[read + unread :]
        kernel(*refs[:read], *results[: len(outs)], *results[len(outs) + len(onward) :])

    first = read + len(after)
    return pl.pallas_call(
        run,
        out_shape=[jax.ShapeDtypeStruct(shape, dtype) for shape, dtype in outs]
        + [jax.ShapeDtypeStruct(array.shape, array.dtype) for array in onward],
        in_specs=specs(len(scalars), len(vmem), len(far) + unread),
        out_specs=specs(0, len(outs), len(onward)),
        scratch_shapes=list(scratch),
        input_output_aliases={first + i: len(outs) + i for i in range(len(onward))},
        compiler_params=pltpu.CompilerParams(vmem_limit_bytes=mib * MIB),
        name=name,
    )(*scalars, *vmem, *far, *after, *onward)


def pack_kernel(experts, place, both, hidden, gain, router, gate, send):
    count = gate.shape[0]
    slot = lax.broadcasted_iota(jnp.int32, (count, hidden.shape[0]), 0)
    table = slot == place[...]
    rows = dot(table.astype(jnp.bfloat16), hidden[...])
    normed = normalize(rows, gain[...])
    send[...] = jnp.concatenate(
        [normed[e * PAD : (e + 1) * PAD] for e in experts], axis=0
    ).astype(jnp.bfloat16)
    logits = dot(normed.astype(jnp.bfloat16), router[...])
    mine = lax.broadcasted_iota(jnp.int32, (count, 1), 0) // PAD
    others = jnp.sum(jnp.where(table, both[...], 0), axis=1, keepdims=True) - mine
    expert = lax.broadcasted_iota(jnp.int32, logits.shape, 1)
    lead = jnp.where(expert == mine, logits, 0.0) - jnp.where(expert == others, logits, 0.0)
    gate[...] = 1.0 / (1.0 + jnp.exp(-jnp.sum(lead, axis=1, keepdims=True)))


def gate_kernel():
    pass


def mlp_kernel(held, rows, w_in, w_out, pieces):
    inner = jnp.maximum(dot(rows[...], w_in[...]), 0.0).astype(jnp.bfloat16)
    piece = dot(inner, w_out[...])
    middle = piece.shape[0] // 2
    first = held[0] == 0
    near = jnp.where(first, piece[:middle], piece[middle:])
    far = jnp.where(first, piece[middle:], piece[:middle])
    for low in range(0, middle, PAD):
        both = jnp.concatenate([near[low : low + PAD], far[low : low + PAD]], axis=0)
        pieces[2 * low : 2 * low + 2 * PAD] = both.astype(jnp.bfloat16)


def sum_kernel(pieces, own, other):
    total = pieces[: 2 * PAD].astype(jnp.float32)
    for low in range(2 * PAD, pieces.shape[0], 2 * PAD):
        total = total + pieces[low : low + 2 * PAD].astype(jnp.float32)
    own[...] = total[:PAD]
    other[...] = total[PAD:]


def rows_kernel(held, gate, own, arrived, rows):
    first = held[0] == 0
    near = jnp.where(first, own[...], arrived[...])
    far = jnp.where(first, arrived[...], own[...])
    rows[...] = gate[...] * jnp.concatenate([near, far], axis=0)


def mixed_rows(hidden, place, rows_ref):
    rows = rows_ref[...]
    count, size = rows.shape[0], hidden.shape[0]
    high = rows.astype(jnp.bfloat16)
    rest = rows - high.astype(jnp.float32)
    middle = rest.astype(jnp.bfloat16)
    low = (rest - middle.astype(jnp.float32)).astype(jnp.bfloat16)
    slot = lax.broadcasted_iota(jnp.int32, (size, 3 * count), 1) % count
    picks = (slot.astype(jnp.float32) == place[...]).astype(jnp.bfloat16)
    added = dot(picks, jnp.concatenate([high, middle, low], axis=0))
    return hidden[...].astype(jnp.float32) + added


def norm_kernel(group, *refs):
    own, other, (memory, target, mixed) = refs[:4], refs[4:8], refs[8:]

    def run(source, wanted):
        hidden, place, rows, gain = source
        values = mixed_rows(hidden, place, rows)
        memory[...] = normalize(values, gain[...]).astype(jnp.bfloat16)
        hidden, place, rows, gain = wanted
        mixed[...] = mixed_rows(hidden, place, rows)
        target[...] = normalize(mixed[: target.shape[0]], gain[...]).astype(jnp.bfloat16)

    pl.when(group[0] == 0)(lambda: run(own, other))
    pl.when(group[0] != 0)(lambda: run(other, own))


def places(routes, slots):
    return jnp.max(jnp.where(slots >= 0, routes * PAD + slots, -1), axis=1)


def expert_rows(hidden, norm_gain, router, w_in, w_out, routes, slots):
    experts = lax.axis_size("ep") // SPLIT
    count = experts * PAD
    width = hidden.shape[1]
    table = jnp.arange(count)[:, None] == places(routes, slots)[None, :]
    rows = dot(table.astype(jnp.bfloat16), hidden)
    normed = normalize(rows, norm_gain).astype(jnp.bfloat16)
    outgoing = jnp.broadcast_to(normed.reshape(experts, 1, PAD, width), (experts, SPLIT, PAD, width))
    arrived = lax.all_to_all(
        outgoing.reshape(experts * SPLIT, PAD, width), "ep", split_axis=0, concat_axis=0, tiled=True
    ).reshape(-1, width)
    inner = jax.nn.relu(dot(arrived, w_in)).astype(jnp.bfloat16)
    piece = dot(inner, w_out).astype(jnp.bfloat16)
    back = lax.all_to_all(
        piece.reshape(-1, PAD, width), "ep", split_axis=0, concat_axis=0, tiled=True
    )
    summed = jnp.sum(back.reshape(experts, SPLIT, PAD, width).astype(jnp.float32), axis=1)
    logits = dot(normed, router)
    mine = jnp.arange(count) // PAD
    both = jnp.sum(routes, axis=1)
    others = jnp.sum(jnp.where(table, both[None, :], 0), axis=1) - mine
    ids = jnp.arange(router.shape[1])[None, :]
    sign = (ids == mine[:, None]).astype(jnp.float32) - (ids == others[:, None]).astype(jnp.float32)
    gate = jax.nn.sigmoid(jnp.sum(logits * sign, axis=1, keepdims=True))
    return gate * summed.reshape(count, width)


def expert_layer(mark, hidden, norm_gain, router, w_in, w_out, routes, slots):
    devices = lax.axis_size("ep")
    experts = devices // SPLIT
    width = hidden.shape[1]
    place = places(routes, slots)
    held = [device // SPLIT for device in range(devices)]
    blocks = (devices * PAD, width)

    depth = chips()[0]
    half = (place_of(lax.axis_index("ep"))[0] // (depth // 2))[None]
    halves = [list(range(low, low + SPLIT)) for low in range(0, devices, SPLIT)]

    def exchanged(values, groups=None):
        parts = values.reshape(len(groups[0]) if groups else devices, -1, width)
        parts = lax.all_to_all(
            parts, "ep", split_axis=0, concat_axis=0, tiled=True, axis_index_groups=groups
        )
        return parts.reshape(values.shape)

    gate, send = local(
        functools.partial(pack_kernel, held),
        "pack",
        [((experts * PAD, 1), jnp.float32), (blocks, jnp.bfloat16)],
        (place[None, :], jnp.sum(routes, axis=1)[None, :], hidden, norm_gain[None, :], router),
    )
    (pieces,) = local(
        mlp_kernel,
        "mlp",
        [(blocks, jnp.bfloat16)],
        (exchanged(send), w_in, w_out),
        mark,
        order=half,
    )
    own, other = local(
        sum_kernel, "sum", [((PAD, width), jnp.float32)] * 2, (exchanged(pieces, halves),)
    )
    (rows,) = local(
        rows_kernel,
        "rows",
        [((2 * PAD, width), jnp.float32)],
        (gate, own, moved(other, dz=depth // 2)),
        order=half,
    )
    return rows


def both_norms(hidden, other_hidden, final_gain, place, rows, targets):
    swap = [(0, 1), (1, 0)]
    place = place[:, None].astype(jnp.float32)
    gain = final_gain[None, :]
    small = jnp.concatenate([gain, jnp.pad(place.T, ((0, 0), (0, gain.shape[1] - place.shape[0])))])
    small = lax.ppermute(small, "grp", swap)
    other_rows = lax.ppermute(rows, "grp", swap)
    own = (hidden, place, rows, gain)
    other = (other_hidden, small[1, : place.shape[0]][:, None], other_rows, small[:1])
    size, width = hidden.shape
    return local(
        norm_kernel,
        "norm",
        [
            ((size, width), jnp.bfloat16),
            ((targets, width), jnp.bfloat16),
            ((size, width), jnp.float32),
        ],
        (*own[:4], *other[:4]),
        order=lax.axis_index("grp")[None],
        mib=12,
    )


EARLY = [
    (0, 0, 0), (1, 0, 0), (2, 0, 0), (3, 0, 0), (0, 0, 1), (1, 0, 1), (0, 1, 0), (1, 1, 0),
    (2, 1, 0), (3, 1, 0), (0, 1, 1), (1, 1, 1), (2, 0, 1),
]
LATE = [(3, 0, 1), (3, 1, 1), (2, 1, 1)]


def gather(part):
    def once(there, *blocks):
        return local(gate_kernel, "gate", [], (), there, blocks)

    z1, x0, y0 = moved(part, dz=1), moved(part, dx=1), moved(part, dy=1)
    (y0,) = once([x0, z1], y0)
    z2, y1, far0 = moved(z1, dz=1), moved(z1, dy=1), moved(y0, dx=1)
    z1, far0 = once([y1, z2], z1, far0)
    second = [z1]
    z3, y2, x1 = moved(z2, dz=1), moved(z2, dy=1), moved(z1, dx=1)
    z2, far0 = once([x1, y2, z3], z2, far0)
    y3, x2, far1 = moved(z3, dy=1), moved(z2, dx=1), moved(far0, dz=1)
    return [part, z1, z2, z3, x0, x1, y0, y1, y2, y3, far0, far1, x2], second


def last_round(early, rows):
    part, z1, z2, z3, x0, x1, y0, y1, y2, y3, far0, far1, x2 = early
    z3, far0, x2 = local(gate_kernel, "gate", [], (), [far1, y3, rows], [z3, far0, x2])
    far3, x3, far2 = moved(far0, dz=-1), moved(z3, dx=1), moved(x2, dy=1)
    return [part, z1, z2, z3, x0, x1, y0, y1, y2, y3, far0, far1, x2], [x3, far3, far2]


def pairs_of(refs):
    return [tuple(range(low, min(low + 2, len(refs)))) for low in range(0, len(refs), 2)]


def joined(parts, axis):
    return parts[0] if len(parts) == 1 else jnp.concatenate(parts, axis=axis)


def fetched(blocks, columns, near, sems):
    rows = blocks[0].shape[0]
    copies = [
        pltpu.make_async_copy(
            block.at[:, columns], near.at[pl.ds(i * rows, rows)], sems.at[i]
        )
        for i, block in enumerate(blocks)
    ]
    for copy in copies:
        copy.start()
    return copies


def add_blocks(order, memory, target, near, copies, kv, q, fresh):
    rows = near.shape[0] // len(copies)
    half = q.shape[1]

    def columns(ref, members):
        return joined(
            [ref[:, pl.ds(pl.multiple_of(order[i] * rows, 128), rows)] for i in members], 1
        )

    for step, members in enumerate(pairs_of(copies)):
        for i in members:
            copies[i].wait()
        weights = near[members[0] * rows : (members[-1] + 1) * rows]
        kv_part = dot(columns(memory, members), weights[:, : 2 * half])
        q_part = dot(columns(target, members), weights[:, 2 * half :])
        if fresh and step == 0:
            kv[...] = kv_part
            q[...] = q_part
        else:
            kv[...] += kv_part
            q[...] += q_part


def project_kernel(count, order, memory, target, *refs):
    blocks, (kv, q, near, sems) = refs[:count], refs[count:]
    copies = fetched(blocks, pl.ds(0, near.shape[1]), near, sems)
    add_blocks(order, memory, target, near, copies, kv, q, True)


def attend_kernel(early, late, order, seg_q, seg_k, memory, target, kv_sum, q_sum, *refs):
    blocks = refs[: early + late]
    own, sent, kv, q, context, near, near_out, sems, sems_out = refs[early + late :]
    half = q.shape[1]
    rows = blocks[0].shape[0]
    kv[...] = kv_sum[...]
    q[...] = q_sum[...]
    if late:
        copies = fetched(blocks[early:], pl.ds(0, 3 * half), near, sems)
    copies_out = fetched(blocks, pl.ds(3 * half, half), near_out, sems_out)
    if late:
        late_order = [order[early + i] for i in range(late)]
        add_blocks(late_order, memory, target, near, copies, kv, q, False)
    allowed = seg_q[...] == seg_k[...]
    for low in range(0, half, HD):
        query = q[:, low : low + HD].astype(jnp.bfloat16)
        keys = kv[:, low : low + HD].astype(jnp.bfloat16)
        values = kv[:, half + low : half + low + HD].astype(jnp.bfloat16)
        scores = jnp.where(allowed, dot_rows(query, keys) * HD ** (-0.5), -1e30)
        expd = jnp.exp(scores - jnp.max(scores, axis=-1, keepdims=True))
        prob = (expd / jnp.sum(expd, axis=-1, keepdims=True)).astype(jnp.bfloat16)
        context[:, low : low + HD] = dot(prob, values).astype(jnp.bfloat16)
    for copy in copies_out:
        copy.wait()
    for members in pairs_of(blocks):
        part = dot_rows(context[...], near_out[members[0] * rows : (members[-1] + 1) * rows])
        for place, i in enumerate(members):
            columns = pl.ds(pl.multiple_of(order[i] * rows, 128), rows)
            value = part[:, place * rows : (place + 1) * rows]
            own[:, columns] = value
            sent[:, columns] = value.astype(jnp.bfloat16)


def finish_kernel(group, memory, mixed, own, received, valid, out):
    count = own.shape[0]

    @pl.when(group[0] == 0)
    def _():
        out[...] = memory[...]

    @pl.when(group[0] != 0)
    def _():
        total = own[...] + received[...].astype(jnp.float32)
        attended = jnp.where(valid[...] > 0.0, total, 0.0)
        out[:count] = (mixed[:count] + attended).astype(jnp.bfloat16)
        out[count:] = mixed[count:].astype(jnp.bfloat16)


def project(order, memory, target, blocks):
    rows, half = blocks[0].shape[0], blocks[0].shape[1] // 4
    return local(
        functools.partial(project_kernel, len(blocks)),
        "project",
        [((memory.shape[0], 2 * half), jnp.float32), ((target.shape[0], half), jnp.float32)],
        (memory, target),
        order=order,
        far=blocks,
        scratch=[
            pltpu.VMEM((len(blocks) * rows, 3 * half), jnp.bfloat16),
            pltpu.SemaphoreType.DMA((len(blocks),)),
        ],
        mib=14,
    )


def attend(order, seg_q, seg_k, memory, target, sums, early, late):
    rows, half = early[0].shape[0], early[0].shape[1] // 4
    count, width = target.shape
    blocks = len(early) + len(late)
    return local(
        functools.partial(attend_kernel, len(early), len(late)),
        "attend",
        [((count, width), jnp.float32), ((count, width), jnp.bfloat16)],
        (seg_q[:, None], seg_k[None, :], memory, target, *sums),
        order=order,
        far=(*early, *late),
        scratch=[
            pltpu.VMEM((memory.shape[0], 2 * half), jnp.float32),
            pltpu.VMEM((count, half), jnp.float32),
            pltpu.VMEM((count, half), jnp.bfloat16),
            pltpu.VMEM((max(len(late), 1) * rows, 3 * half), jnp.bfloat16),
            pltpu.VMEM((blocks * rows, half), jnp.bfloat16),
            pltpu.SemaphoreType.DMA((max(len(late), 1),)),
            pltpu.SemaphoreType.DMA((blocks,)),
        ],
        mib=14,
    )


def body(
    hidden,
    norm_gain,
    final_gain,
    router,
    w_in,
    w_out,
    expert_ids,
    slot_ids,
    src_len,
    tgt_len,
    wq,
    wk,
    wv,
    wo,
):
    group = lax.axis_index("grp")
    rows_here, width = hidden.shape[1:]
    half = wq.shape[1] // lax.axis_size("grp")
    targets = min(rows_here, -(-TGT_TOTAL // 16) * 16)

    def mine(*weights):
        return jnp.concatenate(
            [lax.dynamic_slice_in_dim(weight, group * half, half, 1) for weight in weights], axis=1
        )

    part = mine(wk, wv, wq, wo)
    other_hidden = lax.ppermute(hidden[0], "grp", [(0, 1), (1, 0)])
    layer = (norm_gain[0], router[0], w_in[0], w_out[0], expert_ids[0], slot_ids[0])
    if chips() is None:
        early, late = [lax.all_gather(part, "ep", axis=0, tiled=True)], []
        order = jnp.zeros((1,), jnp.int32)
        rows = expert_rows(hidden[0], *layer)
    else:
        early, mark = gather(part)
        z, y, x = place_of(lax.axis_index("ep"))
        order = jnp.stack([index_of(z - dz, y ^ dy, x ^ dx) for dz, dy, dx in EARLY + LATE])
        rows = expert_layer(mark, hidden[0], *layer)
        early, late = last_round(early, rows)
    memory, target, mixed = both_norms(
        hidden[0], other_hidden, final_gain[0], places(expert_ids[0], slot_ids[0]), rows, targets
    )

    seg_q = positions(tgt_len[0], targets)
    seg_k = positions(src_len[0], rows_here)
    sums = project(order, memory, target, early)
    own, sent = attend(order, seg_q, seg_k, memory, target, sums, early, late)
    received = lax.ppermute(sent, "grp", [(0, 1)])
    (out,) = local(
        finish_kernel,
        "finish",
        [((rows_here, width), jnp.bfloat16)],
        (memory, mixed, own, received, (seg_q < SENT).astype(jnp.float32)[:, None]),
        order=group[None],
        mib=8,
    )
    return out[None]


def solution(mesh):
    in_specs = (
        P("grp", "ep", None),
        P("grp", None),
        P("grp", None),
        P("grp", None, None),
        P("grp", None, "ep"),
        P("grp", "ep", None),
        P("grp", "ep", None),
        P("grp", "ep", None),
        P("ep", None),
        P("ep", None),
        P("ep", None),
        P("ep", None),
        P("ep", None),
        P("ep", None),
    )
    out_specs = P("grp", "ep", None)
    return jax.shard_map(body, mesh=mesh, in_specs=in_specs, out_specs=out_specs, check_vma=False)
```

```python
import functools

import jax
import jax.numpy as jnp
from jax import lax
from jax.experimental import pallas as pl
from jax.experimental.pallas import tpu as pltpu
from jax.sharding import PartitionSpec as P

HD = 128
SPLIT = 8
C = 6
PAD = 8
SENT = 4
TGT_TOTAL = 171
MIB = 1 << 20


def normalize(values, gain):
    mean = jnp.mean(values, -1, keepdims=True)
    centred = values - mean
    spread = jnp.mean(centred * centred, -1, keepdims=True)
    return centred * lax.rsqrt(spread + 1e-05) * gain


def positions(lengths, count):
    upto = jnp.arange(SENT)[:, None] <= jnp.arange(SENT)[None, :]
    ends = jnp.sum(jnp.where(upto, lengths[:, None], 0), axis=0)
    above = (jnp.arange(count, dtype=jnp.int32)[:, None] >= ends[None, :]).astype(jnp.int32)
    return jnp.sum(above, axis=1)


def dot(left, right):
    return jnp.dot(left, right, preferred_element_type=jnp.float32)


def dot_rows(left, right):
    return lax.dot_general(
        left, right, (((1,), (1,)), ((), ())), preferred_element_type=jnp.float32
    )


def chips():
    return (4, 2, 2) if lax.axis_size("ep") == 16 else None


def place_of(index):
    depth, high, wide = chips()
    return index // (high * wide), index // wide % high, index % wide


def index_of(z, y, x):
    depth, high, wide = chips()
    return (z % depth * high + y) * wide + x


def moved(value, dz=0, dy=0, dx=0):
    pairs = []
    for source in range(lax.axis_size("ep")):
        z, y, x = place_of(source)
        pairs.append((source, index_of(z + dz, y ^ dy, x ^ dx)))
    return lax.ppermute(value, "ep", pairs)


def specs(smem, vmem, unread=0):
    return (
        [pl.BlockSpec(memory_space=pltpu.SMEM)] * smem
        + [pl.BlockSpec(memory_space=pltpu.VMEM)] * vmem
        + [pl.BlockSpec(memory_space=pl.ANY)] * unread
    )


def local(kernel, name, outs, vmem, after=(), onward=(), order=None, far=(), scratch=(), mib=6):
    scalars = () if order is None else (order,)
    read = len(scalars) + len(vmem) + len(far)
    unread = len(after) + len(onward)

    def run(*refs):
        results = refs[read + unread :]
        kernel(*refs[:read], *results[: len(outs)], *results[len(outs) + len(onward) :])

    first = read + len(after)
    return pl.pallas_call(
        run,
        out_shape=[jax.ShapeDtypeStruct(shape, dtype) for shape, dtype in outs]
        + [jax.ShapeDtypeStruct(array.shape, array.dtype) for array in onward],
        in_specs=specs(len(scalars), len(vmem), len(far) + unread),
        out_specs=specs(0, len(outs), len(onward)),
        scratch_shapes=list(scratch),
        input_output_aliases={first + i: len(outs) + i for i in range(len(onward))},
        compiler_params=pltpu.CompilerParams(vmem_limit_bytes=mib * MIB),
        name=name,
    )(*scalars, *vmem, *far, *after, *onward)


def pack_kernel(held, place, both, hidden, gain, router, gate, own, other):
    count = gate.shape[0]
    slot = lax.broadcasted_iota(jnp.int32, (count, hidden.shape[0]), 0)
    table = slot == place[...]
    rows = dot(table.astype(jnp.bfloat16), hidden[...])
    normed = normalize(rows, gain[...])
    near, far = halves(held, normed)
    own[...] = near.astype(jnp.bfloat16)
    other[...] = far.astype(jnp.bfloat16)
    logits = dot(normed.astype(jnp.bfloat16), router[...])
    mine = lax.broadcasted_iota(jnp.int32, (count, 1), 0) // PAD
    others = jnp.sum(jnp.where(table, both[...], 0), axis=1, keepdims=True) - mine
    expert = lax.broadcasted_iota(jnp.int32, logits.shape, 1)
    lead = jnp.where(expert == mine, logits, 0.0) - jnp.where(expert == others, logits, 0.0)
    gate[...] = 1.0 / (1.0 + jnp.exp(-jnp.sum(lead, axis=1, keepdims=True)))


def halves(held, rows):
    first = held[0] == 0
    return jnp.where(first, rows[:PAD], rows[PAD:]), jnp.where(first, rows[PAD:], rows[:PAD])


def copies_kernel(own, arrived, out):
    rows = jnp.concatenate([ref[...].astype(jnp.float32) for ref in (own, arrived)], axis=0)
    rows = rows.astype(jnp.bfloat16)
    for low in range(0, out.shape[0], 2 * PAD):
        out[low : low + 2 * PAD] = rows


def gate_kernel():
    pass


def mlp_kernel(rows, w_in, w_out, pieces):
    inner = jnp.maximum(dot(rows[...], w_in[...]), 0.0).astype(jnp.bfloat16)
    pieces[...] = dot(inner, w_out[...]).astype(jnp.bfloat16)


def sum_kernel(pieces, own, other):
    total = pieces[: 2 * PAD].astype(jnp.float32)
    for low in range(2 * PAD, pieces.shape[0], 2 * PAD):
        total = total + pieces[low : low + 2 * PAD].astype(jnp.float32)
    own[...] = total[:PAD]
    other[...] = total[PAD:]


def rows_kernel(held, gate, own, arrived, rows):
    first = held[0] == 0
    near = jnp.where(first, own[...], arrived[...])
    far = jnp.where(first, arrived[...], own[...])
    rows[...] = gate[...] * jnp.concatenate([near, far], axis=0)


def mixed_rows(hidden, place, rows_ref):
    rows = rows_ref[...]
    count, size = rows.shape[0], hidden.shape[0]
    high = rows.astype(jnp.bfloat16)
    rest = rows - high.astype(jnp.float32)
    middle = rest.astype(jnp.bfloat16)
    low = (rest - middle.astype(jnp.float32)).astype(jnp.bfloat16)
    slot = lax.broadcasted_iota(jnp.int32, (size, 3 * count), 1) % count
    picks = (slot.astype(jnp.float32) == place[...]).astype(jnp.bfloat16)
    added = dot(picks, jnp.concatenate([high, middle, low], axis=0))
    return hidden[...].astype(jnp.float32) + added


def norm_kernel(group, *refs):
    own, other, (memory, target, mixed) = refs[:4], refs[4:8], refs[8:]

    def run(source, wanted):
        hidden, place, rows, gain = source
        values = mixed_rows(hidden, place, rows)
        memory[...] = normalize(values, gain[...]).astype(jnp.bfloat16)
        hidden, place, rows, gain = wanted
        mixed[...] = mixed_rows(hidden, place, rows)
        target[...] = normalize(mixed[: target.shape[0]], gain[...]).astype(jnp.bfloat16)

    pl.when(group[0] == 0)(lambda: run(own, other))
    pl.when(group[0] != 0)(lambda: run(other, own))


def places(routes, slots):
    return jnp.max(jnp.where(slots >= 0, routes * PAD + slots, -1), axis=1)


def expert_rows(hidden, norm_gain, router, w_in, w_out, routes, slots):
    experts = lax.axis_size("ep") // SPLIT
    count = experts * PAD
    width = hidden.shape[1]
    table = jnp.arange(count)[:, None] == places(routes, slots)[None, :]
    rows = dot(table.astype(jnp.bfloat16), hidden)
    normed = normalize(rows, norm_gain).astype(jnp.bfloat16)
    outgoing = jnp.broadcast_to(normed.reshape(experts, 1, PAD, width), (experts, SPLIT, PAD, width))
    arrived = lax.all_to_all(
        outgoing.reshape(experts * SPLIT, PAD, width), "ep", split_axis=0, concat_axis=0, tiled=True
    ).reshape(-1, width)
    inner = jax.nn.relu(dot(arrived, w_in)).astype(jnp.bfloat16)
    piece = dot(inner, w_out).astype(jnp.bfloat16)
    back = lax.all_to_all(
        piece.reshape(-1, PAD, width), "ep", split_axis=0, concat_axis=0, tiled=True
    )
    summed = jnp.sum(back.reshape(experts, SPLIT, PAD, width).astype(jnp.float32), axis=1)
    logits = dot(normed, router)
    mine = jnp.arange(count) // PAD
    both = jnp.sum(routes, axis=1)
    others = jnp.sum(jnp.where(table, both[None, :], 0), axis=1) - mine
    ids = jnp.arange(router.shape[1])[None, :]
    sign = (ids == mine[:, None]).astype(jnp.float32) - (ids == others[:, None]).astype(jnp.float32)
    gate = jax.nn.sigmoid(jnp.sum(logits * sign, axis=1, keepdims=True))
    return gate * summed.reshape(count, width)


def expert_layer(mark, hidden, norm_gain, router, w_in, w_out, routes, slots):
    devices = lax.axis_size("ep")
    width = hidden.shape[1]
    depth = chips()[0]
    half = (place_of(lax.axis_index("ep"))[0] // (depth // 2))[None]
    groups = [list(range(low, low + SPLIT)) for low in range(0, devices, SPLIT)]
    small, wide = (PAD, width), (2 * PAD * SPLIT, width)

    def exchanged(values):
        parts = values.reshape(SPLIT, 2 * PAD, width)
        parts = lax.all_to_all(
            parts, "ep", split_axis=0, concat_axis=0, tiled=True, axis_index_groups=groups
        )
        return parts.reshape(values.shape)

    gate, own, other = local(
        pack_kernel,
        "pack",
        [((2 * PAD, 1), jnp.float32), (small, jnp.bfloat16), (small, jnp.bfloat16)],
        (
            places(routes, slots)[None, :],
            jnp.sum(routes, axis=1)[None, :],
            hidden,
            norm_gain[None, :],
            router,
        ),
        order=half,
    )
    (send,) = local(
        copies_kernel, "copies", [(wide, jnp.bfloat16)], (own, moved(other, dz=depth // 2))
    )
    (pieces,) = local(
        mlp_kernel, "mlp", [(wide, jnp.bfloat16)], (exchanged(send), w_in, w_out), mark
    )
    own, other = local(
        sum_kernel, "sum", [((PAD, width), jnp.float32)] * 2, (exchanged(pieces),)
    )
    (rows,) = local(
        rows_kernel,
        "rows",
        [((2 * PAD, width), jnp.float32)],
        (gate, own, moved(other, dz=depth // 2)),
        order=half,
    )
    return rows


def both_norms(hidden, other_hidden, final_gain, place, rows, targets):
    swap = [(0, 1), (1, 0)]
    place = place[:, None].astype(jnp.float32)
    gain = final_gain[None, :]
    small = jnp.concatenate([gain, jnp.pad(place.T, ((0, 0), (0, gain.shape[1] - place.shape[0])))])
    small = lax.ppermute(small, "grp", swap)
    other_rows = lax.ppermute(rows, "grp", swap)
    own = (hidden, place, rows, gain)
    other = (other_hidden, small[1, : place.shape[0]][:, None], other_rows, small[:1])
    size, width = hidden.shape
    return local(
        norm_kernel,
        "norm",
        [
            ((size, width), jnp.bfloat16),
            ((targets, width), jnp.bfloat16),
            ((size, width), jnp.float32),
        ],
        (*own[:4], *other[:4]),
        order=lax.axis_index("grp")[None],
        mib=12,
    )


EARLY = [
    (0, 0, 0), (1, 0, 0), (2, 0, 0), (3, 0, 0), (0, 0, 1), (1, 0, 1), (0, 1, 0), (1, 1, 0),
    (2, 1, 0), (3, 1, 0), (0, 1, 1), (1, 1, 1), (2, 0, 1),
]
LATE = [(3, 0, 1), (3, 1, 1), (2, 1, 1)]


def gather(part):
    def once(there, *blocks):
        return local(gate_kernel, "gate", [], (), there, blocks)

    z1, x0, y0 = moved(part, dz=1), moved(part, dx=1), moved(part, dy=1)
    (y0,) = once([x0, z1], y0)
    z2, y1, far0 = moved(z1, dz=1), moved(z1, dy=1), moved(y0, dx=1)
    z1, far0 = once([y1, z2], z1, far0)
    second = [z1]
    z3, y2, x1 = moved(z2, dz=1), moved(z2, dy=1), moved(z1, dx=1)
    z2, far0 = once([x1, y2, z3], z2, far0)
    y3, x2, far1 = moved(z3, dy=1), moved(z2, dx=1), moved(far0, dz=1)
    return [part, z1, z2, z3, x0, x1, y0, y1, y2, y3, far0, far1, x2], second


def last_round(early, rows):
    part, z1, z2, z3, x0, x1, y0, y1, y2, y3, far0, far1, x2 = early
    z3, far0, x2 = local(gate_kernel, "gate", [], (), [far1, y3, rows], [z3, far0, x2])
    far3, x3, far2 = moved(far0, dz=-1), moved(z3, dx=1), moved(x2, dy=1)
    return [part, z1, z2, z3, x0, x1, y0, y1, y2, y3, far0, far1, x2], [x3, far3, far2]


def pairs_of(refs):
    return [tuple(range(low, min(low + 2, len(refs)))) for low in range(0, len(refs), 2)]


def joined(parts, axis):
    return parts[0] if len(parts) == 1 else jnp.concatenate(parts, axis=axis)


def fetched(blocks, columns, near, sems):
    rows = blocks[0].shape[0]
    copies = [
        pltpu.make_async_copy(
            block.at[:, columns], near.at[pl.ds(i * rows, rows)], sems.at[i]
        )
        for i, block in enumerate(blocks)
    ]
    for copy in copies:
        copy.start()
    return copies


def add_blocks(order, memory, target, near, copies, kv, q, fresh):
    rows = near.shape[0] // len(copies)
    half = q.shape[1]

    def columns(ref, members):
        return joined(
            [ref[:, pl.ds(pl.multiple_of(order[i] * rows, 128), rows)] for i in members], 1
        )

    for step, members in enumerate(pairs_of(copies)):
        for i in members:
            copies[i].wait()
        weights = near[members[0] * rows : (members[-1] + 1) * rows]
        kv_part = dot(columns(memory, members), weights[:, : 2 * half])
        q_part = dot(columns(target, members), weights[:, 2 * half :])
        if fresh and step == 0:
            kv[...] = kv_part
            q[...] = q_part
        else:
            kv[...] += kv_part
            q[...] += q_part


def project_kernel(count, order, memory, target, *refs):
    blocks, (kv, q, near, sems) = refs[:count], refs[count:]
    copies = fetched(blocks, pl.ds(0, near.shape[1]), near, sems)
    add_blocks(order, memory, target, near, copies, kv, q, True)


def attend_kernel(early, late, order, seg_q, seg_k, memory, target, kv_sum, q_sum, *refs):
    blocks = refs[: early + late]
    own, sent, kv, q, context, near, near_out, sems, sems_out = refs[early + late :]
    half = q.shape[1]
    rows = blocks[0].shape[0]
    kv[...] = kv_sum[...]
    q[...] = q_sum[...]
    if late:
        copies = fetched(blocks[early:], pl.ds(0, 3 * half), near, sems)
    copies_out = fetched(blocks, pl.ds(3 * half, half), near_out, sems_out)
    if late:
        late_order = [order[early + i] for i in range(late)]
        add_blocks(late_order, memory, target, near, copies, kv, q, False)
    allowed = seg_q[...] == seg_k[...]
    for low in range(0, half, HD):
        query = q[:, low : low + HD].astype(jnp.bfloat16)
        keys = kv[:, low : low + HD].astype(jnp.bfloat16)
        values = kv[:, half + low : half + low + HD].astype(jnp.bfloat16)
        scores = jnp.where(allowed, dot_rows(query, keys) * HD ** (-0.5), -1e30)
        expd = jnp.exp(scores - jnp.max(scores, axis=-1, keepdims=True))
        prob = (expd / jnp.sum(expd, axis=-1, keepdims=True)).astype(jnp.bfloat16)
        context[:, low : low + HD] = dot(prob, values).astype(jnp.bfloat16)
    for copy in copies_out:
        copy.wait()
    for members in pairs_of(blocks):
        part = dot_rows(context[...], near_out[members[0] * rows : (members[-1] + 1) * rows])
        for place, i in enumerate(members):
            columns = pl.ds(pl.multiple_of(order[i] * rows, 128), rows)
            value = part[:, place * rows : (place + 1) * rows]
            own[:, columns] = value
            sent[:, columns] = value.astype(jnp.bfloat16)


def finish_kernel(group, memory, mixed, own, received, valid, out):
    count = own.shape[0]

    @pl.when(group[0] == 0)
    def _():
        out[...] = memory[...]

    @pl.when(group[0] != 0)
    def _():
        total = own[...] + received[...].astype(jnp.float32)
        attended = jnp.where(valid[...] > 0.0, total, 0.0)
        out[:count] = (mixed[:count] + attended).astype(jnp.bfloat16)
        out[count:] = mixed[count:].astype(jnp.bfloat16)


def project(order, memory, target, blocks):
    rows, half = blocks[0].shape[0], blocks[0].shape[1] // 4
    return local(
        functools.partial(project_kernel, len(blocks)),
        "project",
        [((memory.shape[0], 2 * half), jnp.float32), ((target.shape[0], half), jnp.float32)],
        (memory, target),
        order=order,
        far=blocks,
        scratch=[
            pltpu.VMEM((len(blocks) * rows, 3 * half), jnp.bfloat16),
            pltpu.SemaphoreType.DMA((len(blocks),)),
        ],
        mib=14,
    )


def attend(order, seg_q, seg_k, memory, target, sums, early, late):
    rows, half = early[0].shape[0], early[0].shape[1] // 4
    count, width = target.shape
    blocks = len(early) + len(late)
    return local(
        functools.partial(attend_kernel, len(early), len(late)),
        "attend",
        [((count, width), jnp.float32), ((count, width), jnp.bfloat16)],
        (seg_q[:, None], seg_k[None, :], memory, target, *sums),
        order=order,
        far=(*early, *late),
        scratch=[
            pltpu.VMEM((memory.shape[0], 2 * half), jnp.float32),
            pltpu.VMEM((count, half), jnp.float32),
            pltpu.VMEM((count, half), jnp.bfloat16),
            pltpu.VMEM((max(len(late), 1) * rows, 3 * half), jnp.bfloat16),
            pltpu.VMEM((blocks * rows, half), jnp.bfloat16),
            pltpu.SemaphoreType.DMA((max(len(late), 1),)),
            pltpu.SemaphoreType.DMA((blocks,)),
        ],
        mib=14,
    )


def body(
    hidden,
    norm_gain,
    final_gain,
    router,
    w_in,
    w_out,
    expert_ids,
    slot_ids,
    src_len,
    tgt_len,
    wq,
    wk,
    wv,
    wo,
):
    group = lax.axis_index("grp")
    rows_here, width = hidden.shape[1:]
    half = wq.shape[1] // lax.axis_size("grp")
    targets = min(rows_here, -(-TGT_TOTAL // 16) * 16)

    def mine(*weights):
        return jnp.concatenate(
            [lax.dynamic_slice_in_dim(weight, group * half, half, 1) for weight in weights], axis=1
        )

    part = mine(wk, wv, wq, wo)
    other_hidden = lax.ppermute(hidden[0], "grp", [(0, 1), (1, 0)])
    layer = (norm_gain[0], router[0], w_in[0], w_out[0], expert_ids[0], slot_ids[0])
    if chips() is None:
        early, late = [lax.all_gather(part, "ep", axis=0, tiled=True)], []
        order = jnp.zeros((1,), jnp.int32)
        rows = expert_rows(hidden[0], *layer)
    else:
        early, mark = gather(part)
        z, y, x = place_of(lax.axis_index("ep"))
        order = jnp.stack([index_of(z - dz, y ^ dy, x ^ dx) for dz, dy, dx in EARLY + LATE])
        rows = expert_layer(mark, hidden[0], *layer)
        early, late = last_round(early, rows)
    memory, target, mixed = both_norms(
        hidden[0], other_hidden, final_gain[0], places(expert_ids[0], slot_ids[0]), rows, targets
    )

    seg_q = positions(tgt_len[0], targets)
    seg_k = positions(src_len[0], rows_here)
    sums = project(order, memory, target, early)
    own, sent = attend(order, seg_q, seg_k, memory, target, sums, early, late)
    received = lax.ppermute(sent, "grp", [(0, 1)])
    (out,) = local(
        finish_kernel,
        "finish",
        [((rows_here, width), jnp.bfloat16)],
        (memory, mixed, own, received, (seg_q < SENT).astype(jnp.float32)[:, None]),
        order=group[None],
        mib=8,
    )
    return out[None]


def solution(mesh):
    in_specs = (
        P("grp", "ep", None),
        P("grp", None),
        P("grp", None),
        P("grp", None, None),
        P("grp", None, "ep"),
        P("grp", "ep", None),
        P("grp", "ep", None),
        P("grp", "ep", None),
        P("ep", None),
        P("ep", None),
        P("ep", None),
        P("ep", None),
        P("ep", None),
        P("ep", None),
    )
    out_specs = P("grp", "ep", None)
    return jax.shard_map(body, mesh=mesh, in_specs=in_specs, out_specs=out_specs, check_vma=False)
```
